32 devices in a mesh: tok: 32 (over z, y, x, core).
Axes of the slice: x: 2, y: 2, z: 4, core: 2. Of those that a mesh axis runs over, the one named last changes fastest.
Arguments:
- tokens: bfloat16 [16384, 1536], P('tok'), may hold values from -6 to 6
- cotangent: bfloat16 [16384, 1536], P('tok'), may hold values from -6 to 6
- attn_gain: bfloat16 [1536], P('tok'), may hold values from 0.5 to 1.5
- ffn_gain: bfloat16 [1536], P('tok'), may hold values from 0.5 to 1.5
- w_query: bfloat16 [1536, 1536], P('tok'), may hold values from -0.15625 to 0.15625
- w_key: bfloat16 [1536, 128], P('tok'), may hold values from -0.15625 to 0.15625
- w_value: bfloat16 [1536, 128], P('tok'), may hold values from -0.15625 to 0.15625
- w_out: bfloat16 [1536, 1536], P('tok'), may hold values from -1.25 to 1.25
- w_gate: bfloat16 [1536, 4608], P('tok'), may hold values from -0.15625 to 0.15625
- w_up: bfloat16 [1536, 4608], P('tok'), may hold values from -0.15625 to 0.15625
- w_down: bfloat16 [1536, 4608], P('tok'), may hold values from -0.09375 to 0.09375
- segments: int32 [16384], replicated, may hold values from 0 to 81, as said below
- positions: int32 [16384], P('tok'), may hold values from 0 to 3998, as said below
Outputs:
- output: bfloat16 [16384, 1536], P('tok')
- grad_tokens: bfloat16 [16384, 1536], P('tok')
- grad_attn_gain: float32 [1536], P('tok')
- grad_ffn_gain: float32 [1536], P('tok')
- grad_query: float32 [1536, 1536], P('tok')
- grad_key: float32 [1536, 128], P('tok')
- grad_value: float32 [1536, 128], P('tok')
- grad_out: float32 [1536, 1536], P('tok')
- grad_gate: float32 [1536, 4608], P('tok')
- grad_up: float32 [1536, 4608], P('tok')
- grad_down: float32 [1536, 4608], P('tok')
The draws below stay inside these ranges and needn't reach their ends.
Inputs may be any that keep to these rules, and one draw needn't show every extreme that they name: `segments`: segment numbers never fall along the tokens; one number marks one document of the one packed sequence of 16384 tokens; documents hold 200 to 2000 tokens, except the last, which the sequence's end cuts. Within a document positions rise by one per token; each document starts at 0, except the first, which may start later.
All inputs are finite; a program needn't handle non-finite values.
Results may differ from the reference program's by a relative error of at most 0.015.
Values may be sent and summed in bfloat16 or wider, within the bound.
A program may use at most 384 MiB of HBM per device.

```python
import math
import jax
import jax.numpy as jnp
from jax import lax

D = 1536
HQ = 12
HD = 128
FF = 4608
WINDOW = 1024
DOC_MIN = 200
DOC_MAX = 2000
TOKENS = 16384
SEQ = 16384


def doc_layout(key):
    count = SEQ // DOC_MIN + 1
    lengths = jax.random.randint(jax.random.fold_in(key, 11), (count,), DOC_MIN, DOC_MAX + 1)
    lengths = lengths.at[0].set(DOC_MAX)
    ends = jnp.cumsum(lengths).astype(jnp.int32)
    first_start = DOC_MAX - 1
    index = jnp.arange(TOKENS, dtype=jnp.int32)
    docs = jnp.searchsorted(ends, index, side='right').astype(jnp.int32)
    prior = jnp.where(docs > 0, ends[jnp.maximum(docs - 1, 0)], 0).astype(jnp.int32)
    last_docs = jnp.sum((ends <= TOKENS - 1).astype(jnp.int32))
    segment = (docs + (count - 1 - last_docs)).astype(jnp.int32)
    position = (index - prior + jnp.where(docs == 0, first_start, 0)).astype(jnp.int32)
    return (segment, position)


def draw_segments(key, part):
    return doc_layout(key)[0]


def draw_positions(key, part):
    return doc_layout(key)[1]


def strengthened(values, own_key, source, target, blocks, factor):
    def block_of(dim):
        return (jnp.arange(values.shape[dim]) // (values.shape[dim] // blocks)).reshape((-1,) + (1,) * (values.ndim - 1 - dim))

    near = jax.random.permutation(own_key, blocks)[block_of(target)]
    other_side = (block_of(target) + blocks // 2) % blocks
    return jnp.where((block_of(source) == near) | (block_of(source) == other_side), factor * values, values)


def shard_levels(key, shape, split, smallest, largest):
    def one(dim, blocks):
        heights = jax.random.uniform(jax.random.fold_in(jax.random.fold_in(key, 6), dim), (blocks,), jnp.float32, smallest / len(split), largest / len(split))
        return jnp.repeat(jnp.exp(heights), shape[dim] // blocks).reshape((-1,) + (1,) * (len(shape) - dim - 1))

    loudness = one(*split[0])
    for cut in split[1:]:
        loudness = loudness * one(*cut)
    return loudness


def noise(own_key, dims, deviation, bound, cuts=(), kind=jnp.bfloat16):
    values = jax.random.normal(own_key, dims, jnp.float32) * deviation
    if len(cuts) > 0:
        values = shard_levels(own_key, dims, cuts, -0.22, 0.18) * values
    return jnp.clip(values, min=-bound, max=bound).astype(kind)


def heavy_noise(stream_key, extent, deviation, limit, pieces, heavy, held_as=jnp.bfloat16):
    array = deviation * jax.random.normal(stream_key, extent, jnp.float32)
    if pieces:
        array = array * shard_levels(stream_key, extent, pieces, -0.22, 0.18)
    return jnp.clip(strengthened(array, jax.random.fold_in(stream_key, 3), *heavy), -limit, limit).astype(held_as)


def setup_inputs(seed: int = 0) -> dict:
    keys = jax.random.split(jax.random.key(seed), 14)
    return {
        "tokens": noise(keys[0], (TOKENS, D), 1.0, 6.0, ((0, 32),)),
        "cotangent": heavy_noise(keys[1], (TOKENS, D), 1.0, 6.0, ((0, 32),), (0, 1, 32, 2.75)),
        "attn_gain": jnp.clip(1.0 + 0.1 * jax.random.normal(keys[2], (D,), jnp.float32), 0.5, 1.5).astype(jnp.bfloat16),
        "ffn_gain": jnp.clip(1.0 + 0.1 * jax.random.normal(keys[3], (D,), jnp.float32), 0.5, 1.5).astype(jnp.bfloat16),
        "w_query": noise(keys[4], (D, HQ * HD), D ** -0.5, 0.15625, ((0, 32),)),
        "w_key": noise(keys[5], (D, HD), D ** -0.5, 0.15625, ((0, 32),)),
        "w_value": noise(keys[6], (D, HD), D ** -0.5, 0.15625, ((0, 32),)),
        "w_out": noise(keys[7], (D, HQ * HD), (HQ * HD // 64) ** -0.5, 1.25, ((0, 32),)),
        "w_gate": noise(keys[8], (D, FF), D ** -0.5, 0.15625, ((0, 32),)),
        "w_up": noise(keys[9], (D, FF), D ** -0.5, 0.15625, ((0, 32),)),
        "w_down": noise(keys[10], (D, FF), FF ** -0.5, 0.09375, ((0, 32),)),
        "segments": draw_segments(jax.random.fold_in(keys[13], 71), 0),
        "positions": draw_positions(jax.random.fold_in(keys[13], 71), 0),
    }


@jax.custom_vjp
def low(v):
    return lax.optimization_barrier(v.astype(jnp.bfloat16)).astype(jnp.float32)

@jax.custom_vjp
def low_back(v):
    return v

def low_keep(v):
    return (low(v), None)

def low_pass(kept, grad):
    return (grad,)

def back_keep(v):
    return (v, None)

def back_low(kept, grad):
    return (low(grad),)
low.defvjp(low_keep, low_pass)
low_back.defvjp(back_keep, back_low)
EPSILON = 1e-06
HIGH = lax.Precision.HIGHEST

def rms_norm(values, scales):
    return values * lax.rsqrt(lax.optimization_barrier(jnp.mean(values * values, axis=-1, keepdims=True)) + EPSILON) * scales

def angle_table(positions):
    frequency = 10000.0 ** (-jnp.arange(HD // 2, dtype=jnp.float32) * 2.0 / HD)
    return positions.astype(jnp.float32)[:, None] * frequency[None, :]

def rotate(values, angles):
    half_size = values.shape[-1] // 2
    cosine = jnp.cos(angles)[:, None, :]
    sine_part = jnp.sin(angles)[:, None, :]
    former = values[..., :half_size]
    latter = values[..., half_size:]
    return jnp.concatenate([former * cosine - latter * sine_part, latter * cosine + former * sine_part], axis=-1)

def forward(inputs, gain_one, gain_two, query_w, key_w, value_w, out_w, gate_w, up_w, down_w, segments, angles):
    count = inputs.shape[0]
    normed = low(rms_norm(inputs, gain_one))
    queries = low(rotate(low_back(jnp.dot(normed, query_w, precision=HIGH)).reshape(count, HQ, HD), angles))
    keys_all = low(rotate(low_back(jnp.dot(normed, key_w, precision=HIGH))[:, None, :], angles))[:, 0]
    values_all = low(low_back(jnp.dot(normed, value_w, precision=HIGH)))
    block = math.gcd(512, count)
    keys_pad = jnp.concatenate([jnp.zeros((WINDOW, HD), jnp.float32), keys_all], axis=0)
    values_pad = jnp.concatenate([jnp.zeros((WINDOW, HD), jnp.float32), values_all], axis=0)
    segments_pad = jnp.concatenate([jnp.full((WINDOW,), -1, jnp.int32), segments])
    offsets = jnp.arange(WINDOW + block)[None, :] - jnp.arange(block)[:, None]
    in_window = (offsets > 0) & (offsets <= WINDOW)
    scale = HD ** (-0.5)

    def attend(index):
        start = (index * block).astype(jnp.int32)
        query_block = lax.dynamic_slice_in_dim(queries, start, block, 0)
        key_block = lax.dynamic_slice_in_dim(keys_pad, start, WINDOW + block, 0)
        value_block = lax.dynamic_slice_in_dim(values_pad, start, WINDOW + block, 0)
        query_seg = lax.dynamic_slice_in_dim(segments, start, block, 0)
        key_seg = lax.dynamic_slice_in_dim(segments_pad, start, WINDOW + block, 0)
        allowed = in_window & (query_seg[:, None] == key_seg[None, :])
        raw = low_back(jnp.einsum('qhd,kd->hqk', query_block, key_block, precision=HIGH))
        score = jnp.where(allowed[None], raw * scale, -jnp.inf)
        top = lax.optimization_barrier(jnp.max(score, axis=-1, keepdims=True))
        expo = jnp.exp(score - top)
        prob = low(expo / lax.optimization_barrier(jnp.sum(expo, axis=-1, keepdims=True)))
        mixed = jnp.einsum('hqk,kd->qhd', prob, value_block, precision=HIGH)
        return low(low_back(mixed)).reshape(block, HQ * HD)
    mixed_all = lax.map(jax.checkpoint(attend), jnp.arange(count // block, dtype=jnp.int32)).reshape(count, HQ * HD)
    middle = inputs + low_back(jnp.dot(mixed_all, out_w.T, precision=HIGH))
    normed_two = low(rms_norm(middle, gain_two))
    gate = low_back(jnp.dot(normed_two, gate_w, precision=HIGH))
    up_part = low_back(jnp.dot(normed_two, up_w, precision=HIGH))
    hidden = low(jax.nn.gelu(gate, approximate=True) * up_part)
    return middle + low_back(jnp.dot(hidden, down_w.T, precision=HIGH))

def reference(tokens, cotangent, attn_gain, ffn_gain, w_query, w_key, w_value, w_out, w_gate, w_up, w_down, segments, positions):
    angles = angle_table(positions)
    floats = tuple((item.astype(jnp.float32) for item in (tokens, attn_gain, ffn_gain, w_query, w_key, w_value, w_out, w_gate, w_up, w_down)))

    def run(*values):
        return forward(*values, segments, angles)
    result, pullback = jax.vjp(run, *floats)
    grads = pullback(cotangent.astype(jnp.float32))
    return (result.astype(jnp.bfloat16), grads[0].astype(jnp.bfloat16), grads[1], grads[2], grads[3], grads[4], grads[5], grads[6], grads[7], grads[8], grads[9])
```

```python
import functools

import jax
import jax.numpy as jnp
from jax import lax
from jax.experimental import pallas as pl
from jax.experimental.pallas import tpu as pltpu
from jax.sharding import PartitionSpec as P

HQ = 12
HD = 128
WINDOW = 1024
EPSILON = 1e-06

CORE, NEAR, SIDE, GROUP, RING = 1, 2, 4, 4, 8
LONGEST_RING = 8
LOG2E = 1.4426950408889634
LOW = jnp.bfloat16
FULL = jnp.float32
MIB = 1024 * 1024


def flip(array, bit):
    size = lax.axis_size("tok")
    return lax.ppermute(array, "tok", [(i, i ^ bit) for i in range(size)])


def around(array):
    size = lax.axis_size("tok")
    return lax.ppermute(array, "tok", [(i, (i + RING) % size) for i in range(size)])


def passed_along(array, by):
    size = lax.axis_size("tok")
    pairs = [(i, i + by) for i in range(size) if 0 <= i + by < size]
    return lax.ppermute(array, "tok", pairs)


def rms_norm(values, scales):
    return values * lax.rsqrt(jnp.mean(values * values, axis=-1, keepdims=True) + EPSILON) * scales


def outer_sum(left_side, right_side):
    return lax.dot_general(
        left_side, right_side, (((0,), (0,)), ((), ())), preferred_element_type=FULL
    )


def by_rows(left_side, right_side):
    return lax.dot_general(
        left_side, right_side, (((1,), (1,)), ((), ())), preferred_element_type=FULL
    )


def matmul(left_side, right_side):
    return jnp.dot(left_side, right_side, preferred_element_type=FULL)


def pick(array, index):
    return lax.dynamic_index_in_dim(array, index, 0, keepdims=False)


def place():
    device = lax.axis_index("tok")
    return device, device % 2, (device // 2) % 2, (device // 4) % 2, device // RING


def rows_to_group(array):
    two = jnp.concatenate([array, flip(array, NEAR)], axis=0)
    return jnp.concatenate([two, flip(two, CORE)], axis=0)


def rows_from_group(partial):
    half = partial.shape[0] // 2
    two = partial[:half].astype(FULL) + flip(partial[half:].astype(LOW), CORE).astype(FULL)
    quarter = half // 2
    return two[:quarter] + flip(two[quarter:].astype(LOW), NEAR).astype(FULL)


def slices_to_group(parts):
    _, core, near, _, _ = place()
    rows, columns = parts.shape[1:]
    mine = lax.dynamic_slice_in_dim(parts, 2 * near, 2, 0)
    theirs = flip(lax.dynamic_slice_in_dim(parts, 2 * (1 - near), 2, 0), NEAR)
    here = jnp.stack([pick(mine, core), pick(theirs, core)])
    away = flip(jnp.stack([pick(mine, 1 - core), pick(theirs, 1 - core)]), CORE)
    by_core = jnp.where(core == 0, jnp.stack([here, away], 1), jnp.stack([away, here], 1))
    by_near = jnp.where(near == 0, by_core, by_core[::-1])
    return by_near.reshape(4 * rows, columns)


def slices_from_group(block):
    _, core, near, _, _ = place()
    rows, columns = block.shape[0] // 4, block.shape[1]
    parts = block.astype(LOW).reshape(2, 2, rows, columns)
    mine, theirs = pick(parts, near), flip(pick(parts, 1 - near), NEAR)
    here = jnp.stack([pick(mine, core), pick(theirs, core)])
    away = flip(jnp.stack([pick(mine, 1 - core), pick(theirs, 1 - core)]), CORE)
    by_core = jnp.where(core == 0, jnp.stack([here, away], 1), jnp.stack([away, here], 1))
    by_near = jnp.where(near == 0, by_core, by_core[::-1])
    return by_near.reshape(4, rows, columns)


def groups_of(stride):
    size = lax.axis_size("tok")
    return [[s + stride * k for k in range(size // stride)] for s in range(stride)]


def spread(block, stages):
    size = lax.axis_size("tok")
    ring = size // RING
    if ring > LONGEST_RING:
        return lax.all_gather(
            block, "tok", axis=0, tiled=True, axis_index_groups=groups_of(stages[-1])
        )
    device, _, _, _, z = place()
    rows, columns = block.shape
    steps = RING // stages[-1]
    total = jnp.zeros((ring * steps, rows, columns), block.dtype)
    own = block
    for step in range(ring):
        chunk = lax.rem(z - step + ring, ring)
        blocks = [own]
        for bit in stages:
            stacked = jnp.stack(blocks) if len(blocks) > 1 else blocks[0][None]
            got = flip(stacked, bit)
            blocks = blocks + [got[k] for k in range(len(blocks))]
        low_bits = lax.rem(device, RING) // stages[-1]
        for k, piece in enumerate(blocks):
            mask = 0
            for j, bit in enumerate(stages):
                if (k >> j) & 1:
                    mask |= bit // stages[-1]
            index = chunk * steps + lax.bitwise_xor(low_bits, mask)
            total = lax.dynamic_update_index_in_dim(total, piece, index, 0)
        if step < ring - 1:
            own = around(own)
    return total.reshape(ring * steps * rows, columns)


def collect(partial, stages):
    size = lax.axis_size("tok")
    ring = size // RING
    if ring > LONGEST_RING:
        return lax.psum_scatter(
            partial.astype(FULL),
            "tok",
            scatter_dimension=0,
            tiled=True,
            axis_index_groups=groups_of(stages[-1]),
        )
    device, _, _, _, z = place()
    steps = RING // stages[-1]
    rows, columns = partial.shape[0] // (ring * steps), partial.shape[1]
    parts = partial.astype(LOW).reshape((ring, *([2] * len(stages)), rows, columns))

    def piece(chunk):
        held = pick(parts, chunk)
        for bit in reversed(stages):
            axis = stages.index(bit)
            own_bit = (device // bit) % 2
            keep = lax.dynamic_index_in_dim(held, own_bit, axis, keepdims=False)
            give = lax.dynamic_index_in_dim(held, 1 - own_bit, axis, keepdims=False)
            held = keep.astype(FULL) + flip(give.astype(LOW), bit).astype(FULL)
        return held

    total = piece(lax.rem(z - 1 + ring, ring))
    for step in range(1, ring):
        total = around(total.astype(LOW)).astype(FULL) + piece(lax.rem(z - 1 - step + 2 * ring, ring))
    return total


def turn(values, cosine, sine):
    return values * cosine + pltpu.roll(values, HD // 2, 1) * sine


def mask_into(bias, key_segments, query_segments, block):
    keys, queries = bias.shape
    for start in range(0, queries, block):
        offset = (
            lax.broadcasted_iota(jnp.int32, (keys, block), 0)
            - lax.broadcasted_iota(jnp.int32, (keys, block), 1)
            - start
        )
        same = key_segments[...] == query_segments[:, start : start + block]
        allowed = same & (offset > 0) & (offset <= WINDOW)
        bias[:, start : start + block] = jnp.where(allowed, 0.0, -jnp.inf)


def attend_kernel(
    block, factor, q_ref, key_ref, value_t_ref, ks_ref, qs_ref, cos_ref, sin_ref,
    rot_ref, mixed_ref, log_ref, bias,
):
    @pl.when(pl.program_id(0) == 0)
    def _():
        mask_into(bias, ks_ref, qs_ref, block)

    queries = q_ref.shape[0]
    rot_ref[...] = turn(q_ref[...], cos_ref[...], sin_ref[...]).astype(LOW)
    for start in range(0, queries, block):
        rows, span = pl.ds(start, block), pl.ds(start, WINDOW + block)
        raw = by_rows(key_ref[span, :], rot_ref[rows, :])
        score = raw * factor + bias[span, rows]
        top = jnp.max(score, axis=0, keepdims=True)
        expo = jnp.exp2(score - top)
        total = jnp.sum(expo, axis=0, keepdims=True)
        mixed_t = matmul(value_t_ref[:, span], expo.astype(LOW)) / total
        mixed_ref[rows, :] = mixed_t.T.astype(LOW)
        log_ref[0, :, rows] = top + jnp.log2(total)


def attend(raw_query, key_value, key_segments, query_segments, cosine, sine):
    queries, width = raw_query.shape
    keys = key_value.shape[0]
    heads = width // HD
    block = min(256, queries)
    head = pl.BlockSpec((queries, HD), lambda h: (0, h))
    whole = lambda shape: pl.BlockSpec(shape, lambda h: (0,) * len(shape))
    cost = 4 * width * queries * (WINDOW + block)
    return pl.pallas_call(
        functools.partial(attend_kernel, block, HD**-0.5 * LOG2E),
        grid=(heads,),
        in_specs=[
            head,
            whole((keys, HD)),
            whole((HD, keys)),
            whole((keys, 1)),
            whole((1, queries)),
            whole((queries, HD)),
            whole((queries, HD)),
        ],
        out_specs=[head, head, pl.BlockSpec((1, 1, queries), lambda h: (h, 0, 0))],
        out_shape=[
            jax.ShapeDtypeStruct((queries, width), LOW),
            jax.ShapeDtypeStruct((queries, width), LOW),
            jax.ShapeDtypeStruct((heads, 1, queries), FULL),
        ],
        scratch_shapes=[pltpu.VMEM((keys, queries), FULL)],
        compiler_params=pltpu.CompilerParams(vmem_limit_bytes=40 * MIB),
        cost_estimate=pl.CostEstimate(
            flops=4 * cost, bytes_accessed=8 * queries * width, transcendentals=0
        ),
    )(
        raw_query,
        key_value[:, :HD],
        key_value[:, HD:].T,
        key_segments[:, None],
        query_segments[None, :],
        cosine,
        sine,
    )


def attend_back_kernel(
    block, factor, rot_ref, grad_ref, mixed_ref, log_ref, key_ref, value_ref, key_t_ref, ks_ref, qs_ref,
    cos_ref, sin_ref, query_out, key_out, value_out, bias,
):
    @pl.when(pl.program_id(0) == 0)
    def _():
        mask_into(bias, ks_ref, qs_ref, block)
        key_out[...] = jnp.zeros_like(key_out)
        value_out[...] = jnp.zeros_like(value_out)

    queries = rot_ref.shape[0]
    for start in range(0, queries, block):
        rows, span = pl.ds(start, block), pl.ds(start, WINDOW + block)
        rot, grad = rot_ref[rows, :], grad_ref[rows, :]
        product = grad.astype(FULL) * mixed_ref[rows, :].astype(FULL)
        inner = jnp.sum(product.T, axis=0, keepdims=True)
        raw = by_rows(key_ref[span, :], rot)
        prob = jnp.exp2(raw * factor + (bias[span, rows] - log_ref[0, :, rows]))
        grad_prob = by_rows(value_ref[span, :], grad)
        grad_raw = (prob * (grad_prob - inner)).astype(LOW)
        value_out[span, :] += matmul(prob.astype(LOW), grad)
        key_out[span, :] += matmul(grad_raw, rot)
        back = matmul(key_t_ref[:, span], grad_raw).T * HD**-0.5
        query_out[rows, :] = turn(back, cos_ref[rows, :], -sin_ref[rows, :]).astype(LOW)


def attend_back(rot, grad, mixed, logs, key_value, key_segments, query_segments, cosine, sine):
    queries, width = rot.shape
    keys = key_value.shape[0]
    heads = width // HD
    block = min(256, queries)
    head = pl.BlockSpec((queries, HD), lambda h: (0, h))
    whole = lambda shape: pl.BlockSpec(shape, lambda h: (0,) * len(shape))
    cost = 10 * width * queries * (WINDOW + block)
    return pl.pallas_call(
        functools.partial(attend_back_kernel, block, HD**-0.5 * LOG2E),
        grid=(heads,),
        in_specs=[
            head,
            head,
            head,
            pl.BlockSpec((1, 1, queries), lambda h: (h, 0, 0)),
            whole((keys, HD)),
            whole((keys, HD)),
            whole((HD, keys)),
            whole((keys, 1)),
            whole((1, queries)),
            whole((queries, HD)),
            whole((queries, HD)),
        ],
        out_specs=[head, whole((keys, HD)), whole((keys, HD))],
        out_shape=[
            jax.ShapeDtypeStruct((queries, width), LOW),
            jax.ShapeDtypeStruct((keys, HD), FULL),
            jax.ShapeDtypeStruct((keys, HD), FULL),
        ],
        scratch_shapes=[pltpu.VMEM((keys, queries), FULL)],
        compiler_params=pltpu.CompilerParams(vmem_limit_bytes=40 * MIB),
        cost_estimate=pl.CostEstimate(
            flops=3 * cost, bytes_accessed=8 * queries * width, transcendentals=0
        ),
    )(
        rot,
        grad,
        mixed,
        logs,
        key_value[:, :HD],
        key_value[:, HD:],
        key_value[:, :HD].T,
        key_segments[:, None],
        query_segments[None, :],
        cosine,
        sine,
    )


GELU_A = 0.7978845608028654
GELU_B = 0.044715


def hidden_kernel(normed_ref, cot_ref, gate_ref, up_ref, down_ref, hidden_ref, gate_out, up_out):
    gate = matmul(normed_ref[...], gate_ref[...])
    up = matmul(normed_ref[...], up_ref[...])
    grad_hidden = matmul(cot_ref[...], down_ref[...])
    square = gate * gate
    bent = jnp.tanh(gate * (GELU_A + GELU_A * GELU_B * square))
    half = 0.5 * (1.0 + bent)
    value = gate * half
    slope = half + 0.5 * gate * (1.0 - bent * bent) * (GELU_A + 3.0 * GELU_A * GELU_B * square)
    hidden_ref[...] = (value * up).astype(LOW)
    gate_out[...] = (grad_hidden * up * slope).astype(LOW)
    up_out[...] = (grad_hidden * value).astype(LOW)


def hidden_and_grads(normed, cotangent, gate_w, up_w, down_w):
    tokens, width = normed.shape
    columns = gate_w.shape[1]
    rows, wide = min(512, tokens), 384
    token_block = pl.BlockSpec((rows, width), lambda j, i: (i, 0))
    weight_block = pl.BlockSpec((width, wide), lambda j, i: (0, j))
    out_block = pl.BlockSpec((rows, wide), lambda j, i: (i, j))
    return pl.pallas_call(
        hidden_kernel,
        grid=(columns // wide, tokens // rows),
        in_specs=[token_block, token_block, weight_block, weight_block, weight_block],
        out_specs=[out_block] * 3,
        out_shape=[jax.ShapeDtypeStruct((tokens, columns), LOW)] * 3,
        compiler_params=pltpu.CompilerParams(vmem_limit_bytes=48 * MIB),
        cost_estimate=pl.CostEstimate(
            flops=6 * tokens * width * columns,
            bytes_accessed=12 * tokens * width,
            transcendentals=tokens * columns,
        ),
    )(normed, cotangent, gate_w, up_w, down_w)


def as_column(vector):
    return jnp.pad(vector[:, None], ((0, 0), (0, HD - 1)))


def on_device(
    tokens, cotangent, attn_gain, ffn_gain, w_query, w_key, w_value, w_out, w_gate, w_up, w_down,
    segments, positions,
):
    token_count, width = tokens.shape
    own_rows, hidden_width = w_gate.shape
    slice_width = hidden_width // GROUP
    heads_width = w_query.shape[1]
    tail_rows = min(token_count, WINDOW)
    hop_count = WINDOW // tail_rows
    device = lax.axis_index("tok")
    inputs = tokens.astype(FULL)

    frequency = 10000.0 ** (-jnp.arange(HD // 2, dtype=FULL) * 2.0 / HD)
    angles = positions.astype(FULL)[:, None] * frequency[None, :]
    cosine = jnp.concatenate([jnp.cos(angles)] * 2, axis=1)
    sine_half = jnp.sin(angles)
    sine = jnp.concatenate([-sine_half, sine_half], axis=1)
    padded_segments = jnp.concatenate([jnp.full((WINDOW,), -1, jnp.int32), segments])
    key_segments = lax.dynamic_slice_in_dim(
        padded_segments, device * token_count, WINDOW + token_count
    )
    query_segments = lax.dynamic_slice_in_dim(segments, device * token_count, token_count)

    attn_pack = jnp.concatenate(
        [
            w_query,
            w_key,
            w_value,
            w_out,
            jnp.pad(
                jnp.stack([attn_gain, ffn_gain], axis=1), ((0, 0), (0, HD - 2))
            ),
        ],
        axis=1,
    )
    attn_all = spread(attn_pack, (SIDE, NEAR, CORE))
    edge = heads_width + 2 * HD
    query_w, kv_w = attn_all[:, :heads_width], attn_all[:, heads_width:edge]
    out_w = attn_all[:, edge : edge + heads_width]
    gains = attn_all[:, edge + heads_width : edge + heads_width + 2].astype(FULL)
    gain_one, gain_two = gains[:, 0], gains[:, 1]

    def sliced(weight):
        return weight.reshape(own_rows, GROUP, slice_width).transpose(1, 0, 2)

    ffn_pack = jnp.concatenate([sliced(w_gate), sliced(w_up), sliced(w_down)], axis=2)
    ffn_rows = slices_to_group(ffn_pack)
    gate_up_w = spread(ffn_rows[:, : 2 * slice_width], (SIDE,))
    down_w = spread(ffn_rows[:, 2 * slice_width :], (SIDE,))
    gate_w, up_w = gate_up_w[:, :slice_width], gate_up_w[:, slice_width:]
    cot_group = rows_to_group(cotangent)

    inverse_one = lax.rsqrt(jnp.mean(inputs * inputs, axis=-1, keepdims=True) + EPSILON)
    normed = (inputs * inverse_one * gain_one).astype(LOW)
    kv = matmul(normed, kv_w)

    def turned(values, sine_signed):
        half = HD // 2
        rolled = jnp.concatenate([values[:, half:], values[:, :half]], axis=1)
        return values * cosine + rolled * sine_signed

    key_value = jnp.concatenate([turned(kv[:, :HD], sine), kv[:, HD:]], axis=1).astype(LOW)
    received = [passed_along(key_value, hop) for hop in range(hop_count, 0, -1)]
    all_keys = jnp.concatenate(received + [key_value], axis=0)
    raw_query = matmul(normed, query_w)
    rot, mixed, logs = attend(raw_query, all_keys, key_segments, query_segments, cosine, sine)
    middle = inputs + by_rows(mixed, out_w)
    inverse_two = lax.rsqrt(jnp.mean(middle * middle, axis=-1, keepdims=True) + EPSILON)
    normed_two = (middle * inverse_two * gain_two).astype(LOW)

    normed_group = rows_to_group(normed_two)
    hidden, gate_low, up_low = hidden_and_grads(normed_group, cot_group, gate_w, up_w, down_w)
    grad_down_w = outer_sum(cot_group, hidden).astype(LOW)
    down_sum = collect(grad_down_w, (SIDE,))
    grad_normed_part = by_rows(gate_low, gate_w) + by_rows(up_low, up_w)
    grad_normed_two = rows_from_group(grad_normed_part.astype(LOW))
    gate_up_low = jnp.concatenate([gate_low, up_low], axis=1)
    grad_gate_up_w = outer_sum(normed_group, gate_up_low).astype(LOW)
    gate_up_sum = collect(grad_gate_up_w, (SIDE,))
    result = middle + rows_from_group(by_rows(hidden, down_w).astype(LOW))
    output = result.astype(LOW)

    scaled = grad_normed_two * gain_two
    grad_middle = (
        cotangent.astype(FULL)
        + inverse_two * scaled
        - middle * inverse_two**3 * jnp.mean(scaled * middle, axis=-1, keepdims=True)
    )
    gain_two_part = jnp.sum(grad_normed_two * middle * inverse_two, axis=0)
    branch = grad_middle.astype(LOW)
    grad_mixed = matmul(branch, out_w).astype(LOW)
    grad_out_w = outer_sum(branch, mixed)
    out_sum = collect(
        jnp.concatenate([grad_out_w.astype(LOW), as_column(gain_two_part.astype(LOW))], axis=1),
        (SIDE, NEAR, CORE),
    )

    query_low, key_grads, value_grads = attend_back(
        rot, grad_mixed, mixed, logs, all_keys, key_segments, query_segments, cosine, sine
    )
    grads = jnp.concatenate([key_grads * HD**-0.5, value_grads], axis=1)
    shares = grads[WINDOW:]
    for hop in range(1, hop_count + 1):
        first_row = (hop_count - hop) * tail_rows
        returned = passed_along(grads[first_row : first_row + tail_rows].astype(LOW), -hop)
        shares = shares.at[token_count - tail_rows :].add(returned.astype(FULL))
    kv_low = jnp.concatenate([turned(shares[:, :HD], -sine), shares[:, HD:]], axis=1).astype(LOW)
    grad_query_w = outer_sum(normed, query_low).astype(LOW)
    grad_kv_w = outer_sum(normed, kv_low).astype(LOW)
    grad_normed = by_rows(query_low, query_w) + by_rows(kv_low, kv_w)
    scaled_one = grad_normed * gain_one
    grad_inputs = inverse_one * scaled_one - inputs * inverse_one**3 * jnp.mean(
        scaled_one * inputs, axis=-1, keepdims=True
    )
    grad_tokens = (grad_middle + grad_inputs).astype(LOW)
    gain_one_part = jnp.sum(grad_normed * inputs * inverse_one, axis=0)
    query_sum = collect(
        jnp.concatenate([grad_query_w, grad_kv_w, as_column(gain_one_part.astype(LOW))], axis=1),
        (SIDE, NEAR, CORE),
    )

    down_parts = slices_from_group(down_sum)
    gate_up_parts = slices_from_group(gate_up_sum)

    def joined(parts):
        return parts.transpose(1, 0, 2).reshape(own_rows, hidden_width).astype(FULL)

    return (
        output,
        grad_tokens,
        query_sum[:, edge],
        out_sum[:, heads_width],
        query_sum[:, :heads_width],
        query_sum[:, heads_width : heads_width + HD],
        query_sum[:, heads_width + HD : edge],
        out_sum[:, :heads_width],
        joined(gate_up_parts[:, :, :slice_width]),
        joined(gate_up_parts[:, :, slice_width:]),
        joined(down_parts),
    )


def solution(mesh):
    rows, flat = P("tok", None), P("tok")
    return jax.shard_map(
        on_device,
        mesh=mesh,
        in_specs=(rows, rows, flat, flat, rows, rows, rows, rows, rows, rows, rows, P(), flat),
        out_specs=(rows, rows, flat, flat, rows, rows, rows, rows, rows, rows, rows),
        check_vma=False,
    )
```

```python
import functools

import jax
import jax.numpy as jnp
from jax import lax
from jax.experimental import pallas as pl
from jax.experimental.pallas import tpu as pltpu
from jax.sharding import PartitionSpec as P

HQ = 12
HD = 128
WINDOW = 1024
EPSILON = 1e-06

CORE, NEAR, SIDE, GROUP, RING = 1, 2, 4, 4, 8
LONGEST_RING = 8
LOG2E = 1.4426950408889634
LOW = jnp.bfloat16
FULL = jnp.float32
MIB = 1024 * 1024
LIGHT = pl.CostEstimate(flops=1024, bytes_accessed=1024, transcendentals=0)


def flip(array, bit):
    size = lax.axis_size("tok")
    return lax.ppermute(array, "tok", [(i, i ^ bit) for i in range(size)])


def around(array):
    size = lax.axis_size("tok")
    return lax.ppermute(array, "tok", [(i, (i + RING) % size) for i in range(size)])


def passed_along(array, by):
    size = lax.axis_size("tok")
    pairs = [(i, i + by) for i in range(size) if 0 <= i + by < size]
    return lax.ppermute(array, "tok", pairs)


def rms_norm(values, scales):
    return values * lax.rsqrt(jnp.mean(values * values, axis=-1, keepdims=True) + EPSILON) * scales


def outer_sum(left_side, right_side):
    return lax.dot_general(
        left_side, right_side, (((0,), (0,)), ((), ())), preferred_element_type=FULL
    )


def by_rows(left_side, right_side):
    return lax.dot_general(
        left_side, right_side, (((1,), (1,)), ((), ())), preferred_element_type=FULL
    )


def matmul(left_side, right_side):
    return jnp.dot(left_side, right_side, preferred_element_type=FULL)


def pick(array, index):
    return lax.dynamic_index_in_dim(array, index, 0, keepdims=False)


def place():
    device = lax.axis_index("tok")
    return device, device % 2, (device // 2) % 2, (device // 4) % 2, device // RING


def rows_to_group(array):
    two = jnp.concatenate([array, flip(array, NEAR)], axis=0)
    return jnp.concatenate([two, flip(two, CORE)], axis=0)


def rows_from_group(partial):
    half = partial.shape[0] // 2
    two = partial[:half].astype(FULL) + flip(partial[half:].astype(LOW), CORE).astype(FULL)
    quarter = half // 2
    return two[:quarter] + flip(two[quarter:].astype(LOW), NEAR).astype(FULL)


def slices_to_group(parts):
    _, core, near, _, _ = place()
    rows, columns = parts.shape[1:]
    mine = lax.dynamic_slice_in_dim(parts, 2 * near, 2, 0)
    theirs = flip(lax.dynamic_slice_in_dim(parts, 2 * (1 - near), 2, 0), NEAR)
    here = jnp.stack([pick(mine, core), pick(theirs, core)])
    away = flip(jnp.stack([pick(mine, 1 - core), pick(theirs, 1 - core)]), CORE)
    by_core = jnp.where(core == 0, jnp.stack([here, away], 1), jnp.stack([away, here], 1))
    by_near = jnp.where(near == 0, by_core, by_core[::-1])
    return by_near.reshape(4 * rows, columns)


def slices_from_group(block):
    _, core, near, _, _ = place()
    rows, columns = block.shape[0] // 4, block.shape[1]
    parts = block.astype(LOW).reshape(2, 2, rows, columns)
    mine, theirs = pick(parts, near), flip(pick(parts, 1 - near), NEAR)
    here = jnp.stack([pick(mine, core), pick(theirs, core)])
    away = flip(jnp.stack([pick(mine, 1 - core), pick(theirs, 1 - core)]), CORE)
    by_core = jnp.where(core == 0, jnp.stack([here, away], 1), jnp.stack([away, here], 1))
    by_near = jnp.where(near == 0, by_core, by_core[::-1])
    return by_near.reshape(4, rows, columns)


def gather_kernel(
    ring, bands, attn_ref, ffn_ref, attn_out, ffn_out, local_sem, send_sem, recv_sem
):
    size = ring * RING
    me = lax.axis_index("tok")
    core, near, side, z = me % 2, (me // 2) % 2, (me // 4) % 2, me // RING
    core_mate, near_mate, side_mate = me + 1 - 2 * core, me + 2 - 4 * near, me + 4 - 8 * side
    far_mate = near_mate + 1 - 2 * core
    up, down = (me + RING) % size, (me + size - RING) % size

    barrier = pltpu.get_barrier_semaphore()
    partners = (core_mate, near_mate, side_mate, far_mate, up, down)
    for partner in partners:
        pl.semaphore_signal(
            barrier, inc=1, device_id=(partner,), device_id_type=pl.DeviceIdType.MESH
        )
    pl.semaphore_wait(barrier, len(partners))

    own = pltpu.make_async_copy(attn_ref, attn_out.at[z, side, near, core], local_sem.at[0])
    own.start()
    own_slice = pltpu.make_async_copy(
        ffn_ref.at[2 * near + core], ffn_out.at[2 * near + core], local_sem.at[1]
    )
    own_slice.start()

    copies = []

    def send(src, dst, to):
        index = len(copies)
        copy = pltpu.make_async_remote_copy(
            src_ref=src,
            dst_ref=dst,
            send_sem=send_sem.at[index],
            recv_sem=recv_sem.at[index],
            device_id=(to,),
            device_id_type=pl.DeviceIdType.MESH,
        )
        copy.start()
        copies.append(copy)
        return copy

    def forward(ref, to):
        return send(ref, ref, to)

    def chunk_of(step):
        return (z - step + ring) % ring

    def piece(step, band):
        return attn_out.at[chunk_of(step), side, near, core, bands[band]]

    hops, first, second, last = {}, {}, {}, {}
    over = []

    def finish(step):
        first[0, step].wait_recv()
        second[0, step] = forward(attn_out.at[chunk_of(step), side, :, core, bands[0]], side_mate)
        first[1, step].wait_recv()
        second[1, step] = forward(attn_out.at[chunk_of(step), :, near, core, bands[1]], near_mate)

    def hand_over(step):
        second[0, step].wait_recv()
        second[1, step].wait_recv()
        over.append(forward(attn_out.at[chunk_of(step), :, :, core], core_mate))

    for step in range(ring):
        for band in (0, 1):
            if step > 0:
                hops[band, step].wait_recv()
            source = attn_ref.at[bands[band]] if step == 0 else piece(step, band)
            if step < ring - 1:
                hops[band, step + 1] = send(source, piece(step, band), up)
            mate = near_mate if band == 0 else side_mate
            first[band, step] = send(source, piece(step, band), mate)
        if step == 0:
            begun = send(attn_ref.at[bands[2]], piece(0, 2), near_mate)
            slices = [
                send(ffn_ref.at[index], ffn_out.at[2 * near + core], mate)
                for mate, index in (
                    (near_mate, 2 * (1 - near) + core),
                    (far_mate, 2 * (1 - near) + 1 - core),
                    (core_mate, 2 * near + 1 - core),
                )
            ]
            own.wait()
            begun.wait_recv()
            last[0] = forward(attn_out.at[z, side, :, core, bands[2]], side_mate)
        else:
            last[step - 1].wait_recv()
            last[step] = forward(attn_out.at[chunk_of(step - 1), :, :, core, bands[2]], up)
            finish(step - 1)
        if step >= 2:
            hand_over(step - 2)
    finish(ring - 1)
    hand_over(ring - 2)
    last[ring - 1].wait_recv()
    hand_over(ring - 1)
    own_slice.wait()
    for copy in slices + over:
        copy.wait_recv()
    for copy in copies:
        copy.wait_send()


def gather(attn_pack, ffn_pack):
    size = lax.axis_size("tok")
    ring = size // RING
    rows, columns = attn_pack.shape
    if ring > LONGEST_RING or ring < 2 or rows % 48:
        return lax.all_gather(attn_pack, "tok", axis=0, tiled=True), slices_to_group(ffn_pack)
    third = rows // 3
    bands = [pl.ds(third * band, third) for band in range(3)]
    count = 3 + 2 * (ring - 1) + 2 * ring + 2 * ring + 1 + ring + ring
    anywhere = pl.BlockSpec(memory_space=pl.ANY)
    attn_all, ffn_rows = pl.pallas_call(
        functools.partial(gather_kernel, ring, bands),
        in_specs=[anywhere] * 2,
        out_specs=[anywhere] * 2,
        out_shape=[
            jax.ShapeDtypeStruct((ring, 2, 2, 2, rows, columns), attn_pack.dtype),
            jax.ShapeDtypeStruct(ffn_pack.shape, ffn_pack.dtype),
        ],
        scratch_shapes=[
            pltpu.SemaphoreType.DMA((2,)),
            pltpu.SemaphoreType.DMA((count,)),
            pltpu.SemaphoreType.DMA((count,)),
        ],
        compiler_params=pltpu.CompilerParams(collective_id=0, has_side_effects=True),
    )(attn_pack, ffn_pack)
    return attn_all.reshape(size * rows, columns), ffn_rows.reshape(GROUP * rows, -1)


def scatter_kernel(
    ring, bands, edges, *refs
):
    count = len(edges) - 1
    grad_refs, ffn_ref, attn_out, ffn_out = refs[:count], refs[count], refs[count + 1], refs[count + 2]
    pack, core_in, a_side, a_near, a_ring, b_near, b_side, b_ring, c_ring, c_side, c_near = refs[
        count + 3 : count + 14
    ]
    local_sem, send_sem, recv_sem = refs[count + 14 :]
    size = ring * RING
    me = lax.axis_index("tok")
    core, near, side, z = me % 2, (me // 2) % 2, (me // 4) % 2, me // RING
    core_mate, near_mate, side_mate = me + 1 - 2 * core, me + 2 - 4 * near, me + 4 - 8 * side
    far_mate = near_mate + 1 - 2 * core
    up, down = (me + RING) % size, (me + size - RING) % size

    def chunk_of(step):
        return (z - 1 - step + 2 * ring) % ring

    loads = []
    for step in range(ring):
        row = []
        for k in range(count):
            load = pltpu.make_async_copy(
                grad_refs[k].at[chunk_of(step)],
                pack.at[chunk_of(step), :, :, :, :, pl.ds(edges[k], edges[k + 1] - edges[k])],
                local_sem.at[step * count + k],
            )
            load.start()
            row.append(load)
        loads.append(row)
    own_slice = pltpu.make_async_copy(
        ffn_ref.at[2 * near + core], ffn_out.at[2 * near + core], local_sem.at[ring * count]
    )
    own_slice.start()

    barrier = pltpu.get_barrier_semaphore()
    partners = (core_mate, near_mate, side_mate, far_mate, up, down)
    for partner in partners:
        pl.semaphore_signal(
            barrier, inc=1, device_id=(partner,), device_id_type=pl.DeviceIdType.MESH
        )
    pl.semaphore_wait(barrier, len(partners))

    copies = []

    def send(src, dst, to):
        index = len(copies)
        copy = pltpu.make_async_remote_copy(
            src_ref=src,
            dst_ref=dst,
            send_sem=send_sem.at[index],
            recv_sem=recv_sem.at[index],
            device_id=(to,),
            device_id_type=pl.DeviceIdType.MESH,
        )
        copy.start()
        copies.append(copy)
        return copy

    def add(held, arrived):
        held[...] = (held[...].astype(FULL) + arrived[...].astype(FULL)).astype(LOW)

    def part(step, y, x, band):
        return pack.at[chunk_of(step), y, x, core, bands[band]]

    def own(step, band):
        return part(step, side, near, band)

    across, first, second, hops = {}, {}, {}, {}

    def begin(step):
        chunk = chunk_of(step)
        across[step].wait_recv()

        def one(k, _):
            add(pack.at[chunk, k // 2, k % 2, core], core_in.at[chunk, k // 2, k % 2])
            return 0

        lax.fori_loop(0, 4, one, 0)
        first[0, step] = send(
            pack.at[chunk, 1 - side, :, core, bands[0]], a_side.at[step], side_mate
        )
        first[1, step] = send(
            pack.at[chunk, :, 1 - near, core, bands[1]], b_near.at[step], near_mate
        )
        if step > 0:
            hops[2, step].wait_recv()
            for k in range(4):
                add(part(step, k // 2, k % 2, 2), c_ring.at[step - 1, k // 2, k % 2])
        if step < ring - 1:
            hops[2, step + 1] = send(
                pack.at[chunk, :, :, core, bands[2]], c_ring.at[step], up
            )

    def middle(step):
        first[0, step].wait_recv()
        for x in range(2):
            add(part(step, side, x, 0), a_side.at[step, x])
        second[0, step] = send(part(step, side, 1 - near, 0), a_near.at[step], near_mate)
        first[1, step].wait_recv()
        for y in range(2):
            add(part(step, y, near, 1), b_near.at[step, y])
        second[1, step] = send(part(step, 1 - side, near, 1), b_side.at[step], side_mate)

    def end(step):
        for band, arrived, passing in ((0, a_near, a_ring), (1, b_side, b_ring)):
            second[band, step].wait_recv()
            add(own(step, band), arrived.at[step])
            if step > 0:
                hops[band, step].wait_recv()
                add(own(step, band), passing.at[step - 1])
            if step < ring - 1:
                hops[band, step + 1] = send(own(step, band), passing.at[step], up)

    for step in range(ring):
        for load in loads[step]:
            load.wait()
        across[step] = send(
            pack.at[chunk_of(step), :, :, 1 - core], core_in.at[chunk_of(step)], core_mate
        )
    slices = []
    for step in range(ring + 2):
        if step < ring:
            begin(step)
        if step == 0:
            slices += [
                send(ffn_ref.at[index], ffn_out.at[2 * near + core], mate)
                for mate, index in (
                    (near_mate, 2 * (1 - near) + core),
                    (far_mate, 2 * (1 - near) + 1 - core),
                    (core_mate, 2 * near + 1 - core),
                )
            ]
        if 1 <= step <= ring:
            middle(step - 1)
        if step == ring:
            last = ring - 1
            to_side = send(pack.at[z, 1 - side, :, core, bands[2]], c_side, side_mate)
        if step >= 2:
            end(step - 2)
        if step == ring:
            to_side.wait_recv()
            for x in range(2):
                add(part(last, side, x, 2), c_side.at[x])
            to_near = send(part(last, side, 1 - near, 2), c_near, near_mate)
    to_near.wait_recv()
    add(own(last, 2), c_near)
    attn_out[...] = pack[z, side, near, core].astype(FULL)
    own_slice.wait()
    for copy in slices:
        copy.wait_recv()
    for copy in copies:
        copy.wait_send()


def scatter(grads, ffn_sum):
    size = lax.axis_size("tok")
    ring = size // RING
    rows = grads[0].shape[0] // size
    if ring > LONGEST_RING or ring < 2 or rows % 48:
        joined = jnp.concatenate(grads, axis=1).astype(FULL)
        return (
            lax.psum_scatter(joined, "tok", scatter_dimension=0, tiled=True),
            slices_from_group(ffn_sum),
        )
    third = rows // 3
    bands = [pl.ds(third * band, third) for band in range(3)]
    edges = [0]
    for grad in grads:
        edges.append(edges[-1] + grad.shape[1])
    columns = edges[-1]
    count = ring + 2 * ring + (ring - 1) + 3 + 2 * ring + 1 + 2 * (ring - 1) + 1
    anywhere = pl.BlockSpec(memory_space=pl.ANY)
    band = (third, columns)
    low = lambda *shape: pltpu.VMEM((*shape, *band), LOW)
    return pl.pallas_call(
        functools.partial(scatter_kernel, ring, bands, edges),
        in_specs=[anywhere] * (len(grads) + 1),
        out_specs=[pl.BlockSpec(memory_space=pltpu.VMEM), anywhere],
        out_shape=[
            jax.ShapeDtypeStruct((rows, columns), FULL),
            jax.ShapeDtypeStruct((GROUP, rows, ffn_sum.shape[1]), LOW),
        ],
        scratch_shapes=[
            pltpu.VMEM((ring, 2, 2, 2, rows, columns), LOW),
            pltpu.VMEM((ring, 2, 2, rows, columns), LOW),
            low(ring, 2),
            low(ring),
            low(ring - 1),
            low(ring, 2),
            low(ring),
            low(ring - 1),
            low(ring - 1, 2, 2),
            low(2),
            low(),
            pltpu.SemaphoreType.DMA((ring * len(grads) + 1,)),
            pltpu.SemaphoreType.DMA((count,)),
            pltpu.SemaphoreType.DMA((count,)),
        ],
        compiler_params=pltpu.CompilerParams(
            collective_id=1, has_side_effects=True, vmem_limit_bytes=44 * MIB
        ),
    )(
        *[grad.reshape(ring, 2, 2, 2, rows, -1) for grad in grads],
        ffn_sum.astype(LOW).reshape(GROUP, rows, -1),
    )


def after(value, *marks):
    return lax.optimization_barrier((value, *marks))[0]


def groups_of(stride):
    size = lax.axis_size("tok")
    return [[s + stride * k for k in range(size // stride)] for s in range(stride)]


def spread(block):
    size = lax.axis_size("tok")
    ring = size // RING
    if ring > LONGEST_RING:
        gathered = lax.all_gather(
            block, "tok", axis=0, tiled=True, axis_index_groups=groups_of(GROUP)
        )
        return gathered, []
    _, _, _, side, z = place()
    rows, columns = block.shape
    total = jnp.zeros((ring, 2, rows, columns), block.dtype)
    own, arrivals = block, []
    for step in range(ring):
        chunk = lax.rem(z - step + ring, ring)
        for piece, y in ((own, side), (flip(own, SIDE), 1 - side)):
            total = lax.dynamic_update_slice(total, piece[None, None], (chunk, y, 0, 0))
        if step < ring - 1:
            own = around(own)
            arrivals.append(own)
    return total.reshape(ring * 2 * rows, columns), arrivals


class Reduction:
    def __init__(self, normed, cotangent, array):
        self.given = (normed, cotangent, array)
        self.size = lax.axis_size("tok")
        self.ring = self.size // RING
        _, _, _, self.side, self.z = place()
        self.rows = normed.shape[1] // (self.ring * 2)
        self.short = 2 <= self.ring <= LONGEST_RING and self.rows % 64 == 0
        self.blocks, self.crossing, self.total = {}, None, None

    def multiply(self, step, mark=None):
        if not self.short:
            return ()
        chunk = lax.rem(self.z - 1 - step + 2 * self.ring, self.ring)
        normed, cotangent, array = self.given
        array = after(array, *jax.tree.leaves(mark))
        product = outer_products(normed, cotangent, array, chunk, 2 * self.rows)
        self.blocks[step] = product.reshape(2, self.rows, -1)
        return self.blocks[step]

    def begin(self):
        if self.short:
            self.crossing = flip(pick(self.blocks[0], 1 - self.side), SIDE)

    def advance(self, step, *marks):
        if not self.short:
            return ()
        arrived = (self.crossing,) if self.total is None else (self.crossing, self.total)
        block = self.blocks[min(step + 1, self.ring - 1)]
        block, *arrived = lax.optimization_barrier((block, *arrived, *marks))[: len(arrived) + 1]
        total = pick(self.blocks[step], self.side).astype(FULL)
        for part in arrived:
            total = total + part.astype(FULL)
        if step == self.ring - 1:
            self.sum = total.astype(LOW)
            return (self.sum,)
        low, give = total.astype(LOW), pick(block, 1 - self.side)
        self.total, self.crossing = around(low), flip(give, SIDE)
        return (low, give)

    def result(self):
        if self.short:
            return self.sum
        normed, cotangent, array = self.given
        joined = jnp.concatenate(
            [outer_sum(normed, array[0]), outer_sum(normed, array[1]), outer_sum(cotangent, array[2])],
            axis=1,
        )
        return lax.psum_scatter(
            joined, "tok", scatter_dimension=0, tiled=True, axis_index_groups=groups_of(GROUP)
        )


def turn(values, cosine, sine):
    return values * cosine + pltpu.roll(values, HD // 2, 1) * sine


def mask_into(bias, key_segments, query_segments, block):
    keys, queries = bias.shape
    for start in range(0, queries, block):
        offset = (
            lax.broadcasted_iota(jnp.int32, (keys, block), 0)
            - lax.broadcasted_iota(jnp.int32, (keys, block), 1)
            - start
        )
        same = key_segments[...] == query_segments[:, start : start + block]
        allowed = same & (offset > 0) & (offset <= WINDOW)
        bias[:, start : start + block] = jnp.where(allowed, 0.0, -jnp.inf)


def attend_kernel(
    block, factor, q_ref, key_ref, value_t_ref, ks_ref, qs_ref, cos_ref, sin_ref,
    rot_ref, mixed_ref, log_ref, bias,
):
    @pl.when(pl.program_id(0) == 0)
    def _():
        mask_into(bias, ks_ref, qs_ref, block)

    queries = q_ref.shape[0]
    rot_ref[...] = turn(q_ref[...], cos_ref[...], sin_ref[...]).astype(LOW)
    for start in range(0, queries, block):
        rows, span = pl.ds(start, block), pl.ds(start, WINDOW + block)
        raw = by_rows(key_ref[span, :], rot_ref[rows, :])
        score = raw * factor + bias[span, rows]
        top = jnp.max(score, axis=0, keepdims=True)
        expo = jnp.exp2(score - top)
        total = jnp.sum(expo, axis=0, keepdims=True)
        mixed_t = matmul(value_t_ref[:, span], expo.astype(LOW)) / total
        mixed_ref[rows, :] = mixed_t.T.astype(LOW)
        log_ref[0, :, rows] = top + jnp.log2(total)


def attend(raw_query, key_value, key_segments, query_segments, cosine, sine, first, heads):
    queries, width = raw_query.shape[0], heads * HD
    keys = key_value.shape[0]
    block = min(256, queries)
    head = pl.BlockSpec((queries, HD), lambda h: (0, h))
    whole = lambda shape: pl.BlockSpec(shape, lambda h: (0,) * len(shape))
    return pl.pallas_call(
        functools.partial(attend_kernel, block, HD**-0.5 * LOG2E),
        grid=(heads,),
        in_specs=[
            pl.BlockSpec((queries, HD), lambda h: (0, first + h)),
            whole((keys, HD)),
            whole((HD, keys)),
            whole((keys, 1)),
            whole((1, queries)),
            whole((queries, HD)),
            whole((queries, HD)),
        ],
        out_specs=[head, head, pl.BlockSpec((1, 1, queries), lambda h: (h, 0, 0))],
        out_shape=[
            jax.ShapeDtypeStruct((queries, width), LOW),
            jax.ShapeDtypeStruct((queries, width), LOW),
            jax.ShapeDtypeStruct((heads, 1, queries), FULL),
        ],
        scratch_shapes=[pltpu.VMEM((keys, queries), FULL)],
        compiler_params=pltpu.CompilerParams(vmem_limit_bytes=40 * MIB),
        cost_estimate=LIGHT,
    )(
        raw_query,
        key_value[:, :HD],
        key_value[:, HD:].T,
        key_segments[:, None],
        query_segments[None, :],
        cosine,
        sine,
    )


def attend_back_kernel(
    block, factor, rot_ref, grad_ref, mixed_ref, log_ref, key_ref, value_ref, key_t_ref, ks_ref, qs_ref,
    cos_ref, sin_ref, query_out, key_out, value_out, bias,
):
    @pl.when(pl.program_id(0) == 0)
    def _():
        mask_into(bias, ks_ref, qs_ref, block)
        key_out[...] = jnp.zeros_like(key_out)
        value_out[...] = jnp.zeros_like(value_out)

    queries = rot_ref.shape[0]
    for start in range(0, queries, block):
        rows, span = pl.ds(start, block), pl.ds(start, WINDOW + block)
        rot, grad = rot_ref[rows, :], grad_ref[rows, :]
        product = grad.astype(FULL) * mixed_ref[rows, :].astype(FULL)
        inner = jnp.sum(product.T, axis=0, keepdims=True)
        raw = by_rows(key_ref[span, :], rot)
        prob = jnp.exp2(raw * factor + (bias[span, rows] - log_ref[0, :, rows]))
        grad_prob = by_rows(value_ref[span, :], grad)
        grad_raw = (prob * (grad_prob - inner)).astype(LOW)
        value_out[span, :] += matmul(prob.astype(LOW), grad)
        key_out[span, :] += matmul(grad_raw, rot)
        back = matmul(key_t_ref[:, span], grad_raw).T * HD**-0.5
        query_out[rows, :] = turn(back, cos_ref[rows, :], -sin_ref[rows, :]).astype(LOW)


def attend_back(rot, grad, mixed, logs, key_value, key_segments, query_segments, cosine, sine):
    queries, width = rot.shape
    keys = key_value.shape[0]
    heads = width // HD
    block = min(256, queries)
    head = pl.BlockSpec((queries, HD), lambda h: (0, h))
    whole = lambda shape: pl.BlockSpec(shape, lambda h: (0,) * len(shape))
    return pl.pallas_call(
        functools.partial(attend_back_kernel, block, HD**-0.5 * LOG2E),
        grid=(heads,),
        in_specs=[
            head,
            head,
            head,
            pl.BlockSpec((1, 1, queries), lambda h: (h, 0, 0)),
            whole((keys, HD)),
            whole((keys, HD)),
            whole((HD, keys)),
            whole((keys, 1)),
            whole((1, queries)),
            whole((queries, HD)),
            whole((queries, HD)),
        ],
        out_specs=[head, whole((keys, HD)), whole((keys, HD))],
        out_shape=[
            jax.ShapeDtypeStruct((queries, width), LOW),
            jax.ShapeDtypeStruct((keys, HD), FULL),
            jax.ShapeDtypeStruct((keys, HD), FULL),
        ],
        scratch_shapes=[pltpu.VMEM((keys, queries), FULL)],
        compiler_params=pltpu.CompilerParams(vmem_limit_bytes=40 * MIB),
        cost_estimate=LIGHT,
    )(
        rot,
        grad,
        mixed,
        logs,
        key_value[:, :HD],
        key_value[:, HD:],
        key_value[:, :HD].T,
        key_segments[:, None],
        query_segments[None, :],
        cosine,
        sine,
    )


GELU_A = 0.7978845608028654
GELU_B = 0.044715


def hidden_kernel(normed_ref, cot_ref, gate_ref, up_ref, down_ref, out_ref):
    gate = matmul(normed_ref[...], gate_ref[...])
    up = matmul(normed_ref[...], up_ref[...])
    grad_hidden = matmul(cot_ref[...], down_ref[...])
    square = gate * gate
    bent = jnp.tanh(gate * (GELU_A + GELU_A * GELU_B * square))
    half = 0.5 * (1.0 + bent)
    value = gate * half
    slope = half + 0.5 * gate * (1.0 - bent * bent) * (GELU_A + 3.0 * GELU_A * GELU_B * square)
    out_ref[0] = (grad_hidden * up * slope).astype(LOW)
    out_ref[1] = (grad_hidden * value).astype(LOW)
    out_ref[2] = (value * up).astype(LOW)


def hidden_and_grads(normed, cotangent, pack):
    tokens, width = normed.shape
    columns = pack.shape[1] // 3
    rows, wide = min(256, tokens), columns
    steps = columns // wide
    token_block = pl.BlockSpec((rows, width), lambda j, i: (i, 0))
    weight_blocks = [
        pl.BlockSpec(
            (width, wide),
            lambda j, i, part=part: (0, part * steps + j),
            pipeline_mode=pl.Buffered(1),
        )
        for part in range(3)
    ]
    return pl.pallas_call(
        hidden_kernel,
        grid=(steps, tokens // rows),
        in_specs=[token_block, token_block, *weight_blocks],
        out_specs=pl.BlockSpec((3, rows, wide), lambda j, i: (0, i, j)),
        out_shape=jax.ShapeDtypeStruct((3, tokens, columns), LOW),
        compiler_params=pltpu.CompilerParams(vmem_limit_bytes=48 * MIB),
        cost_estimate=LIGHT,
    )(normed, cotangent, pack, pack, pack)


def project_sum_kernel(count, blocks, array_ref, *refs):
    weight_refs, out_ref = refs[:count], refs[count]
    away, arrived, send_sem, recv_sem = refs[count + 1 :]
    step, column = pl.program_id(0), pl.program_id(1)
    columns, rows = pl.num_programs(1), out_ref.shape[0]
    me = lax.axis_index("tok")
    mate = me + 1 - 2 * (me % 2)

    def crossing(block):
        return pltpu.make_async_remote_copy(
            src_ref=away.at[block],
            dst_ref=arrived.at[block],
            send_sem=send_sem.at[block],
            recv_sem=recv_sem.at[block],
            device_id=(mate,),
            device_id_type=pl.DeviceIdType.MESH,
        )

    @pl.when((step == 0) & (column == 0))
    def _():
        barrier = pltpu.get_barrier_semaphore()
        pl.semaphore_signal(
            barrier, inc=1, device_id=(mate,), device_id_type=pl.DeviceIdType.MESH
        )
        pl.semaphore_wait(barrier, 1)

    total = by_rows(array_ref[0], weight_refs[0][...])
    for k in range(1, count):
        total += by_rows(array_ref[k], weight_refs[k][...])
    for block in range(blocks):

        @pl.when(step == block)
        def _():
            away[block, column] = total.astype(LOW)

            @pl.when(column == columns - 1)
            def _():
                crossing(block).start()

        @pl.when(step == blocks + block)
        def _():
            @pl.when(column == 0)
            def _():
                crossing(block).wait()

            out_ref[...] = (total + arrived[block, column].astype(FULL)).astype(LOW)


def project_sum(array, pack, first, count, identity, marks=()):
    array = after(array, *jax.tree.leaves(marks))
    tokens, columns = array.shape[1:]
    width = pack.shape[0]
    rows, wide = tokens // 4, 512
    blocks = tokens // rows // 2
    return pl.pallas_call(
        functools.partial(project_sum_kernel, count, blocks),
        grid=(2 * blocks, width // wide),
        in_specs=[
            pl.BlockSpec(
                (count, rows, columns), lambda i, j: (first // count, (i + blocks) % (2 * blocks), 0)
            )
        ]
        + [pl.BlockSpec((wide, columns), lambda i, j, k=k: (j, first + k)) for k in range(count)],
        out_specs=pl.BlockSpec(
            (rows, wide),
            lambda i, j: (jnp.maximum(i - blocks, 0), jnp.where(i >= blocks, j, 0)),
        ),
        out_shape=jax.ShapeDtypeStruct((tokens // 2, width), LOW),
        scratch_shapes=[
            pltpu.VMEM((blocks, width // wide, rows, wide), LOW),
            pltpu.VMEM((blocks, width // wide, rows, wide), LOW),
            pltpu.SemaphoreType.DMA((blocks,)),
            pltpu.SemaphoreType.DMA((blocks,)),
        ],
        compiler_params=pltpu.CompilerParams(
            collective_id=identity, has_side_effects=True, vmem_limit_bytes=44 * MIB
        ),
        cost_estimate=LIGHT,
    )(array, *([pack] * count))


def outer_kernel(steps, chunk_ref, normed_ref, cot_ref, right_ref, out_ref, left):
    for start, ref in ((0, normed_ref), (2 * steps, cot_ref)):

        @pl.when(pl.program_id(0) == start)
        def _():
            left[...] = ref[...].T

    out_ref[...] = matmul(left[...], right_ref[0]).astype(LOW)


def outer_products(normed, cotangent, array, chunk, rows):
    tokens, columns = array.shape[1:]
    wide = columns
    steps = columns // wide
    left = pl.BlockSpec((tokens, rows), lambda j, chunk_ref: (0, chunk_ref[0]))
    return pl.pallas_call(
        functools.partial(outer_kernel, steps),
        grid_spec=pltpu.PrefetchScalarGridSpec(
            num_scalar_prefetch=1,
            grid=(3 * steps,),
            in_specs=[
                left,
                left,
                pl.BlockSpec((1, tokens, wide), lambda j, chunk_ref: (j // steps, 0, j % steps)),
            ],
            out_specs=pl.BlockSpec((rows, wide), lambda j, chunk_ref: (0, j)),
            scratch_shapes=[pltpu.VMEM((rows, tokens), LOW)],
        ),
        out_shape=jax.ShapeDtypeStruct((rows, 3 * columns), LOW),
        compiler_params=pltpu.CompilerParams(vmem_limit_bytes=40 * MIB),
        cost_estimate=LIGHT,
    )(chunk[None].astype(jnp.int32), normed, cotangent, array)


def on_device(
    tokens, cotangent, attn_gain, ffn_gain, w_query, w_key, w_value, w_out, w_gate, w_up, w_down,
    segments, positions,
):
    token_count, width = tokens.shape
    own_rows, hidden_width = w_gate.shape
    slice_width = hidden_width // GROUP
    heads_width = w_query.shape[1]
    tail_rows = min(token_count, WINDOW)
    hop_count = WINDOW // tail_rows
    device = lax.axis_index("tok")
    inputs = tokens.astype(FULL)

    frequency = 10000.0 ** (-jnp.arange(HD // 2, dtype=FULL) * 2.0 / HD)
    angles = positions.astype(FULL)[:, None] * frequency[None, :]
    cosine = jnp.concatenate([jnp.cos(angles)] * 2, axis=1)
    sine_half = jnp.sin(angles)
    sine = jnp.concatenate([-sine_half, sine_half], axis=1)
    padded_segments = jnp.concatenate([jnp.full((WINDOW,), -1, jnp.int32), segments])
    key_segments = lax.dynamic_slice_in_dim(
        padded_segments, device * token_count, WINDOW + token_count
    )
    query_segments = lax.dynamic_slice_in_dim(segments, device * token_count, token_count)

    attn_pack = jnp.concatenate(
        [
            w_query,
            w_key,
            w_value,
            w_out,
            jnp.pad(
                jnp.stack([attn_gain, ffn_gain], axis=1), ((0, 0), (0, HD - 2))
            ),
        ],
        axis=1,
    )
    edge = heads_width + 2 * HD
    def sliced(weight):
        return weight.reshape(own_rows, GROUP, slice_width).transpose(1, 0, 2)

    ffn_pack = jnp.concatenate([sliced(w_gate), sliced(w_up), sliced(w_down)], axis=2)
    attn_all, ffn_rows = gather(attn_pack, ffn_pack)
    query_w, kv_w = attn_all[:, :heads_width], attn_all[:, heads_width:edge]
    out_w = attn_all[:, edge : edge + heads_width]
    gains = attn_all[:, edge + heads_width : edge + heads_width + 2].astype(FULL)
    gain_one, gain_two = gains[:, 0], gains[:, 1]

    ffn_w, arrivals = spread(ffn_rows)
    gate_up_w, down_w = ffn_w[:, : 2 * slice_width], ffn_w[:, 2 * slice_width :]
    gate_w, up_w = gate_up_w[:, :slice_width], gate_up_w[:, slice_width:]
    cot_group = rows_to_group(after(cotangent, attn_all))

    inverse_one = lax.rsqrt(jnp.mean(inputs * inputs, axis=-1, keepdims=True) + EPSILON)
    normed = (inputs * inverse_one * gain_one).astype(LOW)
    kv = matmul(normed, kv_w)

    def turned(values, sine_signed):
        half = HD // 2
        rolled = jnp.concatenate([values[:, half:], values[:, :half]], axis=1)
        return values * cosine + rolled * sine_signed

    key_value = jnp.concatenate([turned(kv[:, :HD], sine), kv[:, HD:]], axis=1).astype(LOW)
    received = [passed_along(key_value, hop) for hop in range(hop_count, 0, -1)]
    all_keys = jnp.concatenate(received + [key_value], axis=0)
    raw_query = matmul(normed, query_w)
    heads = heads_width // HD
    given = (all_keys, key_segments, query_segments, cosine, sine)
    early = attend(raw_query, *given, 0, heads // 2)
    late = attend(
        after(raw_query, early[1], *arrivals[:1]), *given, heads // 2, heads - heads // 2
    )
    rot, mixed = (jnp.concatenate([early[k], late[k]], axis=1) for k in range(2))
    logs = jnp.concatenate([early[2], late[2]], axis=0)
    middle = inputs + by_rows(mixed, out_w)
    inverse_two = lax.rsqrt(jnp.mean(middle * middle, axis=-1, keepdims=True) + EPSILON)
    normed_two = (middle * inverse_two * gain_two).astype(LOW)

    normed_group = rows_to_group(after(normed_two, *arrivals[1:2]))
    hidden_pack = hidden_and_grads(normed_group, cot_group, ffn_w)
    reduction = Reduction(normed_group, cot_group, hidden_pack)
    pairs_done = reduction.multiply(0)
    reduction.begin()
    pairs_done = reduction.multiply(1, pairs_done)
    group_sum = project_sum(hidden_pack, ffn_w, 0, 2, 2, pairs_done)
    near_sent = flip(group_sum[token_count:], NEAR)
    marks = reduction.advance(0, group_sum)
    pairs_done = reduction.multiply(2, marks)
    pairs_done = reduction.multiply(3, pairs_done)
    marks = reduction.advance(1, pairs_done)
    output_sum = project_sum(hidden_pack, ffn_w, 2, 1, 3, marks)
    output_near = flip(after(output_sum, near_sent)[token_count:], NEAR)
    grad_normed_two = group_sum[:token_count].astype(FULL) + after(near_sent, output_sum).astype(FULL)

    scaled = grad_normed_two * gain_two
    grad_middle = (
        cotangent.astype(FULL)
        + inverse_two * scaled
        - middle * inverse_two**3 * jnp.mean(scaled * middle, axis=-1, keepdims=True)
    )
    branch = grad_middle.astype(LOW)
    grad_mixed = matmul(branch, out_w).astype(LOW)
    grad_out_w = outer_sum(branch, mixed).astype(LOW)
    marks = reduction.advance(2, grad_mixed)
    query_low, key_grads, value_grads = attend_back(
        rot, after(grad_mixed, *marks), mixed, logs, all_keys, key_segments, query_segments, cosine, sine
    )
    output = (
        middle + output_sum[:token_count].astype(FULL) + after(output_near, query_low).astype(FULL)
    ).astype(LOW)
    grads = jnp.concatenate([key_grads * HD**-0.5, value_grads], axis=1)
    shares = grads[WINDOW:]
    for hop in range(1, hop_count + 1):
        first_row = (hop_count - hop) * tail_rows
        returned = passed_along(grads[first_row : first_row + tail_rows].astype(LOW), -hop)
        shares = shares.at[token_count - tail_rows :].add(returned.astype(FULL))
    kv_low = jnp.concatenate([turned(shares[:, :HD], -sine), shares[:, HD:]], axis=1).astype(LOW)
    grad_query_w = outer_sum(normed, query_low).astype(LOW)
    grad_kv_w = outer_sum(normed, kv_low).astype(LOW)
    grad_normed = by_rows(query_low, query_w) + by_rows(kv_low, kv_w)
    scaled_one = grad_normed * gain_one
    grad_inputs = inverse_one * scaled_one - inputs * inverse_one**3 * jnp.mean(
        scaled_one * inputs, axis=-1, keepdims=True
    )
    grad_tokens = (grad_middle + grad_inputs).astype(LOW)
    lane = lax.broadcasted_iota(jnp.int32, (token_count, HD), 1)
    grad_gains = (
        outer_sum((grad_normed * inputs * inverse_one).astype(LOW), (lane == 0).astype(LOW))
        + outer_sum((grad_normed_two * middle * inverse_two).astype(LOW), (lane == 1).astype(LOW))
    ).astype(LOW)
    reduction.advance(3, grad_query_w)
    attn_sum, ffn_parts = scatter(
        [grad_query_w, grad_kv_w, grad_out_w, grad_gains], reduction.result()
    )

    def joined(parts):
        return parts.transpose(1, 0, 2).reshape(own_rows, hidden_width).astype(FULL)

    return (
        output,
        grad_tokens,
        attn_sum[:, edge + heads_width],
        attn_sum[:, edge + heads_width + 1],
        attn_sum[:, :heads_width],
        attn_sum[:, heads_width : heads_width + HD],
        attn_sum[:, heads_width + HD : edge],
        attn_sum[:, edge : edge + heads_width],
        joined(ffn_parts[:, :, :slice_width]),
        joined(ffn_parts[:, :, slice_width : 2 * slice_width]),
        joined(ffn_parts[:, :, 2 * slice_width :]),
    )


def solution(mesh):
    rows, flat = P("tok", None), P("tok")
    return jax.shard_map(
        on_device,
        mesh=mesh,
        in_specs=(rows, rows, flat, flat, rows, rows, rows, rows, rows, rows, rows, P(), flat),
        out_specs=(rows, rows, flat, flat, rows, rows, rows, rows, rows, rows, rows),
        check_vma=False,
    )
```

```python
import functools

import jax
import jax.numpy as jnp
from jax import lax
from jax.experimental import pallas as pl
from jax.experimental.pallas import tpu as pltpu
from jax.sharding import PartitionSpec as P

HQ = 12
HD = 128
WINDOW = 1024
EPSILON = 1e-06

CORE, NEAR, SIDE, GROUP, RING = 1, 2, 4, 4, 8
LONGEST_RING = 8
LOG2E = 1.4426950408889634
LOW = jnp.bfloat16
FULL = jnp.float32
MIB = 1024 * 1024
LIGHT = pl.CostEstimate(flops=1024, bytes_accessed=1024, transcendentals=0)


def flip(array, bit):
    size = lax.axis_size("tok")
    return lax.ppermute(array, "tok", [(i, i ^ bit) for i in range(size)])


def around(array):
    size = lax.axis_size("tok")
    return lax.ppermute(array, "tok", [(i, (i + RING) % size) for i in range(size)])


def passed_along(array, by):
    size = lax.axis_size("tok")
    pairs = [(i, i + by) for i in range(size) if 0 <= i + by < size]
    return lax.ppermute(array, "tok", pairs)


def rms_norm(values, scales):
    return values * lax.rsqrt(jnp.mean(values * values, axis=-1, keepdims=True) + EPSILON) * scales


def outer_sum(left_side, right_side):
    return lax.dot_general(
        left_side, right_side, (((0,), (0,)), ((), ())), preferred_element_type=FULL
    )


def by_rows(left_side, right_side):
    return lax.dot_general(
        left_side, right_side, (((1,), (1,)), ((), ())), preferred_element_type=FULL
    )


def matmul(left_side, right_side):
    return jnp.dot(left_side, right_side, preferred_element_type=FULL)


def pick(array, index):
    return lax.dynamic_index_in_dim(array, index, 0, keepdims=False)


def place():
    device = lax.axis_index("tok")
    return device, device % 2, (device // 2) % 2, (device // 4) % 2, device // RING


def rows_to_group(array, marks=()):
    two = jnp.concatenate([array, after(flip(array, NEAR), *marks)], axis=0)
    return two, flip(two, CORE)


def slices_to_group(parts):
    _, core, near, _, _ = place()
    rows, columns = parts.shape[1:]
    mine = lax.dynamic_slice_in_dim(parts, 2 * near, 2, 0)
    theirs = flip(lax.dynamic_slice_in_dim(parts, 2 * (1 - near), 2, 0), NEAR)
    here = jnp.stack([pick(mine, core), pick(theirs, core)])
    away = flip(jnp.stack([pick(mine, 1 - core), pick(theirs, 1 - core)]), CORE)
    by_core = jnp.where(core == 0, jnp.stack([here, away], 1), jnp.stack([away, here], 1))
    by_near = jnp.where(near == 0, by_core, by_core[::-1])
    return by_near.reshape(4 * rows, columns)


def slices_from_group(block):
    _, core, near, _, _ = place()
    rows, columns = block.shape[0] // 4, block.shape[1]
    parts = block.astype(LOW).reshape(2, 2, rows, columns)
    mine, theirs = pick(parts, near), flip(pick(parts, 1 - near), NEAR)
    here = jnp.stack([pick(mine, core), pick(theirs, core)])
    away = flip(jnp.stack([pick(mine, 1 - core), pick(theirs, 1 - core)]), CORE)
    by_core = jnp.where(core == 0, jnp.stack([here, away], 1), jnp.stack([away, here], 1))
    by_near = jnp.where(near == 0, by_core, by_core[::-1])
    return by_near.reshape(4, rows, columns)


def gather_kernel(
    ring, bands, attn_ref, ffn_ref, attn_out, ffn_out, local_sem, send_sem, recv_sem
):
    size = ring * RING
    me = lax.axis_index("tok")
    core, near, side, z = me % 2, (me // 2) % 2, (me // 4) % 2, me // RING
    core_mate, near_mate, side_mate = me + 1 - 2 * core, me + 2 - 4 * near, me + 4 - 8 * side
    far_mate = near_mate + 1 - 2 * core
    up, down = (me + RING) % size, (me + size - RING) % size

    barrier = pltpu.get_barrier_semaphore()
    partners = (core_mate, near_mate, side_mate, far_mate, up, down)
    for partner in partners:
        pl.semaphore_signal(
            barrier, inc=1, device_id=(partner,), device_id_type=pl.DeviceIdType.MESH
        )
    pl.semaphore_wait(barrier, len(partners))

    own = pltpu.make_async_copy(attn_ref, attn_out.at[z, side, near, core], local_sem.at[0])
    own.start()
    own_slice = pltpu.make_async_copy(
        ffn_ref.at[2 * near + core], ffn_out.at[2 * near + core], local_sem.at[1]
    )
    own_slice.start()

    copies = []

    def send(src, dst, to):
        index = len(copies)
        copy = pltpu.make_async_remote_copy(
            src_ref=src,
            dst_ref=dst,
            send_sem=send_sem.at[index],
            recv_sem=recv_sem.at[index],
            device_id=(to,),
            device_id_type=pl.DeviceIdType.MESH,
        )
        copy.start()
        copies.append(copy)
        return copy

    def forward(ref, to):
        return send(ref, ref, to)

    def chunk_of(step):
        return (z - step + ring) % ring

    def piece(step, band):
        return attn_out.at[chunk_of(step), side, near, core, bands[band]]

    hops, first, second, last = {}, {}, {}, {}
    over = []

    def finish(step):
        first[0, step].wait_recv()
        second[0, step] = forward(attn_out.at[chunk_of(step), side, :, core, bands[0]], side_mate)
        first[1, step].wait_recv()
        second[1, step] = forward(attn_out.at[chunk_of(step), :, near, core, bands[1]], near_mate)

    def hand_over(step):
        second[0, step].wait_recv()
        second[1, step].wait_recv()
        over.append(forward(attn_out.at[chunk_of(step), :, :, core], core_mate))

    for step in range(ring):
        for band in (0, 1):
            if step > 0:
                hops[band, step].wait_recv()
            source = attn_ref.at[bands[band]] if step == 0 else piece(step, band)
            if step < ring - 1:
                hops[band, step + 1] = send(source, piece(step, band), up)
            mate = near_mate if band == 0 else side_mate
            first[band, step] = send(source, piece(step, band), mate)
        if step == 0:
            begun = send(attn_ref.at[bands[2]], piece(0, 2), near_mate)
            slices = [
                send(ffn_ref.at[index], ffn_out.at[2 * near + core], mate)
                for mate, index in (
                    (near_mate, 2 * (1 - near) + core),
                    (far_mate, 2 * (1 - near) + 1 - core),
                    (core_mate, 2 * near + 1 - core),
                )
            ]
            own.wait()
            begun.wait_recv()
            last[0] = forward(attn_out.at[z, side, :, core, bands[2]], side_mate)
        else:
            last[step - 1].wait_recv()
            last[step] = forward(attn_out.at[chunk_of(step - 1), :, :, core, bands[2]], up)
            finish(step - 1)
        if step >= 2:
            hand_over(step - 2)
    finish(ring - 1)
    hand_over(ring - 2)
    last[ring - 1].wait_recv()
    hand_over(ring - 1)
    own_slice.wait()
    for copy in slices + over:
        copy.wait_recv()
    for copy in copies:
        copy.wait_send()


def gather(attn_pack, ffn_pack):
    size = lax.axis_size("tok")
    ring = size // RING
    rows, columns = attn_pack.shape
    if ring > LONGEST_RING or ring < 2 or rows % 48:
        return lax.all_gather(attn_pack, "tok", axis=0, tiled=True), slices_to_group(ffn_pack)
    third = rows // 3
    bands = [pl.ds(third * band, third) for band in range(3)]
    count = 3 + 2 * (ring - 1) + 2 * ring + 2 * ring + 1 + ring + ring
    anywhere = pl.BlockSpec(memory_space=pl.ANY)
    attn_all, ffn_rows = pl.pallas_call(
        functools.partial(gather_kernel, ring, bands),
        in_specs=[anywhere] * 2,
        out_specs=[anywhere] * 2,
        out_shape=[
            jax.ShapeDtypeStruct((ring, 2, 2, 2, rows, columns), attn_pack.dtype),
            jax.ShapeDtypeStruct(ffn_pack.shape, ffn_pack.dtype),
        ],
        scratch_shapes=[
            pltpu.SemaphoreType.DMA((2,)),
            pltpu.SemaphoreType.DMA((count,)),
            pltpu.SemaphoreType.DMA((count,)),
        ],
        compiler_params=pltpu.CompilerParams(collective_id=0, has_side_effects=True),
    )(attn_pack, ffn_pack)
    return attn_all.reshape(size * rows, columns), ffn_rows.reshape(GROUP * rows, -1)


def scatter_kernel(
    ring, bands, edges, *refs
):
    count = len(edges) - 1
    grad_refs, ffn_ref, attn_out, ffn_out = refs[:count], refs[count], refs[count + 1], refs[count + 2]
    pack, core_in, a_side, a_near, a_ring, b_near, b_side, b_ring, c_ring, c_side, c_near = refs[
        count + 3 : count + 14
    ]
    local_sem, send_sem, recv_sem = refs[count + 14 :]
    size = ring * RING
    me = lax.axis_index("tok")
    core, near, side, z = me % 2, (me // 2) % 2, (me // 4) % 2, me // RING
    core_mate, near_mate, side_mate = me + 1 - 2 * core, me + 2 - 4 * near, me + 4 - 8 * side
    far_mate = near_mate + 1 - 2 * core
    up, down = (me + RING) % size, (me + size - RING) % size

    def chunk_of(step):
        return (z - 1 - step + 2 * ring) % ring

    loads = []
    for step in range(ring):
        row = []
        for k in range(count):
            load = pltpu.make_async_copy(
                grad_refs[k].at[chunk_of(step)],
                pack.at[chunk_of(step), :, :, :, :, pl.ds(edges[k], edges[k + 1] - edges[k])],
                local_sem.at[step * count + k],
            )
            load.start()
            row.append(load)
        loads.append(row)
    own_slice = pltpu.make_async_copy(
        ffn_ref.at[2 * near + core], ffn_out.at[2 * near + core], local_sem.at[ring * count]
    )
    own_slice.start()

    barrier = pltpu.get_barrier_semaphore()
    partners = (core_mate, near_mate, side_mate, far_mate, up, down)
    for partner in partners:
        pl.semaphore_signal(
            barrier, inc=1, device_id=(partner,), device_id_type=pl.DeviceIdType.MESH
        )
    pl.semaphore_wait(barrier, len(partners))

    copies = []

    def send(src, dst, to):
        index = len(copies)
        copy = pltpu.make_async_remote_copy(
            src_ref=src,
            dst_ref=dst,
            send_sem=send_sem.at[index],
            recv_sem=recv_sem.at[index],
            device_id=(to,),
            device_id_type=pl.DeviceIdType.MESH,
        )
        copy.start()
        copies.append(copy)
        return copy

    def add(held, arrived):
        held[...] = (held[...].astype(FULL) + arrived[...].astype(FULL)).astype(LOW)

    def part(step, y, x, band):
        return pack.at[chunk_of(step), y, x, core, bands[band]]

    def own(step, band):
        return part(step, side, near, band)

    across, first, second, hops = {}, {}, {}, {}

    def begin(step):
        chunk = chunk_of(step)
        across[step].wait_recv()

        def one(k, _):
            add(pack.at[chunk, k // 2, k % 2, core], core_in.at[chunk, k // 2, k % 2])
            return 0

        lax.fori_loop(0, 4, one, 0)
        first[0, step] = send(
            pack.at[chunk, 1 - side, :, core, bands[0]], a_side.at[step], side_mate
        )
        first[1, step] = send(
            pack.at[chunk, :, 1 - near, core, bands[1]], b_near.at[step], near_mate
        )
        if step > 0:
            hops[2, step].wait_recv()
            for k in range(4):
                add(part(step, k // 2, k % 2, 2), c_ring.at[step - 1, k // 2, k % 2])
        if step < ring - 1:
            hops[2, step + 1] = send(
                pack.at[chunk, :, :, core, bands[2]], c_ring.at[step], up
            )

    def middle(step):
        first[0, step].wait_recv()
        for x in range(2):
            add(part(step, side, x, 0), a_side.at[step, x])
        second[0, step] = send(part(step, side, 1 - near, 0), a_near.at[step], near_mate)
        first[1, step].wait_recv()
        for y in range(2):
            add(part(step, y, near, 1), b_near.at[step, y])
        second[1, step] = send(part(step, 1 - side, near, 1), b_side.at[step], side_mate)

    def end(step):
        for band, arrived, passing in ((0, a_near, a_ring), (1, b_side, b_ring)):
            second[band, step].wait_recv()
            add(own(step, band), arrived.at[step])
            if step > 0:
                hops[band, step].wait_recv()
                add(own(step, band), passing.at[step - 1])
            if step < ring - 1:
                hops[band, step + 1] = send(own(step, band), passing.at[step], up)

    for step in range(ring):
        for load in loads[step]:
            load.wait()
        across[step] = send(
            pack.at[chunk_of(step), :, :, 1 - core], core_in.at[chunk_of(step)], core_mate
        )
    slices = []
    for step in range(ring + 2):
        if step < ring:
            begin(step)
        if step == 0:
            slices += [
                send(ffn_ref.at[index], ffn_out.at[2 * near + core], mate)
                for mate, index in (
                    (near_mate, 2 * (1 - near) + core),
                    (far_mate, 2 * (1 - near) + 1 - core),
                    (core_mate, 2 * near + 1 - core),
                )
            ]
        if 1 <= step <= ring:
            middle(step - 1)
        if step == ring:
            last = ring - 1
            to_side = send(pack.at[z, 1 - side, :, core, bands[2]], c_side, side_mate)
        if step >= 2:
            end(step - 2)
        if step == ring:
            to_side.wait_recv()
            for x in range(2):
                add(part(last, side, x, 2), c_side.at[x])
            to_near = send(part(last, side, 1 - near, 2), c_near, near_mate)
    to_near.wait_recv()
    add(own(last, 2), c_near)
    attn_out[...] = pack[z, side, near, core].astype(FULL)
    own_slice.wait()
    for copy in slices:
        copy.wait_recv()
    for copy in copies:
        copy.wait_send()


def scatter(grads, ffn_sum):
    size = lax.axis_size("tok")
    ring = size // RING
    rows = grads[0].shape[0] // size
    if ring > LONGEST_RING or ring < 2 or rows % 48:
        joined = jnp.concatenate(grads, axis=1).astype(FULL)
        return (
            lax.psum_scatter(joined, "tok", scatter_dimension=0, tiled=True),
            slices_from_group(ffn_sum),
        )
    third = rows // 3
    bands = [pl.ds(third * band, third) for band in range(3)]
    edges = [0]
    for grad in grads:
        edges.append(edges[-1] + grad.shape[1])
    columns = edges[-1]
    count = ring + 2 * ring + (ring - 1) + 3 + 2 * ring + 1 + 2 * (ring - 1) + 1
    anywhere = pl.BlockSpec(memory_space=pl.ANY)
    band = (third, columns)
    low = lambda *shape: pltpu.VMEM((*shape, *band), LOW)
    return pl.pallas_call(
        functools.partial(scatter_kernel, ring, bands, edges),
        in_specs=[anywhere] * (len(grads) + 1),
        out_specs=[pl.BlockSpec(memory_space=pltpu.VMEM), anywhere],
        out_shape=[
            jax.ShapeDtypeStruct((rows, columns), FULL),
            jax.ShapeDtypeStruct((GROUP, rows, ffn_sum.shape[1]), LOW),
        ],
        scratch_shapes=[
            pltpu.VMEM((ring, 2, 2, 2, rows, columns), LOW),
            pltpu.VMEM((ring, 2, 2, rows, columns), LOW),
            low(ring, 2),
            low(ring),
            low(ring - 1),
            low(ring, 2),
            low(ring),
            low(ring - 1),
            low(ring - 1, 2, 2),
            low(2),
            low(),
            pltpu.SemaphoreType.DMA((ring * len(grads) + 1,)),
            pltpu.SemaphoreType.DMA((count,)),
            pltpu.SemaphoreType.DMA((count,)),
        ],
        compiler_params=pltpu.CompilerParams(
            collective_id=1, has_side_effects=True, vmem_limit_bytes=44 * MIB
        ),
    )(
        *[grad.reshape(ring, 2, 2, 2, rows, -1) for grad in grads],
        ffn_sum.astype(LOW).reshape(GROUP, rows, -1),
    )


def after(value, *marks):
    return lax.optimization_barrier((value, *marks))[0]


def groups_of(stride):
    size = lax.axis_size("tok")
    return [[s + stride * k for k in range(size // stride)] for s in range(stride)]


def spread(block, marks):
    size = lax.axis_size("tok")
    ring = size // RING
    if ring > LONGEST_RING:
        gathered = lax.all_gather(
            block, "tok", axis=0, tiled=True, axis_index_groups=groups_of(GROUP)
        )
        return [gathered], [()] * 3
    own, crossed = [block], []
    for step in range(ring):
        crossed.append(flip(own[-1], SIDE))
        if step < ring - 1:
            arrived = around(own[-1])
            if step == 0:
                arrived, crossed[0] = lax.optimization_barrier((arrived, crossed[0], *marks))[:2]
            own.append(arrived)
    pieces = [piece for pair in zip(own, crossed) for piece in pair]
    return pieces, [(*own[step + 1 : step + 2], crossed[step]) for step in range(ring)]


class Reduction:
    def __init__(self, normed, cotangent, array):
        self.given = (normed, cotangent, array)
        self.size = lax.axis_size("tok")
        self.ring = self.size // RING
        _, _, _, self.side, self.z = place()
        self.rows = normed[0].shape[1] // (self.ring * 2)
        self.short = 2 <= self.ring <= LONGEST_RING and self.rows % 64 == 0
        self.blocks, self.crossing, self.total = {}, None, None

    def multiply(self, step, mark=None):
        if not self.short:
            return ()
        chunk = lax.rem(self.z - 1 - step + 2 * self.ring, self.ring)
        normed, cotangent, array = self.given
        array = after(array, *jax.tree.leaves(mark))
        product = outer_products(normed, cotangent, array, chunk, 2 * self.rows)
        self.blocks[step] = product.reshape(2, self.rows, -1)
        return self.blocks[step]

    def begin(self):
        if self.short:
            self.crossing = flip(pick(self.blocks[0], 1 - self.side), SIDE)

    def advance(self, step, *marks):
        if not self.short:
            return ()
        arrived = (self.crossing,) if self.total is None else (self.crossing, self.total)
        block = self.blocks[min(step + 1, self.ring - 1)]
        block, *arrived = lax.optimization_barrier((block, *arrived, *marks))[: len(arrived) + 1]
        total = pick(self.blocks[step], self.side).astype(FULL)
        for part in arrived:
            total = total + part.astype(FULL)
        if step == self.ring - 1:
            self.sum = total.astype(LOW)
            return (self.sum,)
        low, give = total.astype(LOW), pick(block, 1 - self.side)
        self.total, self.crossing = around(low), flip(give, SIDE)
        return (low, give)

    def result(self):
        if self.short:
            return self.sum
        normed, cotangent = (jnp.concatenate(pair, axis=0) for pair in self.given[:2])
        array = self.given[2]
        joined = jnp.concatenate(
            [outer_sum(normed, array[0]), outer_sum(normed, array[1]), outer_sum(cotangent, array[2])],
            axis=1,
        )
        return lax.psum_scatter(
            joined, "tok", scatter_dimension=0, tiled=True, axis_index_groups=groups_of(GROUP)
        )


def turn(values, cosine, sine):
    return values * cosine + pltpu.roll(values, HD // 2, 1) * sine


def mask_into(bias, key_segments, query_segments, block):
    keys, queries = bias.shape
    for start in range(0, queries, block):
        offset = (
            lax.broadcasted_iota(jnp.int32, (keys, block), 0)
            - lax.broadcasted_iota(jnp.int32, (keys, block), 1)
            - start
        )
        same = key_segments[...] == query_segments[:, start : start + block]
        allowed = same & (offset > 0) & (offset <= WINDOW)
        bias[:, start : start + block] = jnp.where(allowed, 0.0, -jnp.inf)


def attend_kernel(
    block, factor, q_ref, key_ref, value_t_ref, ks_ref, qs_ref, cos_ref, sin_ref,
    rot_ref, mixed_ref, log_ref, bias,
):
    @pl.when(pl.program_id(0) == 0)
    def _():
        mask_into(bias, ks_ref, qs_ref, block)

    queries = q_ref.shape[0]
    rot_ref[...] = turn(q_ref[...], cos_ref[...], sin_ref[...]).astype(LOW)
    for start in range(0, queries, block):
        rows, span = pl.ds(start, block), pl.ds(start, WINDOW + block)
        raw = by_rows(key_ref[span, :], rot_ref[rows, :])
        score = raw * factor + bias[span, rows]
        top = jnp.max(score, axis=0, keepdims=True)
        expo = jnp.exp2(score - top)
        total = jnp.sum(expo, axis=0, keepdims=True)
        mixed_t = matmul(value_t_ref[:, span], expo.astype(LOW)) / total
        mixed_ref[rows, :] = mixed_t.T.astype(LOW)
        log_ref[0, :, rows] = top + jnp.log2(total)


def attend(raw_query, key_value, key_segments, query_segments, cosine, sine, first, heads):
    queries, width = raw_query.shape[0], heads * HD
    keys = key_value.shape[0]
    block = min(256, queries)
    head = pl.BlockSpec((queries, HD), lambda h: (0, h))
    whole = lambda shape: pl.BlockSpec(shape, lambda h: (0,) * len(shape))
    return pl.pallas_call(
        functools.partial(attend_kernel, block, HD**-0.5 * LOG2E),
        grid=(heads,),
        in_specs=[
            pl.BlockSpec((queries, HD), lambda h: (0, first + h)),
            whole((keys, HD)),
            whole((HD, keys)),
            whole((keys, 1)),
            whole((1, queries)),
            whole((queries, HD)),
            whole((queries, HD)),
        ],
        out_specs=[head, head, pl.BlockSpec((1, 1, queries), lambda h: (h, 0, 0))],
        out_shape=[
            jax.ShapeDtypeStruct((queries, width), LOW),
            jax.ShapeDtypeStruct((queries, width), LOW),
            jax.ShapeDtypeStruct((heads, 1, queries), FULL),
        ],
        scratch_shapes=[pltpu.VMEM((keys, queries), FULL)],
        compiler_params=pltpu.CompilerParams(vmem_limit_bytes=40 * MIB),
        cost_estimate=LIGHT,
    )(
        raw_query,
        key_value[:, :HD],
        key_value[:, HD:].T,
        key_segments[:, None],
        query_segments[None, :],
        cosine,
        sine,
    )


def attend_back_kernel(
    block, factor, rot_ref, grad_ref, mixed_ref, log_ref, key_ref, value_ref, key_t_ref, ks_ref, qs_ref,
    cos_ref, sin_ref, query_out, key_out, value_out, bias,
):
    @pl.when(pl.program_id(0) == 0)
    def _():
        mask_into(bias, ks_ref, qs_ref, block)
        key_out[...] = jnp.zeros_like(key_out)
        value_out[...] = jnp.zeros_like(value_out)

    queries = rot_ref.shape[0]
    for start in range(0, queries, block):
        rows, span = pl.ds(start, block), pl.ds(start, WINDOW + block)
        rot, grad = rot_ref[rows, :], grad_ref[rows, :]
        product = grad.astype(FULL) * mixed_ref[rows, :].astype(FULL)
        inner = jnp.sum(product.T, axis=0, keepdims=True)
        raw = by_rows(key_ref[span, :], rot)
        prob = jnp.exp2(raw * factor + (bias[span, rows] - log_ref[0, :, rows]))
        grad_prob = by_rows(value_ref[span, :], grad)
        grad_raw = (prob * (grad_prob - inner)).astype(LOW)
        value_out[span, :] += matmul(prob.astype(LOW), grad)
        key_out[span, :] += matmul(grad_raw, rot)
        back = matmul(key_t_ref[:, span], grad_raw).T * HD**-0.5
        query_out[rows, :] = turn(back, cos_ref[rows, :], -sin_ref[rows, :]).astype(LOW)


def attend_back(rot, grad, mixed, logs, key_value, key_segments, query_segments, cosine, sine):
    queries, width = rot.shape
    keys = key_value.shape[0]
    heads = width // HD
    block = min(256, queries)
    head = pl.BlockSpec((queries, HD), lambda h: (0, h))
    whole = lambda shape: pl.BlockSpec(shape, lambda h: (0,) * len(shape))
    return pl.pallas_call(
        functools.partial(attend_back_kernel, block, HD**-0.5 * LOG2E),
        grid=(heads,),
        in_specs=[
            head,
            head,
            head,
            pl.BlockSpec((1, 1, queries), lambda h: (h, 0, 0)),
            whole((keys, HD)),
            whole((keys, HD)),
            whole((HD, keys)),
            whole((keys, 1)),
            whole((1, queries)),
            whole((queries, HD)),
            whole((queries, HD)),
        ],
        out_specs=[head, whole((keys, HD)), whole((keys, HD))],
        out_shape=[
            jax.ShapeDtypeStruct((queries, width), LOW),
            jax.ShapeDtypeStruct((keys, HD), FULL),
            jax.ShapeDtypeStruct((keys, HD), FULL),
        ],
        scratch_shapes=[pltpu.VMEM((keys, queries), FULL)],
        compiler_params=pltpu.CompilerParams(vmem_limit_bytes=40 * MIB),
        cost_estimate=LIGHT,
    )(
        rot,
        grad,
        mixed,
        logs,
        key_value[:, :HD],
        key_value[:, HD:],
        key_value[:, :HD].T,
        key_segments[:, None],
        query_segments[None, :],
        cosine,
        sine,
    )


GELU_A = 0.7978845608028654
GELU_B = 0.044715


def hidden_kernel(count, *refs):
    normed_refs, cot_refs, pieces = refs[:2], refs[2:4], refs[4 : 4 + count]
    out_ref, weights_out, weights, sems = refs[4 + count :]
    step, steps = pl.program_id(0), pl.num_programs(0)
    me = lax.axis_index("tok")
    side, z, ring = (me // SIDE) % 2, me // RING, count // 2
    rows = weights.shape[0] // count

    def load(k):
        if count == 1:
            start = 0
        else:
            start = 2 * ((z - k // 2 + ring) % ring) + (side if k % 2 == 0 else 1 - side)
        return pltpu.make_async_copy(
            pieces[k], weights.at[pl.ds(pl.multiple_of(start * rows, 16), rows)], sems.at[k]
        )

    keep = pltpu.make_async_copy(weights, weights_out, sems.at[count])

    @pl.when(step == 0)
    def _():
        for k in range(count):
            load(k).start()
        for k in range(count):
            load(k).wait()
        keep.start()

    early = step < steps // 2
    normed = jnp.where(early, normed_refs[0][...], normed_refs[1][...])
    cotangent = jnp.where(early, cot_refs[0][...], cot_refs[1][...])
    columns = out_ref.shape[2]
    gate = matmul(normed, weights[:, :columns])
    up = matmul(normed, weights[:, columns : 2 * columns])
    grad_hidden = matmul(cotangent, weights[:, 2 * columns :])
    square = gate * gate
    bent = jnp.tanh(gate * (GELU_A + GELU_A * GELU_B * square))
    half = 0.5 * (1.0 + bent)
    value = gate * half
    slope = half + 0.5 * gate * (1.0 - bent * bent) * (GELU_A + 3.0 * GELU_A * GELU_B * square)
    out_ref[0] = (grad_hidden * up * slope).astype(LOW)
    out_ref[1] = (grad_hidden * value).astype(LOW)
    out_ref[2] = (value * up).astype(LOW)

    @pl.when(step == steps - 1)
    def _():
        keep.wait()


def hidden_and_grads(normed, cotangent, pieces):
    half, width = normed[0].shape
    columns = pieces[0].shape[1] // 3
    rows = min(256, half)
    steps = half // rows
    count = len(pieces)
    blocks = [
        pl.BlockSpec((rows, width), lambda i: (jnp.minimum(i, steps - 1), 0)),
        pl.BlockSpec((rows, width), lambda i: (jnp.maximum(i - steps, 0), 0)),
    ]
    anywhere = pl.BlockSpec(memory_space=pl.ANY)
    return pl.pallas_call(
        functools.partial(hidden_kernel, count),
        grid=(2 * steps,),
        in_specs=blocks * 2 + [anywhere] * count,
        out_specs=[pl.BlockSpec((3, rows, columns), lambda i: (0, i, 0)), anywhere],
        out_shape=[
            jax.ShapeDtypeStruct((3, 2 * half, columns), LOW),
            jax.ShapeDtypeStruct((width, 3 * columns), LOW),
        ],
        scratch_shapes=[
            pltpu.VMEM((width, 3 * columns), LOW),
            pltpu.SemaphoreType.DMA((count + 1,)),
        ],
        compiler_params=pltpu.CompilerParams(vmem_limit_bytes=48 * MIB),
        cost_estimate=LIGHT,
    )(*normed, *cotangent, *pieces)


def project_sum_kernel(count, blocks, array_ref, *refs):
    weight_refs, out_ref = refs[:count], refs[count]
    away, arrived, send_sem, recv_sem = refs[count + 1 :]
    step, column = pl.program_id(0), pl.program_id(1)
    columns, rows = pl.num_programs(1), out_ref.shape[0]
    me = lax.axis_index("tok")
    mate = me + 1 - 2 * (me % 2)

    def crossing(block):
        return pltpu.make_async_remote_copy(
            src_ref=away.at[block],
            dst_ref=arrived.at[block],
            send_sem=send_sem.at[block],
            recv_sem=recv_sem.at[block],
            device_id=(mate,),
            device_id_type=pl.DeviceIdType.MESH,
        )

    @pl.when((step == 0) & (column == 0))
    def _():
        barrier = pltpu.get_barrier_semaphore()
        pl.semaphore_signal(
            barrier, inc=1, device_id=(mate,), device_id_type=pl.DeviceIdType.MESH
        )
        pl.semaphore_wait(barrier, 1)

    total = by_rows(array_ref[0], weight_refs[0][...])
    for k in range(1, count):
        total += by_rows(array_ref[k], weight_refs[k][...])
    for block in range(blocks):

        @pl.when(step == block)
        def _():
            away[block, column] = total.astype(LOW)

            @pl.when(column == columns - 1)
            def _():
                crossing(block).start()

        @pl.when(step == blocks + block)
        def _():
            @pl.when(column == 0)
            def _():
                crossing(block).wait()

            out_ref[...] = (total + arrived[block, column].astype(FULL)).astype(LOW)


def project_sum(array, pack, first, count, identity, marks=()):
    array = after(array, *jax.tree.leaves(marks))
    tokens, columns = array.shape[1:]
    width = pack.shape[0]
    rows, wide = tokens // 4, width
    blocks = tokens // rows // 2
    return pl.pallas_call(
        functools.partial(project_sum_kernel, count, blocks),
        grid=(2 * blocks, width // wide),
        in_specs=[
            pl.BlockSpec(
                (count, rows, columns), lambda i, j: (first // count, (i + blocks) % (2 * blocks), 0)
            )
        ]
        + [
            pl.BlockSpec(
                (wide, columns), lambda i, j, k=k: (j, first + k), pipeline_mode=pl.Buffered(1)
            )
            for k in range(count)
        ],
        out_specs=pl.BlockSpec(
            (rows, wide),
            lambda i, j: (jnp.maximum(i - blocks, 0), jnp.where(i >= blocks, j, 0)),
        ),
        out_shape=jax.ShapeDtypeStruct((tokens // 2, width), LOW),
        scratch_shapes=[
            pltpu.VMEM((blocks, width // wide, rows, wide), LOW),
            pltpu.VMEM((blocks, width // wide, rows, wide), LOW),
            pltpu.SemaphoreType.DMA((blocks,)),
            pltpu.SemaphoreType.DMA((blocks,)),
        ],
        compiler_params=pltpu.CompilerParams(
            collective_id=identity, has_side_effects=True, vmem_limit_bytes=44 * MIB
        ),
        cost_estimate=LIGHT,
    )(array, *([pack] * count))


def outer_kernel(chunk_ref, *refs):
    normed_refs, cot_refs, right_ref, out_ref, total = refs[:2], refs[2:4], *refs[4:]
    step, steps = pl.program_id(0), pl.num_programs(0)
    early = step < steps // 2
    normed = jnp.where(early, normed_refs[0][...], normed_refs[1][...])
    cotangent = jnp.where(early, cot_refs[0][...], cot_refs[1][...])
    columns = right_ref.shape[2]

    @pl.when(step == 0)
    def _():
        total[...] = jnp.zeros_like(total)

    for k, left in enumerate((normed, normed, cotangent)):
        total[:, k * columns : (k + 1) * columns] += outer_sum(left, right_ref[k])

    @pl.when(step == steps - 1)
    def _():
        out_ref[...] = total[...].astype(LOW)


def outer_products(normed, cotangent, array, chunk, rows):
    tokens, columns = array.shape[1:]
    deep = min(512, tokens // 2)
    steps = tokens // 2 // deep
    lefts = [
        pl.BlockSpec((deep, rows), lambda i, chunk_ref: (jnp.minimum(i, steps - 1), chunk_ref[0])),
        pl.BlockSpec((deep, rows), lambda i, chunk_ref: (jnp.maximum(i - steps, 0), chunk_ref[0])),
    ]
    return pl.pallas_call(
        outer_kernel,
        grid_spec=pltpu.PrefetchScalarGridSpec(
            num_scalar_prefetch=1,
            grid=(2 * steps,),
            in_specs=lefts * 2
            + [pl.BlockSpec((3, deep, columns), lambda i, chunk_ref: (0, i, 0))],
            out_specs=pl.BlockSpec((rows, 3 * columns), lambda i, chunk_ref: (0, 0)),
            scratch_shapes=[pltpu.VMEM((rows, 3 * columns), FULL)],
        ),
        out_shape=jax.ShapeDtypeStruct((rows, 3 * columns), LOW),
        compiler_params=pltpu.CompilerParams(vmem_limit_bytes=40 * MIB),
        cost_estimate=LIGHT,
    )(chunk[None].astype(jnp.int32), *normed, *cotangent, array)


def join_kernel(count, epsilon, *refs):
    inputs_ref, gain_ref, weight_ref = refs[:3]
    parts, (middle_ref, normed_ref, inverse_ref) = refs[3 : 3 + count], refs[3 + count :]
    total, start = inputs_ref[...].astype(FULL), 0
    for part in parts:
        columns = part.shape[1]
        total += by_rows(part[...], weight_ref[:, start : start + columns])
        start += columns
    inverse = lax.rsqrt(jnp.mean(total * total, axis=1, keepdims=True) + epsilon)
    middle_ref[...] = total
    inverse_ref[...] = jnp.broadcast_to(inverse, inverse_ref.shape)
    normed_ref[...] = (total * inverse * gain_ref[...]).astype(LOW)


def join(tokens, gain, weight, parts):
    count, width = tokens.shape
    rows = min(256, count)
    block = lambda columns: pl.BlockSpec((rows, columns), lambda i: (i, 0))
    return pl.pallas_call(
        functools.partial(join_kernel, len(parts), EPSILON),
        grid=(count // rows,),
        in_specs=[
            block(width),
            pl.BlockSpec((1, width), lambda i: (0, 0)),
            pl.BlockSpec((width, width), lambda i: (0, 0), pipeline_mode=pl.Buffered(1)),
        ]
        + [block(part.shape[1]) for part in parts],
        out_specs=[block(width), block(width), block(HD)],
        out_shape=[
            jax.ShapeDtypeStruct((count, width), FULL),
            jax.ShapeDtypeStruct((count, width), LOW),
            jax.ShapeDtypeStruct((count, HD), FULL),
        ],
        compiler_params=pltpu.CompilerParams(vmem_limit_bytes=40 * MIB),
        cost_estimate=LIGHT,
    )(tokens, gain[None], weight, *parts)


def branch_kernel(
    group_ref, near_ref, cot_ref, middle_ref, inverse_ref, gain_ref, weight_ref,
    grad_ref, branch_ref, mixed_ref, scaled_ref,
):
    grad = group_ref[...].astype(FULL) + near_ref[...].astype(FULL)
    middle, inverse = middle_ref[...], inverse_ref[:, :1]
    normal = middle * inverse
    scaled_ref[...] = (grad * normal).astype(LOW)
    scaled = grad * gain_ref[...]
    total = (
        cot_ref[...].astype(FULL)
        + inverse * scaled
        - normal * (inverse * jnp.mean(scaled * normal, axis=1, keepdims=True))
    )
    grad_ref[...] = total
    branch = total.astype(LOW)
    branch_ref[...] = branch
    mixed_ref[...] = matmul(branch, weight_ref[...]).astype(LOW)


def branch_back(group, near, cotangent, middle, inverse, gain, weight):
    count, width = middle.shape
    rows = min(256, count)
    block = lambda columns: pl.BlockSpec((rows, columns), lambda i: (i, 0))
    return pl.pallas_call(
        branch_kernel,
        grid=(count // rows,),
        in_specs=[
            block(width),
            block(width),
            block(width),
            block(width),
            block(HD),
            pl.BlockSpec((1, width), lambda i: (0, 0)),
            pl.BlockSpec((width, width), lambda i: (0, 0), pipeline_mode=pl.Buffered(1)),
        ],
        out_specs=[block(width)] * 4,
        out_shape=[
            jax.ShapeDtypeStruct((count, width), FULL),
            jax.ShapeDtypeStruct((count, width), LOW),
            jax.ShapeDtypeStruct((count, width), LOW),
            jax.ShapeDtypeStruct((count, width), LOW),
        ],
        compiler_params=pltpu.CompilerParams(vmem_limit_bytes=48 * MIB),
        cost_estimate=LIGHT,
    )(group, near, cotangent, middle, inverse, gain[None], weight)


def on_device(
    tokens, cotangent, attn_gain, ffn_gain, w_query, w_key, w_value, w_out, w_gate, w_up, w_down,
    segments, positions,
):
    token_count, width = tokens.shape
    own_rows, hidden_width = w_gate.shape
    slice_width = hidden_width // GROUP
    heads_width = w_query.shape[1]
    tail_rows = min(token_count, WINDOW)
    hop_count = WINDOW // tail_rows
    device = lax.axis_index("tok")
    inputs = tokens.astype(FULL)

    frequency = 10000.0 ** (-jnp.arange(HD // 2, dtype=FULL) * 2.0 / HD)
    angles = positions.astype(FULL)[:, None] * frequency[None, :]
    cosine = jnp.concatenate([jnp.cos(angles)] * 2, axis=1)
    sine_half = jnp.sin(angles)
    sine = jnp.concatenate([-sine_half, sine_half], axis=1)
    padded_segments = jnp.concatenate([jnp.full((WINDOW,), -1, jnp.int32), segments])
    key_segments = lax.dynamic_slice_in_dim(
        padded_segments, device * token_count, WINDOW + token_count
    )
    query_segments = lax.dynamic_slice_in_dim(segments, device * token_count, token_count)

    attn_pack = jnp.concatenate(
        [
            w_query,
            w_key,
            w_value,
            jnp.pad(
                jnp.stack([attn_gain, ffn_gain], axis=1), ((0, 0), (0, HD - 2))
            ),
        ],
        axis=1,
    )
    edge = heads_width + 2 * HD
    def sliced(weight):
        return weight.reshape(own_rows, GROUP, slice_width).transpose(1, 0, 2)

    ffn_pack = jnp.concatenate([sliced(w_gate), sliced(w_up), sliced(w_down)], axis=2)
    attn_all, ffn_rows = gather(attn_pack, ffn_pack)
    out_w = lax.all_gather(w_out, "tok", axis=0, tiled=True)
    query_w, kv_w = attn_all[:, :heads_width], attn_all[:, heads_width:edge]
    gains = attn_all[:, edge : edge + 2].astype(FULL)
    gain_one, gain_two = gains[:, 0], gains[:, 1]

    inverse_one = lax.rsqrt(jnp.mean(inputs * inputs, axis=-1, keepdims=True) + EPSILON)
    normed = (inputs * inverse_one * gain_one).astype(LOW)
    kv = matmul(normed, kv_w)

    def turned(values, sine_signed):
        half = HD // 2
        rolled = jnp.concatenate([values[:, half:], values[:, :half]], axis=1)
        return values * cosine + rolled * sine_signed

    key_value = jnp.concatenate([turned(kv[:, :HD], sine), kv[:, HD:]], axis=1).astype(LOW)
    received = [passed_along(key_value, hop) for hop in range(hop_count, 0, -1)]
    all_keys = jnp.concatenate(received + [key_value], axis=0)
    raw_query = matmul(normed, query_w)
    heads = heads_width // HD
    given = (all_keys, key_segments, query_segments, cosine, sine)
    early = attend(raw_query, *given, 0, heads // 2)
    pieces, steps = spread(ffn_rows, (early[1],))
    cot_group = rows_to_group(after(cotangent, attn_all), steps[1])
    late = attend(
        after(raw_query, early[1]), *given, heads // 2, heads - heads // 2
    )
    rot, mixed = (jnp.concatenate([early[k], late[k]], axis=1) for k in range(2))
    logs = jnp.concatenate([early[2], late[2]], axis=0)
    middle, normed_two, inverse_two = join(tokens, gain_two, out_w, (early[1], late[1]))

    normed_group = rows_to_group(after(normed_two, *steps[1]), steps[2])
    hidden_pack, ffn_w = hidden_and_grads(normed_group, cot_group, pieces)
    reduction = Reduction(normed_group, cot_group, hidden_pack)
    pairs_done = reduction.multiply(0)
    reduction.begin()
    pairs_done = reduction.multiply(1, pairs_done)
    group_sum = project_sum(hidden_pack, ffn_w, 0, 2, 2, pairs_done)
    near_sent = flip(group_sum[token_count:], NEAR)
    marks = reduction.advance(0, group_sum)
    pairs_done = reduction.multiply(2, marks)
    pairs_done = reduction.multiply(3, pairs_done)
    marks = reduction.advance(1, pairs_done)
    output_sum = project_sum(hidden_pack, ffn_w, 2, 1, 3, marks)
    output_near = flip(after(output_sum, near_sent)[token_count:], NEAR)

    grad_middle, branch, grad_mixed, gain_two_parts = branch_back(
        group_sum[:token_count], after(near_sent, output_sum), cotangent, middle, inverse_two, gain_two, out_w
    )
    grad_out_w = outer_sum(branch, mixed).astype(LOW)
    out_sum = lax.psum_scatter(grad_out_w, "tok", scatter_dimension=0, tiled=True).astype(FULL)
    marks = reduction.advance(2, grad_mixed)
    query_low, key_grads, value_grads = attend_back(
        rot, after(grad_mixed, *marks), mixed, logs, all_keys, key_segments, query_segments, cosine, sine
    )
    output = (
        middle + output_sum[:token_count].astype(FULL) + after(output_near, query_low).astype(FULL)
    ).astype(LOW)
    grads = jnp.concatenate([key_grads * HD**-0.5, value_grads], axis=1)
    shares = grads[WINDOW:]
    for hop in range(1, hop_count + 1):
        first_row = (hop_count - hop) * tail_rows
        returned = passed_along(grads[first_row : first_row + tail_rows].astype(LOW), -hop)
        shares = shares.at[token_count - tail_rows :].add(returned.astype(FULL))
    kv_low = jnp.concatenate([turned(shares[:, :HD], -sine), shares[:, HD:]], axis=1).astype(LOW)
    grad_query_w = outer_sum(normed, query_low).astype(LOW)
    grad_kv_w = outer_sum(normed, kv_low).astype(LOW)
    grad_normed = by_rows(query_low, query_w) + by_rows(kv_low, kv_w)
    scaled_one = grad_normed * gain_one
    grad_inputs = inverse_one * scaled_one - inputs * inverse_one**3 * jnp.mean(
        scaled_one * inputs, axis=-1, keepdims=True
    )
    grad_tokens = (grad_middle + grad_inputs).astype(LOW)
    lane = lax.broadcasted_iota(jnp.int32, (token_count, HD), 1)
    grad_gains = (
        outer_sum((grad_normed * inputs * inverse_one).astype(LOW), (lane == 0).astype(LOW))
        + outer_sum(gain_two_parts, (lane == 1).astype(LOW))
    ).astype(LOW)
    reduction.advance(3, grad_query_w)
    attn_sum, ffn_parts = scatter(
        [grad_query_w, grad_kv_w, grad_gains], reduction.result()
    )

    def joined(parts):
        return parts.transpose(1, 0, 2).reshape(own_rows, hidden_width).astype(FULL)

    return (
        output,
        grad_tokens,
        attn_sum[:, edge],
        attn_sum[:, edge + 1],
        attn_sum[:, :heads_width],
        attn_sum[:, heads_width : heads_width + HD],
        attn_sum[:, heads_width + HD : edge],
        out_sum,
        joined(ffn_parts[:, :, :slice_width]),
        joined(ffn_parts[:, :, slice_width : 2 * slice_width]),
        joined(ffn_parts[:, :, 2 * slice_width :]),
    )


def solution(mesh):
    rows, flat = P("tok", None), P("tok")
    return jax.shard_map(
        on_device,
        mesh=mesh,
        in_specs=(rows, rows, flat, flat, rows, rows, rows, rows, rows, rows, rows, P(), flat),
        out_specs=(rows, rows, flat, flat, rows, rows, rows, rows, rows, rows, rows),
        check_vma=False,
    )
```

```python
import functools

import jax
import jax.numpy as jnp
from jax import lax
from jax.experimental import pallas as pl
from jax.experimental.pallas import tpu as pltpu
from jax.sharding import PartitionSpec as P

HQ = 12
HD = 128
WINDOW = 1024
EPSILON = 1e-06

CORE, NEAR, SIDE, GROUP, RING = 1, 2, 4, 4, 8
LONGEST_RING = 8
LOG2E = 1.4426950408889634
LOW = jnp.bfloat16
FULL = jnp.float32
MIB = 1024 * 1024
LIGHT = pl.CostEstimate(flops=1024, bytes_accessed=1024, transcendentals=0)


def flip(array, bit):
    size = lax.axis_size("tok")
    return lax.ppermute(array, "tok", [(i, i ^ bit) for i in range(size)])


def around(array):
    size = lax.axis_size("tok")
    return lax.ppermute(array, "tok", [(i, (i + RING) % size) for i in range(size)])


def passed_along(array, by):
    size = lax.axis_size("tok")
    pairs = [(i, i + by) for i in range(size) if 0 <= i + by < size]
    return lax.ppermute(array, "tok", pairs)


def rms_norm(values, scales):
    return values * lax.rsqrt(jnp.mean(values * values, axis=-1, keepdims=True) + EPSILON) * scales


def outer_sum(left_side, right_side):
    return lax.dot_general(
        left_side, right_side, (((0,), (0,)), ((), ())), preferred_element_type=FULL
    )


def by_rows(left_side, right_side):
    return lax.dot_general(
        left_side, right_side, (((1,), (1,)), ((), ())), preferred_element_type=FULL
    )


def matmul(left_side, right_side):
    return jnp.dot(left_side, right_side, preferred_element_type=FULL)


def pick(array, index):
    return lax.dynamic_index_in_dim(array, index, 0, keepdims=False)


def place():
    device = lax.axis_index("tok")
    return device, device % 2, (device // 2) % 2, (device // 4) % 2, device // RING


def rows_to_group(array, marks=()):
    two = jnp.concatenate([array, after(flip(array, NEAR), *marks)], axis=0)
    return two, flip(two, CORE)


def slices_to_group(parts):
    _, core, near, _, _ = place()
    rows, columns = parts.shape[1:]
    mine = lax.dynamic_slice_in_dim(parts, 2 * near, 2, 0)
    theirs = flip(lax.dynamic_slice_in_dim(parts, 2 * (1 - near), 2, 0), NEAR)
    here = jnp.stack([pick(mine, core), pick(theirs, core)])
    away = flip(jnp.stack([pick(mine, 1 - core), pick(theirs, 1 - core)]), CORE)
    by_core = jnp.where(core == 0, jnp.stack([here, away], 1), jnp.stack([away, here], 1))
    by_near = jnp.where(near == 0, by_core, by_core[::-1])
    return by_near.reshape(4 * rows, columns)


def slices_from_group(block):
    _, core, near, _, _ = place()
    rows, columns = block.shape[0] // 4, block.shape[1]
    parts = block.astype(LOW).reshape(2, 2, rows, columns)
    mine, theirs = pick(parts, near), flip(pick(parts, 1 - near), NEAR)
    here = jnp.stack([pick(mine, core), pick(theirs, core)])
    away = flip(jnp.stack([pick(mine, 1 - core), pick(theirs, 1 - core)]), CORE)
    by_core = jnp.where(core == 0, jnp.stack([here, away], 1), jnp.stack([away, here], 1))
    by_near = jnp.where(near == 0, by_core, by_core[::-1])
    return by_near.reshape(4, rows, columns)


def gather_kernel(
    ring, bands, attn_ref, ffn_ref, attn_out, ffn_out, local_sem, send_sem, recv_sem
):
    size = ring * RING
    me = lax.axis_index("tok")
    core, near, side, z = me % 2, (me // 2) % 2, (me // 4) % 2, me // RING
    core_mate, near_mate, side_mate = me + 1 - 2 * core, me + 2 - 4 * near, me + 4 - 8 * side
    far_mate = near_mate + 1 - 2 * core
    up, down = (me + RING) % size, (me + size - RING) % size

    barrier = pltpu.get_barrier_semaphore()
    partners = (core_mate, near_mate, side_mate, far_mate, up, down)
    for partner in partners:
        pl.semaphore_signal(
            barrier, inc=1, device_id=(partner,), device_id_type=pl.DeviceIdType.MESH
        )
    pl.semaphore_wait(barrier, len(partners))

    own = pltpu.make_async_copy(attn_ref, attn_out.at[z, side, near, core], local_sem.at[0])
    own.start()
    own_slice = pltpu.make_async_copy(
        ffn_ref.at[2 * near + core], ffn_out.at[2 * near + core], local_sem.at[1]
    )
    own_slice.start()

    copies = []

    def send(src, dst, to):
        index = len(copies)
        copy = pltpu.make_async_remote_copy(
            src_ref=src,
            dst_ref=dst,
            send_sem=send_sem.at[index],
            recv_sem=recv_sem.at[index],
            device_id=(to,),
            device_id_type=pl.DeviceIdType.MESH,
        )
        copy.start()
        copies.append(copy)
        return copy

    def forward(ref, to):
        return send(ref, ref, to)

    def chunk_of(step):
        return (z - step + ring) % ring

    def piece(step, band):
        return attn_out.at[chunk_of(step), side, near, core, bands[band]]

    hops, first, second, last = {}, {}, {}, {}
    over = []

    def finish(step):
        first[0, step].wait_recv()
        second[0, step] = forward(attn_out.at[chunk_of(step), side, :, core, bands[0]], side_mate)
        first[1, step].wait_recv()
        second[1, step] = forward(attn_out.at[chunk_of(step), :, near, core, bands[1]], near_mate)

    def hand_over(step):
        second[0, step].wait_recv()
        second[1, step].wait_recv()
        over.append(forward(attn_out.at[chunk_of(step), :, :, core], core_mate))

    for step in range(ring):
        for band in (0, 1):
            if step > 0:
                hops[band, step].wait_recv()
            source = attn_ref.at[bands[band]] if step == 0 else piece(step, band)
            if step < ring - 1:
                hops[band, step + 1] = send(source, piece(step, band), up)
            mate = near_mate if band == 0 else side_mate
            first[band, step] = send(source, piece(step, band), mate)
        if step == 0:
            begun = send(attn_ref.at[bands[2]], piece(0, 2), near_mate)
            slices = [
                send(ffn_ref.at[index], ffn_out.at[2 * near + core], mate)
                for mate, index in (
                    (near_mate, 2 * (1 - near) + core),
                    (far_mate, 2 * (1 - near) + 1 - core),
                    (core_mate, 2 * near + 1 - core),
                )
            ]
            own.wait()
            begun.wait_recv()
            last[0] = forward(attn_out.at[z, side, :, core, bands[2]], side_mate)
        else:
            last[step - 1].wait_recv()
            last[step] = forward(attn_out.at[chunk_of(step - 1), :, :, core, bands[2]], up)
            finish(step - 1)
        if step >= 2:
            hand_over(step - 2)
    finish(ring - 1)
    hand_over(ring - 2)
    last[ring - 1].wait_recv()
    hand_over(ring - 1)
    own_slice.wait()
    for copy in slices + over:
        copy.wait_recv()
    for copy in copies:
        copy.wait_send()


def gather(attn_pack, ffn_pack):
    size = lax.axis_size("tok")
    ring = size // RING
    rows, columns = attn_pack.shape
    if ring > LONGEST_RING or ring < 2 or rows % 48:
        return lax.all_gather(attn_pack, "tok", axis=0, tiled=True), slices_to_group(ffn_pack)
    third = rows // 3
    bands = [pl.ds(third * band, third) for band in range(3)]
    count = 3 + 2 * (ring - 1) + 2 * ring + 2 * ring + 1 + ring + ring
    anywhere = pl.BlockSpec(memory_space=pl.ANY)
    attn_all, ffn_rows = pl.pallas_call(
        functools.partial(gather_kernel, ring, bands),
        in_specs=[anywhere] * 2,
        out_specs=[anywhere] * 2,
        out_shape=[
            jax.ShapeDtypeStruct((ring, 2, 2, 2, rows, columns), attn_pack.dtype),
            jax.ShapeDtypeStruct(ffn_pack.shape, ffn_pack.dtype),
        ],
        scratch_shapes=[
            pltpu.SemaphoreType.DMA((2,)),
            pltpu.SemaphoreType.DMA((count,)),
            pltpu.SemaphoreType.DMA((count,)),
        ],
        compiler_params=pltpu.CompilerParams(collective_id=0, has_side_effects=True),
    )(attn_pack, ffn_pack)
    return attn_all.reshape(size * rows, columns), ffn_rows.reshape(GROUP * rows, -1)


def scatter_kernel(
    ring, bands, edges, *refs
):
    count = len(edges) - 1
    grad_refs, ffn_ref, attn_out, ffn_out = refs[:count], refs[count], refs[count + 1], refs[count + 2]
    pack, core_in, a_side, a_near, a_ring, b_near, b_side, b_ring, c_ring, c_side, c_near = refs[
        count + 3 : count + 14
    ]
    local_sem, send_sem, recv_sem = refs[count + 14 :]
    size = ring * RING
    me = lax.axis_index("tok")
    core, near, side, z = me % 2, (me // 2) % 2, (me // 4) % 2, me // RING
    core_mate, near_mate, side_mate = me + 1 - 2 * core, me + 2 - 4 * near, me + 4 - 8 * side
    far_mate = near_mate + 1 - 2 * core
    up, down = (me + RING) % size, (me + size - RING) % size

    def chunk_of(step):
        return (z - 1 - step + 2 * ring) % ring

    loads = []
    for step in range(ring):
        row = []
        for k in range(count):
            load = pltpu.make_async_copy(
                grad_refs[k].at[chunk_of(step)],
                pack.at[chunk_of(step), :, :, :, :, pl.ds(edges[k], edges[k + 1] - edges[k])],
                local_sem.at[step * count + k],
            )
            load.start()
            row.append(load)
        loads.append(row)
    own_slice = pltpu.make_async_copy(
        ffn_ref.at[2 * near + core], ffn_out.at[2 * near + core], local_sem.at[ring * count]
    )
    own_slice.start()

    barrier = pltpu.get_barrier_semaphore()
    partners = (core_mate, near_mate, side_mate, far_mate, up, down)
    for partner in partners:
        pl.semaphore_signal(
            barrier, inc=1, device_id=(partner,), device_id_type=pl.DeviceIdType.MESH
        )
    pl.semaphore_wait(barrier, len(partners))

    copies = []

    def send(src, dst, to):
        index = len(copies)
        copy = pltpu.make_async_remote_copy(
            src_ref=src,
            dst_ref=dst,
            send_sem=send_sem.at[index],
            recv_sem=recv_sem.at[index],
            device_id=(to,),
            device_id_type=pl.DeviceIdType.MESH,
        )
        copy.start()
        copies.append(copy)
        return copy

    def add(held, arrived):
        held[...] = (held[...].astype(FULL) + arrived[...].astype(FULL)).astype(LOW)

    def part(step, y, x, band):
        return pack.at[chunk_of(step), y, x, core, bands[band]]

    def own(step, band):
        return part(step, side, near, band)

    across, first, second, hops = {}, {}, {}, {}

    def begin(step):
        chunk = chunk_of(step)
        across[step].wait_recv()

        def one(k, _):
            add(pack.at[chunk, k // 2, k % 2, core], core_in.at[chunk, k // 2, k % 2])
            return 0

        lax.fori_loop(0, 4, one, 0)
        first[0, step] = send(
            pack.at[chunk, 1 - side, :, core, bands[0]], a_side.at[step], side_mate
        )
        first[1, step] = send(
            pack.at[chunk, :, 1 - near, core, bands[1]], b_near.at[step], near_mate
        )
        if step > 0:
            hops[2, step].wait_recv()
            for k in range(4):
                add(part(step, k // 2, k % 2, 2), c_ring.at[step - 1, k // 2, k % 2])
        if step < ring - 1:
            hops[2, step + 1] = send(
                pack.at[chunk, :, :, core, bands[2]], c_ring.at[step], up
            )

    def middle(step):
        first[0, step].wait_recv()
        for x in range(2):
            add(part(step, side, x, 0), a_side.at[step, x])
        second[0, step] = send(part(step, side, 1 - near, 0), a_near.at[step], near_mate)
        first[1, step].wait_recv()
        for y in range(2):
            add(part(step, y, near, 1), b_near.at[step, y])
        second[1, step] = send(part(step, 1 - side, near, 1), b_side.at[step], side_mate)

    def end(step):
        for band, arrived, passing in ((0, a_near, a_ring), (1, b_side, b_ring)):
            second[band, step].wait_recv()
            add(own(step, band), arrived.at[step])
            if step > 0:
                hops[band, step].wait_recv()
                add(own(step, band), passing.at[step - 1])
            if step < ring - 1:
                hops[band, step + 1] = send(own(step, band), passing.at[step], up)

    for step in range(ring):
        for load in loads[step]:
            load.wait()
        across[step] = send(
            pack.at[chunk_of(step), :, :, 1 - core], core_in.at[chunk_of(step)], core_mate
        )
    slices = []
    for step in range(ring + 2):
        if step < ring:
            begin(step)
        if step == 0:
            slices += [
                send(ffn_ref.at[index], ffn_out.at[2 * near + core], mate)
                for mate, index in (
                    (near_mate, 2 * (1 - near) + core),
                    (far_mate, 2 * (1 - near) + 1 - core),
                    (core_mate, 2 * near + 1 - core),
                )
            ]
        if 1 <= step <= ring:
            middle(step - 1)
        if step == ring:
            last = ring - 1
            to_side = send(pack.at[z, 1 - side, :, core, bands[2]], c_side, side_mate)
        if step >= 2:
            end(step - 2)
        if step == ring:
            to_side.wait_recv()
            for x in range(2):
                add(part(last, side, x, 2), c_side.at[x])
            to_near = send(part(last, side, 1 - near, 2), c_near, near_mate)
    to_near.wait_recv()
    add(own(last, 2), c_near)
    attn_out[...] = pack[z, side, near, core].astype(FULL)
    own_slice.wait()
    for copy in slices:
        copy.wait_recv()
    for copy in copies:
        copy.wait_send()


def scatter(grads, ffn_sum):
    size = lax.axis_size("tok")
    ring = size // RING
    rows = grads[0].shape[0] // size
    if ring > LONGEST_RING or ring < 2 or rows % 48:
        joined = jnp.concatenate(grads, axis=1).astype(FULL)
        return (
            lax.psum_scatter(joined, "tok", scatter_dimension=0, tiled=True),
            slices_from_group(ffn_sum),
        )
    third = rows // 3
    bands = [pl.ds(third * band, third) for band in range(3)]
    edges = [0]
    for grad in grads:
        edges.append(edges[-1] + grad.shape[1])
    columns = edges[-1]
    count = ring + 2 * ring + (ring - 1) + 3 + 2 * ring + 1 + 2 * (ring - 1) + 1
    anywhere = pl.BlockSpec(memory_space=pl.ANY)
    band = (third, columns)
    low = lambda *shape: pltpu.VMEM((*shape, *band), LOW)
    return pl.pallas_call(
        functools.partial(scatter_kernel, ring, bands, edges),
        in_specs=[anywhere] * (len(grads) + 1),
        out_specs=[pl.BlockSpec(memory_space=pltpu.VMEM), anywhere],
        out_shape=[
            jax.ShapeDtypeStruct((rows, columns), FULL),
            jax.ShapeDtypeStruct((GROUP, rows, ffn_sum.shape[1]), LOW),
        ],
        scratch_shapes=[
            pltpu.VMEM((ring, 2, 2, 2, rows, columns), LOW),
            pltpu.VMEM((ring, 2, 2, rows, columns), LOW),
            low(ring, 2),
            low(ring),
            low(ring - 1),
            low(ring, 2),
            low(ring),
            low(ring - 1),
            low(ring - 1, 2, 2),
            low(2),
            low(),
            pltpu.SemaphoreType.DMA((ring * len(grads) + 1,)),
            pltpu.SemaphoreType.DMA((count,)),
            pltpu.SemaphoreType.DMA((count,)),
        ],
        compiler_params=pltpu.CompilerParams(
            collective_id=1, has_side_effects=True, vmem_limit_bytes=44 * MIB
        ),
    )(
        *[grad.reshape(ring, 2, 2, 2, rows, -1) for grad in grads],
        ffn_sum.astype(LOW).reshape(GROUP, rows, -1),
    )


def after(value, *marks):
    return lax.optimization_barrier((value, *marks))[0]


def groups_of(stride):
    size = lax.axis_size("tok")
    return [[s + stride * k for k in range(size // stride)] for s in range(stride)]


def spread(block, marks):
    size = lax.axis_size("tok")
    ring = size // RING
    if ring > LONGEST_RING:
        gathered = lax.all_gather(
            block, "tok", axis=0, tiled=True, axis_index_groups=groups_of(GROUP)
        )
        return [gathered], [()] * 3
    own, crossed = [block], []
    for step in range(ring):
        crossed.append(flip(own[-1], SIDE))
        if step < ring - 1:
            arrived = around(own[-1])
            if step == 0:
                arrived, crossed[0] = lax.optimization_barrier((arrived, crossed[0], *marks))[:2]
            own.append(arrived)
    pieces = [piece for pair in zip(own, crossed) for piece in pair]
    return pieces, [(*own[step + 1 : step + 2], crossed[step]) for step in range(ring)]


class Reduction:
    def __init__(self, normed, cotangent, array):
        self.given = (normed, cotangent, array)
        self.size = lax.axis_size("tok")
        self.ring = self.size // RING
        _, _, _, self.side, self.z = place()
        self.rows = normed[0].shape[1] // (self.ring * 2)
        self.short = 2 <= self.ring <= LONGEST_RING and self.rows % 64 == 0
        self.blocks, self.crossing, self.total = {}, None, None

    def multiply(self, step, mark=None):
        if not self.short:
            return ()
        chunk = lax.rem(self.z - 1 - step + 2 * self.ring, self.ring)
        normed, cotangent, array = self.given
        array = after(array, *jax.tree.leaves(mark))
        product = outer_products(normed, cotangent, array, chunk, 2 * self.rows)
        self.blocks[step] = product.reshape(2, self.rows, -1)
        return self.blocks[step]

    def begin(self):
        if self.short:
            self.crossing = flip(pick(self.blocks[0], 1 - self.side), SIDE)

    def advance(self, step, *marks):
        if not self.short:
            return ()
        arrived = (self.crossing,) if self.total is None else (self.crossing, self.total)
        block = self.blocks[min(step + 1, self.ring - 1)]
        block, *arrived = lax.optimization_barrier((block, *arrived, *marks))[: len(arrived) + 1]
        total = pick(self.blocks[step], self.side).astype(FULL)
        for part in arrived:
            total = total + part.astype(FULL)
        if step == self.ring - 1:
            self.sum = total.astype(LOW)
            return (self.sum,)
        low, give = total.astype(LOW), pick(block, 1 - self.side)
        self.total, self.crossing = around(low), flip(give, SIDE)
        return (low, give)

    def result(self):
        if self.short:
            return self.sum
        normed, cotangent = (jnp.concatenate(pair, axis=0) for pair in self.given[:2])
        array = self.given[2]
        joined = jnp.concatenate(
            [outer_sum(normed, array[0]), outer_sum(normed, array[1]), outer_sum(cotangent, array[2])],
            axis=1,
        )
        return lax.psum_scatter(
            joined, "tok", scatter_dimension=0, tiled=True, axis_index_groups=groups_of(GROUP)
        )


def turn(values, cosine, sine):
    return values * cosine + pltpu.roll(values, HD // 2, 1) * sine


def mask_into(bias, key_segments, query_segments, block):
    keys, queries = bias.shape
    for start in range(0, queries, block):
        offset = (
            lax.broadcasted_iota(jnp.int32, (keys, block), 0)
            - lax.broadcasted_iota(jnp.int32, (keys, block), 1)
            - start
        )
        same = key_segments[...] == query_segments[:, start : start + block]
        allowed = same & (offset > 0) & (offset <= WINDOW)
        bias[:, start : start + block] = jnp.where(allowed, 0.0, -jnp.inf)


def attend_kernel(
    block, factor, q_ref, key_ref, value_t_ref, ks_ref, qs_ref, cos_ref, sin_ref,
    rot_ref, mixed_ref, log_ref, bias,
):
    @pl.when(pl.program_id(0) == 0)
    def _():
        mask_into(bias, ks_ref, qs_ref, block)

    queries = q_ref.shape[0]
    rot_ref[...] = turn(q_ref[...], cos_ref[...], sin_ref[...]).astype(LOW)
    for start in range(0, queries, block):
        rows, span = pl.ds(start, block), pl.ds(start, WINDOW + block)
        raw = by_rows(key_ref[span, :], rot_ref[rows, :])
        score = raw * factor + bias[span, rows]
        top = jnp.max(score, axis=0, keepdims=True)
        expo = jnp.exp2(score - top)
        total = jnp.sum(expo, axis=0, keepdims=True)
        mixed_t = matmul(value_t_ref[:, span], expo.astype(LOW)) / total
        mixed_ref[rows, :] = mixed_t.T.astype(LOW)
        log_ref[0, :, rows] = top + jnp.log2(total)


def attend(raw_query, key_value, key_segments, query_segments, cosine, sine, first, heads):
    queries, width = raw_query.shape[0], heads * HD
    keys = key_value.shape[0]
    block = min(256, queries)
    head = pl.BlockSpec((queries, HD), lambda h: (0, h))
    whole = lambda shape: pl.BlockSpec(shape, lambda h: (0,) * len(shape))
    return pl.pallas_call(
        functools.partial(attend_kernel, block, HD**-0.5 * LOG2E),
        grid=(heads,),
        in_specs=[
            pl.BlockSpec((queries, HD), lambda h: (0, first + h)),
            whole((keys, HD)),
            whole((HD, keys)),
            whole((keys, 1)),
            whole((1, queries)),
            whole((queries, HD)),
            whole((queries, HD)),
        ],
        out_specs=[head, head, pl.BlockSpec((1, 1, queries), lambda h: (h, 0, 0))],
        out_shape=[
            jax.ShapeDtypeStruct((queries, width), LOW),
            jax.ShapeDtypeStruct((queries, width), LOW),
            jax.ShapeDtypeStruct((heads, 1, queries), FULL),
        ],
        scratch_shapes=[pltpu.VMEM((keys, queries), FULL)],
        compiler_params=pltpu.CompilerParams(vmem_limit_bytes=40 * MIB),
        cost_estimate=LIGHT,
    )(
        raw_query,
        key_value[:, :HD],
        key_value[:, HD:].T,
        key_segments[:, None],
        query_segments[None, :],
        cosine,
        sine,
    )


def attend_back_kernel(
    block, factor, rot_ref, grad_ref, mixed_ref, log_ref, key_ref, value_ref, key_t_ref, ks_ref, qs_ref,
    cos_ref, sin_ref, query_out, key_out, value_out, bias,
):
    @pl.when(pl.program_id(0) == 0)
    def _():
        mask_into(bias, ks_ref, qs_ref, block)
        key_out[...] = jnp.zeros_like(key_out)
        value_out[...] = jnp.zeros_like(value_out)

    queries = rot_ref.shape[0]
    for start in range(0, queries, block):
        rows, span = pl.ds(start, block), pl.ds(start, WINDOW + block)
        rot, grad = rot_ref[rows, :], grad_ref[rows, :]
        product = grad.astype(FULL) * mixed_ref[rows, :].astype(FULL)
        inner = jnp.sum(product.T, axis=0, keepdims=True)
        raw = by_rows(key_ref[span, :], rot)
        prob = jnp.exp2(raw * factor + (bias[span, rows] - log_ref[0, :, rows]))
        grad_prob = by_rows(value_ref[span, :], grad)
        grad_raw = (prob * (grad_prob - inner)).astype(LOW)
        value_out[span, :] += matmul(prob.astype(LOW), grad)
        key_out[span, :] += matmul(grad_raw, rot)
        back = matmul(key_t_ref[:, span], grad_raw).T * HD**-0.5
        query_out[rows, :] = turn(back, cos_ref[rows, :], -sin_ref[rows, :]).astype(LOW)


def attend_back(rot, grad, mixed, logs, key_value, key_segments, query_segments, cosine, sine):
    queries, width = rot.shape
    keys = key_value.shape[0]
    heads = width // HD
    block = min(256, queries)
    head = pl.BlockSpec((queries, HD), lambda h: (0, h))
    whole = lambda shape: pl.BlockSpec(shape, lambda h: (0,) * len(shape))
    return pl.pallas_call(
        functools.partial(attend_back_kernel, block, HD**-0.5 * LOG2E),
        grid=(heads,),
        in_specs=[
            head,
            head,
            head,
            pl.BlockSpec((1, 1, queries), lambda h: (h, 0, 0)),
            whole((keys, HD)),
            whole((keys, HD)),
            whole((HD, keys)),
            whole((keys, 1)),
            whole((1, queries)),
            whole((queries, HD)),
            whole((queries, HD)),
        ],
        out_specs=[head, whole((keys, HD)), whole((keys, HD))],
        out_shape=[
            jax.ShapeDtypeStruct((queries, width), LOW),
            jax.ShapeDtypeStruct((keys, HD), FULL),
            jax.ShapeDtypeStruct((keys, HD), FULL),
        ],
        scratch_shapes=[pltpu.VMEM((keys, queries), FULL)],
        compiler_params=pltpu.CompilerParams(vmem_limit_bytes=40 * MIB),
        cost_estimate=LIGHT,
    )(
        rot,
        grad,
        mixed,
        logs,
        key_value[:, :HD],
        key_value[:, HD:],
        key_value[:, :HD].T,
        key_segments[:, None],
        query_segments[None, :],
        cosine,
        sine,
    )


GELU_A = 0.7978845608028654
GELU_B = 0.044715


def hidden_kernel(count, *refs):
    normed_refs, cot_refs, pieces = refs[:2], refs[2:4], refs[4 : 4 + count]
    out_ref, weights_out, weights, sems = refs[4 + count :]
    step, steps = pl.program_id(0), pl.num_programs(0)
    me = lax.axis_index("tok")
    side, z, ring = (me // SIDE) % 2, me // RING, count // 2
    rows = weights.shape[0] // count

    def load(k):
        if count == 1:
            start = 0
        else:
            start = 2 * ((z - k // 2 + ring) % ring) + (side if k % 2 == 0 else 1 - side)
        return pltpu.make_async_copy(
            pieces[k], weights.at[pl.ds(pl.multiple_of(start * rows, 16), rows)], sems.at[k]
        )

    keep = pltpu.make_async_copy(weights, weights_out, sems.at[count])

    @pl.when(step == 0)
    def _():
        for k in range(count):
            load(k).start()
        for k in range(count):
            load(k).wait()
        keep.start()

    early = step < steps // 2
    normed = jnp.where(early, normed_refs[0][...], normed_refs[1][...])
    cotangent = jnp.where(early, cot_refs[0][...], cot_refs[1][...])
    columns = out_ref.shape[2]
    gate = matmul(normed, weights[:, :columns])
    up = matmul(normed, weights[:, columns : 2 * columns])
    grad_hidden = matmul(cotangent, weights[:, 2 * columns :])
    activation_grads(out_ref, gate, up, grad_hidden)

    @pl.when(step == steps - 1)
    def _():
        keep.wait()


def hidden_and_grads(normed, cotangent, pieces):
    half, width = normed[0].shape
    columns = pieces[0].shape[1] // 3
    rows = min(256, half)
    steps = half // rows
    count = len(pieces)
    if count >= 4 and pieces[0].shape[0] % 64 == 0:
        return hidden_by_depth(normed, cotangent, pieces)
    blocks = [
        pl.BlockSpec((rows, width), lambda i: (jnp.minimum(i, steps - 1), 0)),
        pl.BlockSpec((rows, width), lambda i: (jnp.maximum(i - steps, 0), 0)),
    ]
    anywhere = pl.BlockSpec(memory_space=pl.ANY)
    return pl.pallas_call(
        functools.partial(hidden_kernel, count),
        grid=(2 * steps,),
        in_specs=blocks * 2 + [anywhere] * count,
        out_specs=[pl.BlockSpec((3, rows, columns), lambda i: (0, i, 0)), anywhere],
        out_shape=[
            jax.ShapeDtypeStruct((3, 2 * half, columns), LOW),
            jax.ShapeDtypeStruct((width, 3 * columns), LOW),
        ],
        scratch_shapes=[
            pltpu.VMEM((width, 3 * columns), LOW),
            pltpu.SemaphoreType.DMA((count + 1,)),
        ],
        compiler_params=pltpu.CompilerParams(vmem_limit_bytes=48 * MIB),
        cost_estimate=LIGHT,
    )(*normed, *cotangent, *pieces)


def activation_grads(out_ref, gate, up, grad_hidden):
    square = gate * gate
    bent = jnp.tanh(gate * (GELU_A + GELU_A * GELU_B * square))
    half = 0.5 * (1.0 + bent)
    value = gate * half
    slope = half + 0.5 * gate * (1.0 - bent * bent) * (GELU_A + 3.0 * GELU_A * GELU_B * square)
    out_ref[0] = (grad_hidden * up * slope).astype(LOW)
    out_ref[1] = (grad_hidden * value).astype(LOW)
    out_ref[2] = (value * up).astype(LOW)


def depth_kernel(ring, first, count, last, *refs):
    normed_refs, cot_refs, pieces, refs = refs[:2], refs[2:4], refs[4 : 4 + count], refs[4 + count :]
    if last:
        partial_ref, _, out_ref, weights_out, weights, sems = refs
    else:
        out_ref, weights_out, weights, sems = refs
    step, steps = pl.program_id(0), pl.num_programs(0)
    me = lax.axis_index("tok")
    side, z = (me // SIDE) % 2, me // RING
    rows = weights.shape[0] // count
    wide = 2 * rows

    def chunk(k):
        return (z - first - k + 2 * ring) % ring

    def load(k):
        start = wide * (k // 2) + rows * (side if k % 2 == 0 else 1 - side)
        return pltpu.make_async_copy(
            pieces[k], weights.at[pl.ds(pl.multiple_of(start, 16), rows)], sems.at[k]
        )

    def keep(k):
        return pltpu.make_async_copy(
            weights.at[pl.ds(wide * k, wide)],
            weights_out.at[pl.ds(pl.multiple_of(chunk(k) * wide, 16), wide)],
            sems.at[count + k],
        )

    @pl.when(step == 0)
    def _():
        for k in range(count):
            load(k).start()
        for k in range(count):
            load(k).wait()
        for k in range(count // 2):
            keep(k).start()

    early = step < steps // 2

    def columns_of(pair):
        parts = []
        for k in range(count // 2):
            lanes = pl.ds(pl.multiple_of(chunk(k) * wide, HD), wide)
            parts.append(jnp.where(early, pair[0][:, lanes], pair[1][:, lanes]))
        return parts[0] if len(parts) == 1 else jnp.concatenate(parts, axis=1)

    normed, cotangent = columns_of(normed_refs), columns_of(cot_refs)
    columns = out_ref.shape[2]
    products = [
        matmul(left, weights[:, k * columns : (k + 1) * columns])
        for k, left in enumerate((normed, normed, cotangent))
    ]
    if last:
        activation_grads(out_ref, *(products[k] + partial_ref[k].astype(FULL) for k in range(3)))
    else:
        for k in range(3):
            out_ref[k] = products[k].astype(LOW)

    @pl.when(step == steps - 1)
    def _():
        for k in range(count // 2):
            keep(k).wait()


def hidden_by_depth(normed, cotangent, pieces):
    half, width = normed[0].shape
    columns = pieces[0].shape[1] // 3
    rows = min(256, half)
    steps = half // rows
    ring = len(pieces) // 2
    deep = width // ring
    blocks = [
        pl.BlockSpec((rows, width), lambda i: (jnp.minimum(i, steps - 1), 0)),
        pl.BlockSpec((rows, width), lambda i: (jnp.maximum(i - steps, 0), 0)),
    ]
    anywhere = pl.BlockSpec(memory_space=pl.ANY)
    block = pl.BlockSpec((3, rows, columns), lambda i: (0, i, 0))
    weights_shape = jax.ShapeDtypeStruct((width, 3 * columns), LOW)

    def part(first, given, more):
        count = len(given)
        return pl.pallas_call(
            functools.partial(depth_kernel, ring, first, count, len(more) > 0),
            grid=(2 * steps,),
            in_specs=blocks * 2 + [anywhere] * count + [block, anywhere][: len(more)],
            out_specs=[block, anywhere],
            out_shape=[jax.ShapeDtypeStruct((3, 2 * half, columns), LOW), weights_shape],
            input_output_aliases={5 + count: 1} if more else {},
            scratch_shapes=[
                pltpu.VMEM((deep * (count // 2), 3 * columns), LOW),
                pltpu.SemaphoreType.DMA((count + count // 2,)),
            ],
            compiler_params=pltpu.CompilerParams(vmem_limit_bytes=48 * MIB),
            cost_estimate=LIGHT,
        )(*normed, *cotangent, *given, *more)

    partial = part(0, pieces[:-2], [])
    return part(ring - 1, pieces[-2:], partial)


def project_sum_kernel(count, blocks, array_ref, *refs):
    weight_refs, out_ref = refs[:count], refs[count]
    away, arrived, send_sem, recv_sem = refs[count + 1 :]
    step, column = pl.program_id(0), pl.program_id(1)
    columns, rows = pl.num_programs(1), out_ref.shape[0]
    me = lax.axis_index("tok")
    mate = me + 1 - 2 * (me % 2)

    def crossing(block):
        return pltpu.make_async_remote_copy(
            src_ref=away.at[block],
            dst_ref=arrived.at[block],
            send_sem=send_sem.at[block],
            recv_sem=recv_sem.at[block],
            device_id=(mate,),
            device_id_type=pl.DeviceIdType.MESH,
        )

    @pl.when((step == 0) & (column == 0))
    def _():
        barrier = pltpu.get_barrier_semaphore()
        pl.semaphore_signal(
            barrier, inc=1, device_id=(mate,), device_id_type=pl.DeviceIdType.MESH
        )
        pl.semaphore_wait(barrier, 1)

    total = by_rows(array_ref[0], weight_refs[0][...])
    for k in range(1, count):
        total += by_rows(array_ref[k], weight_refs[k][...])
    for block in range(blocks):

        @pl.when(step == block)
        def _():
            away[block, column] = total.astype(LOW)

            @pl.when(column == columns - 1)
            def _():
                crossing(block).start()

        @pl.when(step == blocks + block)
        def _():
            @pl.when(column == 0)
            def _():
                crossing(block).wait()

            out_ref[...] = (total + arrived[block, column].astype(FULL)).astype(LOW)


def project_sum(array, pack, first, count, identity, marks=()):
    array = after(array, *jax.tree.leaves(marks))
    tokens, columns = array.shape[1:]
    width = pack.shape[0]
    rows, wide = tokens // 4, width
    blocks = tokens // rows // 2
    return pl.pallas_call(
        functools.partial(project_sum_kernel, count, blocks),
        grid=(2 * blocks, width // wide),
        in_specs=[
            pl.BlockSpec(
                (count, rows, columns), lambda i, j: (first // count, (i + blocks) % (2 * blocks), 0)
            )
        ]
        + [
            pl.BlockSpec(
                (wide, columns), lambda i, j, k=k: (j, first + k), pipeline_mode=pl.Buffered(1)
            )
            for k in range(count)
        ],
        out_specs=pl.BlockSpec(
            (rows, wide),
            lambda i, j: (jnp.maximum(i - blocks, 0), jnp.where(i >= blocks, j, 0)),
        ),
        out_shape=jax.ShapeDtypeStruct((tokens // 2, width), LOW),
        scratch_shapes=[
            pltpu.VMEM((blocks, width // wide, rows, wide), LOW),
            pltpu.VMEM((blocks, width // wide, rows, wide), LOW),
            pltpu.SemaphoreType.DMA((blocks,)),
            pltpu.SemaphoreType.DMA((blocks,)),
        ],
        compiler_params=pltpu.CompilerParams(
            collective_id=identity, has_side_effects=True, vmem_limit_bytes=44 * MIB
        ),
        cost_estimate=LIGHT,
    )(array, *([pack] * count))


def outer_kernel(chunk_ref, *refs):
    normed_refs, cot_refs, right_ref, out_ref, total = refs[:2], refs[2:4], *refs[4:]
    step, steps = pl.program_id(0), pl.num_programs(0)
    early = step < steps // 2
    normed = jnp.where(early, normed_refs[0][...], normed_refs[1][...])
    cotangent = jnp.where(early, cot_refs[0][...], cot_refs[1][...])
    columns = right_ref.shape[2]

    @pl.when(step == 0)
    def _():
        total[...] = jnp.zeros_like(total)

    for k, left in enumerate((normed, normed, cotangent)):
        total[:, k * columns : (k + 1) * columns] += outer_sum(left, right_ref[k])

    @pl.when(step == steps - 1)
    def _():
        out_ref[...] = total[...].astype(LOW)


def outer_products(normed, cotangent, array, chunk, rows):
    tokens, columns = array.shape[1:]
    deep = min(512, tokens // 2)
    steps = tokens // 2 // deep
    lefts = [
        pl.BlockSpec((deep, rows), lambda i, chunk_ref: (jnp.minimum(i, steps - 1), chunk_ref[0])),
        pl.BlockSpec((deep, rows), lambda i, chunk_ref: (jnp.maximum(i - steps, 0), chunk_ref[0])),
    ]
    return pl.pallas_call(
        outer_kernel,
        grid_spec=pltpu.PrefetchScalarGridSpec(
            num_scalar_prefetch=1,
            grid=(2 * steps,),
            in_specs=lefts * 2
            + [pl.BlockSpec((3, deep, columns), lambda i, chunk_ref: (0, i, 0))],
            out_specs=pl.BlockSpec((rows, 3 * columns), lambda i, chunk_ref: (0, 0)),
            scratch_shapes=[pltpu.VMEM((rows, 3 * columns), FULL)],
        ),
        out_shape=jax.ShapeDtypeStruct((rows, 3 * columns), LOW),
        compiler_params=pltpu.CompilerParams(vmem_limit_bytes=40 * MIB),
        cost_estimate=LIGHT,
    )(chunk[None].astype(jnp.int32), *normed, *cotangent, array)


def join_kernel(count, epsilon, *refs):
    inputs_ref, gain_ref, weight_ref = refs[:3]
    parts, (middle_ref, normed_ref, inverse_ref) = refs[3 : 3 + count], refs[3 + count :]
    total, start = inputs_ref[...].astype(FULL), 0
    for part in parts:
        columns = part.shape[1]
        total += by_rows(part[...], weight_ref[:, start : start + columns])
        start += columns
    inverse = lax.rsqrt(jnp.mean(total * total, axis=1, keepdims=True) + epsilon)
    middle_ref[...] = total
    inverse_ref[...] = jnp.broadcast_to(inverse, inverse_ref.shape)
    normed_ref[...] = (total * inverse * gain_ref[...]).astype(LOW)


def join(tokens, gain, weight, parts):
    count, width = tokens.shape
    rows = min(256, count)
    block = lambda columns: pl.BlockSpec((rows, columns), lambda i: (i, 0))
    return pl.pallas_call(
        functools.partial(join_kernel, len(parts), EPSILON),
        grid=(count // rows,),
        in_specs=[
            block(width),
            pl.BlockSpec((1, width), lambda i: (0, 0)),
            pl.BlockSpec((width, width), lambda i: (0, 0), pipeline_mode=pl.Buffered(1)),
        ]
        + [block(part.shape[1]) for part in parts],
        out_specs=[block(width), block(width), block(HD)],
        out_shape=[
            jax.ShapeDtypeStruct((count, width), FULL),
            jax.ShapeDtypeStruct((count, width), LOW),
            jax.ShapeDtypeStruct((count, HD), FULL),
        ],
        compiler_params=pltpu.CompilerParams(vmem_limit_bytes=40 * MIB),
        cost_estimate=LIGHT,
    )(tokens, gain[None], weight, *parts)


def branch_kernel(
    group_ref, near_ref, cot_ref, middle_ref, inverse_ref, gain_ref, weight_ref,
    grad_ref, branch_ref, mixed_ref, scaled_ref,
):
    grad = group_ref[...].astype(FULL) + near_ref[...].astype(FULL)
    middle, inverse = middle_ref[...], inverse_ref[:, :1]
    normal = middle * inverse
    scaled_ref[...] = (grad * normal).astype(LOW)
    scaled = grad * gain_ref[...]
    total = (
        cot_ref[...].astype(FULL)
        + inverse * scaled
        - normal * (inverse * jnp.mean(scaled * normal, axis=1, keepdims=True))
    )
    grad_ref[...] = total
    branch = total.astype(LOW)
    branch_ref[...] = branch
    mixed_ref[...] = matmul(branch, weight_ref[...]).astype(LOW)


def branch_back(group, near, cotangent, middle, inverse, gain, weight):
    count, width = middle.shape
    rows = min(256, count)
    block = lambda columns: pl.BlockSpec((rows, columns), lambda i: (i, 0))
    return pl.pallas_call(
        branch_kernel,
        grid=(count // rows,),
        in_specs=[
            block(width),
            block(width),
            block(width),
            block(width),
            block(HD),
            pl.BlockSpec((1, width), lambda i: (0, 0)),
            pl.BlockSpec((width, width), lambda i: (0, 0), pipeline_mode=pl.Buffered(1)),
        ],
        out_specs=[block(width)] * 4,
        out_shape=[
            jax.ShapeDtypeStruct((count, width), FULL),
            jax.ShapeDtypeStruct((count, width), LOW),
            jax.ShapeDtypeStruct((count, width), LOW),
            jax.ShapeDtypeStruct((count, width), LOW),
        ],
        compiler_params=pltpu.CompilerParams(vmem_limit_bytes=48 * MIB),
        cost_estimate=LIGHT,
    )(group, near, cotangent, middle, inverse, gain[None], weight)


def on_device(
    tokens, cotangent, attn_gain, ffn_gain, w_query, w_key, w_value, w_out, w_gate, w_up, w_down,
    segments, positions,
):
    token_count, width = tokens.shape
    own_rows, hidden_width = w_gate.shape
    slice_width = hidden_width // GROUP
    heads_width = w_query.shape[1]
    tail_rows = min(token_count, WINDOW)
    hop_count = WINDOW // tail_rows
    device = lax.axis_index("tok")
    inputs = tokens.astype(FULL)

    frequency = 10000.0 ** (-jnp.arange(HD // 2, dtype=FULL) * 2.0 / HD)
    angles = positions.astype(FULL)[:, None] * frequency[None, :]
    cosine = jnp.concatenate([jnp.cos(angles)] * 2, axis=1)
    sine_half = jnp.sin(angles)
    sine = jnp.concatenate([-sine_half, sine_half], axis=1)
    padded_segments = jnp.concatenate([jnp.full((WINDOW,), -1, jnp.int32), segments])
    key_segments = lax.dynamic_slice_in_dim(
        padded_segments, device * token_count, WINDOW + token_count
    )
    query_segments = lax.dynamic_slice_in_dim(segments, device * token_count, token_count)

    attn_pack = jnp.concatenate(
        [
            w_query,
            w_key,
            w_value,
            jnp.pad(
                jnp.stack([attn_gain, ffn_gain], axis=1), ((0, 0), (0, HD - 2))
            ),
        ],
        axis=1,
    )
    edge = heads_width + 2 * HD
    def sliced(weight):
        return weight.reshape(own_rows, GROUP, slice_width).transpose(1, 0, 2)

    ffn_pack = jnp.concatenate([sliced(w_gate), sliced(w_up), sliced(w_down)], axis=2)
    attn_all, ffn_rows = gather(attn_pack, ffn_pack)
    out_w = lax.all_gather(w_out, "tok", axis=0, tiled=True)
    query_w, kv_w = attn_all[:, :heads_width], attn_all[:, heads_width:edge]
    gains = attn_all[:, edge : edge + 2].astype(FULL)
    gain_one, gain_two = gains[:, 0], gains[:, 1]

    inverse_one = lax.rsqrt(jnp.mean(inputs * inputs, axis=-1, keepdims=True) + EPSILON)
    normed = (inputs * inverse_one * gain_one).astype(LOW)
    kv = matmul(normed, kv_w)

    def turned(values, sine_signed):
        half = HD // 2
        rolled = jnp.concatenate([values[:, half:], values[:, :half]], axis=1)
        return values * cosine + rolled * sine_signed

    key_value = jnp.concatenate([turned(kv[:, :HD], sine), kv[:, HD:]], axis=1).astype(LOW)
    received = [passed_along(key_value, hop) for hop in range(hop_count, 0, -1)]
    all_keys = jnp.concatenate(received + [key_value], axis=0)
    raw_query = matmul(normed, query_w)
    heads = heads_width // HD
    given = (all_keys, key_segments, query_segments, cosine, sine)
    early = attend(raw_query, *given, 0, heads // 2)
    pieces, steps = spread(ffn_rows, (early[1],))
    cot_group = rows_to_group(after(cotangent, attn_all), steps[1])
    late = attend(
        after(raw_query, early[1]), *given, heads // 2, heads - heads // 2
    )
    rot, mixed = (jnp.concatenate([early[k], late[k]], axis=1) for k in range(2))
    logs = jnp.concatenate([early[2], late[2]], axis=0)
    middle, normed_two, inverse_two = join(tokens, gain_two, out_w, (early[1], late[1]))

    normed_group = rows_to_group(after(normed_two, *steps[1]), steps[2])
    hidden_pack, ffn_w = hidden_and_grads(normed_group, cot_group, pieces)
    reduction = Reduction(normed_group, cot_group, hidden_pack)
    pairs_done = reduction.multiply(0)
    reduction.begin()
    pairs_done = reduction.multiply(1, pairs_done)
    group_sum = project_sum(hidden_pack, ffn_w, 0, 2, 2, pairs_done)
    near_sent = flip(group_sum[token_count:], NEAR)
    marks = reduction.advance(0, group_sum)
    pairs_done = reduction.multiply(2, marks)
    pairs_done = reduction.multiply(3, pairs_done)
    marks = reduction.advance(1, pairs_done)
    output_sum = project_sum(hidden_pack, ffn_w, 2, 1, 3, marks)
    output_near = flip(after(output_sum, near_sent)[token_count:], NEAR)

    grad_middle, branch, grad_mixed, gain_two_parts = branch_back(
        group_sum[:token_count], after(near_sent, output_sum), cotangent, middle, inverse_two, gain_two, out_w
    )
    grad_out_w = outer_sum(branch, mixed).astype(LOW)
    out_sum = lax.psum_scatter(grad_out_w, "tok", scatter_dimension=0, tiled=True).astype(FULL)
    marks = reduction.advance(2, grad_mixed)
    query_low, key_grads, value_grads = attend_back(
        rot, after(grad_mixed, *marks), mixed, logs, all_keys, key_segments, query_segments, cosine, sine
    )
    output = (
        middle + output_sum[:token_count].astype(FULL) + after(output_near, query_low).astype(FULL)
    ).astype(LOW)
    grads = jnp.concatenate([key_grads * HD**-0.5, value_grads], axis=1)
    shares = grads[WINDOW:]
    for hop in range(1, hop_count + 1):
        first_row = (hop_count - hop) * tail_rows
        returned = passed_along(grads[first_row : first_row + tail_rows].astype(LOW), -hop)
        shares = shares.at[token_count - tail_rows :].add(returned.astype(FULL))
    kv_low = jnp.concatenate([turned(shares[:, :HD], -sine), shares[:, HD:]], axis=1).astype(LOW)
    grad_query_w = outer_sum(normed, query_low).astype(LOW)
    grad_kv_w = outer_sum(normed, kv_low).astype(LOW)
    grad_normed = by_rows(query_low, query_w) + by_rows(kv_low, kv_w)
    scaled_one = grad_normed * gain_one
    grad_inputs = inverse_one * scaled_one - inputs * inverse_one**3 * jnp.mean(
        scaled_one * inputs, axis=-1, keepdims=True
    )
    grad_tokens = (grad_middle + grad_inputs).astype(LOW)
    lane = lax.broadcasted_iota(jnp.int32, (token_count, HD), 1)
    grad_gains = (
        outer_sum((grad_normed * inputs * inverse_one).astype(LOW), (lane == 0).astype(LOW))
        + outer_sum(gain_two_parts, (lane == 1).astype(LOW))
    ).astype(LOW)
    reduction.advance(3, grad_query_w)
    attn_sum, ffn_parts = scatter(
        [grad_query_w, grad_kv_w, grad_gains], reduction.result()
    )

    def joined(parts):
        return parts.transpose(1, 0, 2).reshape(own_rows, hidden_width).astype(FULL)

    return (
        output,
        grad_tokens,
        attn_sum[:, edge],
        attn_sum[:, edge + 1],
        attn_sum[:, :heads_width],
        attn_sum[:, heads_width : heads_width + HD],
        attn_sum[:, heads_width + HD : edge],
        out_sum,
        joined(ffn_parts[:, :, :slice_width]),
        joined(ffn_parts[:, :, slice_width : 2 * slice_width]),
        joined(ffn_parts[:, :, 2 * slice_width :]),
    )


def solution(mesh):
    rows, flat = P("tok", None), P("tok")
    return jax.shard_map(
        on_device,
        mesh=mesh,
        in_specs=(rows, rows, flat, flat, rows, rows, rows, rows, rows, rows, rows, P(), flat),
        out_specs=(rows, rows, flat, flat, rows, rows, rows, rows, rows, rows, rows),
        check_vma=False,
    )
```

```python
import functools

import jax
import jax.numpy as jnp
from jax import lax
from jax.experimental import pallas as pl
from jax.experimental.pallas import tpu as pltpu
from jax.sharding import PartitionSpec as P

HQ = 12
HD = 128
WINDOW = 1024
EPSILON = 1e-06

CORE, NEAR, SIDE, GROUP, RING = 1, 2, 4, 4, 8
LONGEST_RING = 8
LOG2E = 1.4426950408889634
LOW = jnp.bfloat16
FULL = jnp.float32
MIB = 1024 * 1024
LIGHT = pl.CostEstimate(flops=1024, bytes_accessed=1024, transcendentals=0)


def flip(array, bit):
    size = lax.axis_size("tok")
    return lax.ppermute(array, "tok", [(i, i ^ bit) for i in range(size)])


def around(array):
    size = lax.axis_size("tok")
    return lax.ppermute(array, "tok", [(i, (i + RING) % size) for i in range(size)])


def passed_along(array, by):
    size = lax.axis_size("tok")
    pairs = [(i, i + by) for i in range(size) if 0 <= i + by < size]
    return lax.ppermute(array, "tok", pairs)


def rms_norm(values, scales):
    return values * lax.rsqrt(jnp.mean(values * values, axis=-1, keepdims=True) + EPSILON) * scales


def outer_sum(left_side, right_side):
    return lax.dot_general(
        left_side, right_side, (((0,), (0,)), ((), ())), preferred_element_type=FULL
    )


def by_rows(left_side, right_side):
    return lax.dot_general(
        left_side, right_side, (((1,), (1,)), ((), ())), preferred_element_type=FULL
    )


def matmul(left_side, right_side):
    return jnp.dot(left_side, right_side, preferred_element_type=FULL)


def pick(array, index):
    return lax.dynamic_index_in_dim(array, index, 0, keepdims=False)


def place():
    device = lax.axis_index("tok")
    return device, device % 2, (device // 2) % 2, (device // 4) % 2, device // RING


def rows_to_group(array, marks=()):
    two = jnp.concatenate([array, after(flip(array, NEAR), *marks)], axis=0)
    return two, flip(two, CORE)


def slices_to_group(parts):
    _, core, near, _, _ = place()
    rows, columns = parts.shape[1:]
    mine = lax.dynamic_slice_in_dim(parts, 2 * near, 2, 0)
    theirs = flip(lax.dynamic_slice_in_dim(parts, 2 * (1 - near), 2, 0), NEAR)
    here = jnp.stack([pick(mine, core), pick(theirs, core)])
    away = flip(jnp.stack([pick(mine, 1 - core), pick(theirs, 1 - core)]), CORE)
    by_core = jnp.where(core == 0, jnp.stack([here, away], 1), jnp.stack([away, here], 1))
    by_near = jnp.where(near == 0, by_core, by_core[::-1])
    return by_near.reshape(4 * rows, columns)


def slices_from_group(block):
    _, core, near, _, _ = place()
    rows, columns = block.shape[0] // 4, block.shape[1]
    parts = block.astype(LOW).reshape(2, 2, rows, columns)
    mine, theirs = pick(parts, near), flip(pick(parts, 1 - near), NEAR)
    here = jnp.stack([pick(mine, core), pick(theirs, core)])
    away = flip(jnp.stack([pick(mine, 1 - core), pick(theirs, 1 - core)]), CORE)
    by_core = jnp.where(core == 0, jnp.stack([here, away], 1), jnp.stack([away, here], 1))
    by_near = jnp.where(near == 0, by_core, by_core[::-1])
    return by_near.reshape(4, rows, columns)


def gather_kernel(
    ring, bands, attn_ref, ffn_ref, attn_out, ffn_out, local_sem, send_sem, recv_sem
):
    size = ring * RING
    me = lax.axis_index("tok")
    core, near, side, z = me % 2, (me // 2) % 2, (me // 4) % 2, me // RING
    core_mate, near_mate, side_mate = me + 1 - 2 * core, me + 2 - 4 * near, me + 4 - 8 * side
    far_mate = near_mate + 1 - 2 * core
    up, down = (me + RING) % size, (me + size - RING) % size

    barrier = pltpu.get_barrier_semaphore()
    partners = (core_mate, near_mate, side_mate, far_mate, up, down)
    for partner in partners:
        pl.semaphore_signal(
            barrier, inc=1, device_id=(partner,), device_id_type=pl.DeviceIdType.MESH
        )
    pl.semaphore_wait(barrier, len(partners))

    own = pltpu.make_async_copy(attn_ref, attn_out.at[z, side, near, core], local_sem.at[0])
    own.start()
    own_slice = pltpu.make_async_copy(
        ffn_ref.at[2 * near + core], ffn_out.at[2 * near + core], local_sem.at[1]
    )
    own_slice.start()

    copies = []

    def send(src, dst, to):
        index = len(copies)
        copy = pltpu.make_async_remote_copy(
            src_ref=src,
            dst_ref=dst,
            send_sem=send_sem.at[index],
            recv_sem=recv_sem.at[index],
            device_id=(to,),
            device_id_type=pl.DeviceIdType.MESH,
        )
        copy.start()
        copies.append(copy)
        return copy

    def forward(ref, to):
        return send(ref, ref, to)

    def chunk_of(step):
        return (z - step + ring) % ring

    def piece(step, band):
        return attn_out.at[chunk_of(step), side, near, core, bands[band]]

    hops, first, second, last = {}, {}, {}, {}
    over = []

    def finish(step):
        first[0, step].wait_recv()
        second[0, step] = forward(attn_out.at[chunk_of(step), side, :, core, bands[0]], side_mate)
        first[1, step].wait_recv()
        second[1, step] = forward(attn_out.at[chunk_of(step), :, near, core, bands[1]], near_mate)

    def hand_over(step):
        second[0, step].wait_recv()
        second[1, step].wait_recv()
        over.append(forward(attn_out.at[chunk_of(step), :, :, core], core_mate))

    for step in range(ring):
        for band in (0, 1):
            if step > 0:
                hops[band, step].wait_recv()
            source = attn_ref.at[bands[band]] if step == 0 else piece(step, band)
            if step < ring - 1:
                hops[band, step + 1] = send(source, piece(step, band), up)
            mate = near_mate if band == 0 else side_mate
            first[band, step] = send(source, piece(step, band), mate)
        if step == 0:
            begun = send(attn_ref.at[bands[2]], piece(0, 2), near_mate)
            slices = [
                send(ffn_ref.at[index], ffn_out.at[2 * near + core], mate)
                for mate, index in (
                    (near_mate, 2 * (1 - near) + core),
                    (far_mate, 2 * (1 - near) + 1 - core),
                    (core_mate, 2 * near + 1 - core),
                )
            ]
            own.wait()
            begun.wait_recv()
            last[0] = forward(attn_out.at[z, side, :, core, bands[2]], side_mate)
        else:
            last[step - 1].wait_recv()
            last[step] = forward(attn_out.at[chunk_of(step - 1), :, :, core, bands[2]], up)
            finish(step - 1)
        if step >= 2:
            hand_over(step - 2)
    finish(ring - 1)
    hand_over(ring - 2)
    last[ring - 1].wait_recv()
    hand_over(ring - 1)
    own_slice.wait()
    for copy in slices + over:
        copy.wait_recv()
    for copy in copies:
        copy.wait_send()


def gather(attn_pack, ffn_pack):
    size = lax.axis_size("tok")
    ring = size // RING
    rows, columns = attn_pack.shape
    if ring > LONGEST_RING or ring < 2 or rows % 48:
        return lax.all_gather(attn_pack, "tok", axis=0, tiled=True), slices_to_group(ffn_pack)
    third = rows // 3
    bands = [pl.ds(third * band, third) for band in range(3)]
    count = 3 + 2 * (ring - 1) + 2 * ring + 2 * ring + 1 + ring + ring
    anywhere = pl.BlockSpec(memory_space=pl.ANY)
    attn_all, ffn_rows = pl.pallas_call(
        functools.partial(gather_kernel, ring, bands),
        in_specs=[anywhere] * 2,
        out_specs=[anywhere] * 2,
        out_shape=[
            jax.ShapeDtypeStruct((ring, 2, 2, 2, rows, columns), attn_pack.dtype),
            jax.ShapeDtypeStruct(ffn_pack.shape, ffn_pack.dtype),
        ],
        scratch_shapes=[
            pltpu.SemaphoreType.DMA((2,)),
            pltpu.SemaphoreType.DMA((count,)),
            pltpu.SemaphoreType.DMA((count,)),
        ],
        compiler_params=pltpu.CompilerParams(collective_id=0, has_side_effects=True),
    )(attn_pack, ffn_pack)
    return attn_all.reshape(size * rows, columns), ffn_rows.reshape(GROUP * rows, -1)


def scatter_kernel(
    ring, bands, edges, *refs
):
    count = len(edges) - 1
    grad_refs, ffn_ref, attn_out, ffn_out = refs[:count], refs[count], refs[count + 1], refs[count + 2]
    pack, core_in, a_side, a_near, a_ring, b_near, b_side, b_ring, c_ring, c_side, c_near = refs[
        count + 3 : count + 14
    ]
    local_sem, send_sem, recv_sem = refs[count + 14 :]
    size = ring * RING
    me = lax.axis_index("tok")
    core, near, side, z = me % 2, (me // 2) % 2, (me // 4) % 2, me // RING
    core_mate, near_mate, side_mate = me + 1 - 2 * core, me + 2 - 4 * near, me + 4 - 8 * side
    far_mate = near_mate + 1 - 2 * core
    up, down = (me + RING) % size, (me + size - RING) % size

    def chunk_of(step):
        return (z - 1 - step + 2 * ring) % ring

    loads = []
    for step in range(ring):
        row = []
        for k in range(count):
            load = pltpu.make_async_copy(
                grad_refs[k].at[chunk_of(step)],
                pack.at[chunk_of(step), :, :, :, :, pl.ds(edges[k], edges[k + 1] - edges[k])],
                local_sem.at[step * count + k],
            )
            load.start()
            row.append(load)
        loads.append(row)
    own_slice = pltpu.make_async_copy(
        ffn_ref.at[2 * near + core], ffn_out.at[2 * near + core], local_sem.at[ring * count]
    )
    own_slice.start()

    barrier = pltpu.get_barrier_semaphore()
    partners = (core_mate, near_mate, side_mate, far_mate, up, down)
    for partner in partners:
        pl.semaphore_signal(
            barrier, inc=1, device_id=(partner,), device_id_type=pl.DeviceIdType.MESH
        )
    pl.semaphore_wait(barrier, len(partners))

    copies = []

    def send(src, dst, to):
        index = len(copies)
        copy = pltpu.make_async_remote_copy(
            src_ref=src,
            dst_ref=dst,
            send_sem=send_sem.at[index],
            recv_sem=recv_sem.at[index],
            device_id=(to,),
            device_id_type=pl.DeviceIdType.MESH,
        )
        copy.start()
        copies.append(copy)
        return copy

    def add(held, arrived):
        held[...] = (held[...].astype(FULL) + arrived[...].astype(FULL)).astype(LOW)

    def part(step, y, x, band):
        return pack.at[chunk_of(step), y, x, core, bands[band]]

    def own(step, band):
        return part(step, side, near, band)

    across, first, second, hops = {}, {}, {}, {}

    def begin(step):
        chunk = chunk_of(step)
        across[step].wait_recv()

        def one(k, _):
            add(pack.at[chunk, k // 2, k % 2, core], core_in.at[chunk, k // 2, k % 2])
            return 0

        lax.fori_loop(0, 4, one, 0)
        first[0, step] = send(
            pack.at[chunk, 1 - side, :, core, bands[0]], a_side.at[step], side_mate
        )
        first[1, step] = send(
            pack.at[chunk, :, 1 - near, core, bands[1]], b_near.at[step], near_mate
        )
        if step > 0:
            hops[2, step].wait_recv()
            for k in range(4):
                add(part(step, k // 2, k % 2, 2), c_ring.at[step - 1, k // 2, k % 2])
        if step < ring - 1:
            hops[2, step + 1] = send(
                pack.at[chunk, :, :, core, bands[2]], c_ring.at[step], up
            )

    def middle(step):
        first[0, step].wait_recv()
        for x in range(2):
            add(part(step, side, x, 0), a_side.at[step, x])
        second[0, step] = send(part(step, side, 1 - near, 0), a_near.at[step], near_mate)
        first[1, step].wait_recv()
        for y in range(2):
            add(part(step, y, near, 1), b_near.at[step, y])
        second[1, step] = send(part(step, 1 - side, near, 1), b_side.at[step], side_mate)

    def end(step):
        for band, arrived, passing in ((0, a_near, a_ring), (1, b_side, b_ring)):
            second[band, step].wait_recv()
            add(own(step, band), arrived.at[step])
            if step > 0:
                hops[band, step].wait_recv()
                add(own(step, band), passing.at[step - 1])
            if step < ring - 1:
                hops[band, step + 1] = send(own(step, band), passing.at[step], up)

    for step in range(ring):
        for load in loads[step]:
            load.wait()
        across[step] = send(
            pack.at[chunk_of(step), :, :, 1 - core], core_in.at[chunk_of(step)], core_mate
        )
    slices = []
    for step in range(ring + 2):
        if step < ring:
            begin(step)
        if step == 0:
            slices += [
                send(ffn_ref.at[index], ffn_out.at[2 * near + core], mate)
                for mate, index in (
                    (near_mate, 2 * (1 - near) + core),
                    (far_mate, 2 * (1 - near) + 1 - core),
                    (core_mate, 2 * near + 1 - core),
                )
            ]
        if 1 <= step <= ring:
            middle(step - 1)
        if step == ring:
            last = ring - 1
            to_side = send(pack.at[z, 1 - side, :, core, bands[2]], c_side, side_mate)
        if step >= 2:
            end(step - 2)
        if step == ring:
            to_side.wait_recv()
            for x in range(2):
                add(part(last, side, x, 2), c_side.at[x])
            to_near = send(part(last, side, 1 - near, 2), c_near, near_mate)
    to_near.wait_recv()
    add(own(last, 2), c_near)
    attn_out[...] = pack[z, side, near, core].astype(FULL)
    own_slice.wait()
    for copy in slices:
        copy.wait_recv()
    for copy in copies:
        copy.wait_send()


def scatter(grads, ffn_sum):
    size = lax.axis_size("tok")
    ring = size // RING
    rows = grads[0].shape[0] // size
    if ring > LONGEST_RING or ring < 2 or rows % 48:
        joined = jnp.concatenate(grads, axis=1).astype(FULL)
        return (
            lax.psum_scatter(joined, "tok", scatter_dimension=0, tiled=True),
            slices_from_group(ffn_sum),
        )
    third = rows // 3
    bands = [pl.ds(third * band, third) for band in range(3)]
    edges = [0]
    for grad in grads:
        edges.append(edges[-1] + grad.shape[1])
    columns = edges[-1]
    count = ring + 2 * ring + (ring - 1) + 3 + 2 * ring + 1 + 2 * (ring - 1) + 1
    anywhere = pl.BlockSpec(memory_space=pl.ANY)
    band = (third, columns)
    low = lambda *shape: pltpu.VMEM((*shape, *band), LOW)
    return pl.pallas_call(
        functools.partial(scatter_kernel, ring, bands, edges),
        in_specs=[anywhere] * (len(grads) + 1),
        out_specs=[pl.BlockSpec(memory_space=pltpu.VMEM), anywhere],
        out_shape=[
            jax.ShapeDtypeStruct((rows, columns), FULL),
            jax.ShapeDtypeStruct((GROUP, rows, ffn_sum.shape[1]), LOW),
        ],
        scratch_shapes=[
            pltpu.VMEM((ring, 2, 2, 2, rows, columns), LOW),
            pltpu.VMEM((ring, 2, 2, rows, columns), LOW),
            low(ring, 2),
            low(ring),
            low(ring - 1),
            low(ring, 2),
            low(ring),
            low(ring - 1),
            low(ring - 1, 2, 2),
            low(2),
            low(),
            pltpu.SemaphoreType.DMA((ring * len(grads) + 1,)),
            pltpu.SemaphoreType.DMA((count,)),
            pltpu.SemaphoreType.DMA((count,)),
        ],
        compiler_params=pltpu.CompilerParams(
            collective_id=1, has_side_effects=True, vmem_limit_bytes=44 * MIB
        ),
    )(
        *[grad.reshape(ring, 2, 2, 2, rows, -1) for grad in grads],
        ffn_sum.astype(LOW).reshape(GROUP, rows, -1),
    )


def after(value, *marks):
    return lax.optimization_barrier((value, *marks))[0]


def groups_of(stride):
    size = lax.axis_size("tok")
    return [[s + stride * k for k in range(size // stride)] for s in range(stride)]


def spread(block, marks):
    size = lax.axis_size("tok")
    ring = size // RING
    if ring > LONGEST_RING:
        gathered = lax.all_gather(
            block, "tok", axis=0, tiled=True, axis_index_groups=groups_of(GROUP)
        )
        return [gathered], [()] * 3
    own, crossed = [block], []
    for step in range(ring):
        crossed.append(flip(own[-1], SIDE))
        if step < ring - 1:
            arrived = around(own[-1])
            if step == 0:
                arrived, crossed[0] = lax.optimization_barrier((arrived, crossed[0], *marks))[:2]
            own.append(arrived)
    pieces = [piece for pair in zip(own, crossed) for piece in pair]
    return pieces, [(*own[step + 1 : step + 2], crossed[step]) for step in range(ring)]


class Reduction:
    def __init__(self, normed, cotangent, array):
        self.given = (normed, cotangent, array)
        self.size = lax.axis_size("tok")
        self.ring = self.size // RING
        _, _, _, _, self.z = place()
        self.rows = normed[0].shape[1] // (self.ring * 2)
        self.short = 2 <= self.ring <= LONGEST_RING and self.rows % 64 == 0
        self.blocks, self.crossing, self.total = {}, None, None

    def multiply(self, step, mark=None):
        if not self.short:
            return ()
        chunk = lax.rem(self.z - 1 - step + 2 * self.ring, self.ring)
        normed, cotangent, array = self.given
        array = after(array, *jax.tree.leaves(mark))
        self.blocks[step] = outer_products(normed, cotangent, array, chunk, 2 * self.rows)
        return self.blocks[step][0]

    def begin(self):
        if self.short:
            self.crossing = flip(self.blocks[0][0], SIDE)

    def advance(self, step, *marks):
        if not self.short:
            return ()
        arrived = (self.crossing,) if self.total is None else (self.crossing, self.total)
        give = self.blocks[min(step + 1, self.ring - 1)][0]
        give, *arrived = lax.optimization_barrier((give, *arrived, *marks))[: len(arrived) + 1]
        total = self.blocks[step][1].astype(FULL)
        for part in arrived:
            total = total + part.astype(FULL)
        if step == self.ring - 1:
            self.sum = total.astype(LOW)
            return (self.sum,)
        low = total.astype(LOW)
        self.total, self.crossing = around(low), flip(give, SIDE)
        return (low, give)

    def result(self):
        if self.short:
            return self.sum
        normed, cotangent = (jnp.concatenate(pair, axis=0) for pair in self.given[:2])
        array = self.given[2]
        joined = jnp.concatenate(
            [outer_sum(normed, array[0]), outer_sum(normed, array[1]), outer_sum(cotangent, array[2])],
            axis=1,
        )
        return lax.psum_scatter(
            joined, "tok", scatter_dimension=0, tiled=True, axis_index_groups=groups_of(GROUP)
        )


def turn(values, cosine, sine):
    return values * cosine + pltpu.roll(values, HD // 2, 1) * sine


def mask_into(bias, key_segments, query_segments, block):
    keys, queries = bias.shape
    for start in range(0, queries, block):
        offset = (
            lax.broadcasted_iota(jnp.int32, (keys, block), 0)
            - lax.broadcasted_iota(jnp.int32, (keys, block), 1)
            - start
        )
        same = key_segments[...] == query_segments[:, start : start + block]
        allowed = same & (offset > 0) & (offset <= WINDOW)
        bias[:, start : start + block] = jnp.where(allowed, 0.0, -jnp.inf)


def attend_kernel(
    block, factor, q_ref, key_ref, value_t_ref, ks_ref, qs_ref, cos_ref, sin_ref,
    rot_ref, mixed_ref, log_ref, bias,
):
    @pl.when(pl.program_id(0) == 0)
    def _():
        mask_into(bias, ks_ref, qs_ref, block)

    queries = q_ref.shape[0]
    rot_ref[...] = turn(q_ref[...], cos_ref[...], sin_ref[...]).astype(LOW)
    for start in range(0, queries, block):
        rows, span = pl.ds(start, block), pl.ds(start, WINDOW + block)
        raw = by_rows(key_ref[span, :], rot_ref[rows, :])
        score = raw * factor + bias[span, rows]
        top = jnp.max(score, axis=0, keepdims=True)
        expo = jnp.exp2(score - top)
        total = jnp.sum(expo, axis=0, keepdims=True)
        mixed_t = matmul(value_t_ref[:, span], expo.astype(LOW)) / total
        mixed_ref[rows, :] = mixed_t.T.astype(LOW)
        log_ref[0, :, rows] = top + jnp.log2(total)


def attend(raw_query, key_value, key_segments, query_segments, cosine, sine, first, heads):
    queries, width = raw_query.shape[0], heads * HD
    keys = key_value.shape[0]
    block = min(256, queries)
    head = pl.BlockSpec((queries, HD), lambda h: (0, h))
    whole = lambda shape: pl.BlockSpec(shape, lambda h: (0,) * len(shape))
    return pl.pallas_call(
        functools.partial(attend_kernel, block, HD**-0.5 * LOG2E),
        grid=(heads,),
        in_specs=[
            pl.BlockSpec((queries, HD), lambda h: (0, first + h)),
            whole((keys, HD)),
            whole((HD, keys)),
            whole((keys, 1)),
            whole((1, queries)),
            whole((queries, HD)),
            whole((queries, HD)),
        ],
        out_specs=[head, head, pl.BlockSpec((1, 1, queries), lambda h: (h, 0, 0))],
        out_shape=[
            jax.ShapeDtypeStruct((queries, width), LOW),
            jax.ShapeDtypeStruct((queries, width), LOW),
            jax.ShapeDtypeStruct((heads, 1, queries), FULL),
        ],
        scratch_shapes=[pltpu.VMEM((keys, queries), FULL)],
        compiler_params=pltpu.CompilerParams(vmem_limit_bytes=40 * MIB),
        cost_estimate=LIGHT,
    )(
        raw_query,
        key_value[:, :HD],
        key_value[:, HD:].T,
        key_segments[:, None],
        query_segments[None, :],
        cosine,
        sine,
    )


def attend_back_kernel(
    block, factor, rot_ref, grad_ref, mixed_ref, log_ref, key_ref, value_ref, ks_ref, qs_ref,
    cos_ref, sin_ref, query_out, key_out, value_out, bias, key_t_ref,
):
    @pl.when(pl.program_id(0) == 0)
    def _():
        mask_into(bias, ks_ref, qs_ref, block)
        key_t_ref[...] = key_ref[...].T
        key_out[...] = jnp.zeros_like(key_out)
        value_out[...] = jnp.zeros_like(value_out)

    queries = rot_ref.shape[0]
    for start in range(0, queries, block):
        rows, span = pl.ds(start, block), pl.ds(start, WINDOW + block)
        rot, grad = rot_ref[rows, :], grad_ref[rows, :]
        product = grad.astype(FULL) * mixed_ref[rows, :].astype(FULL)
        inner = jnp.sum(product.T, axis=0, keepdims=True)
        raw = by_rows(key_ref[span, :], rot)
        prob = jnp.exp2(raw * factor + (bias[span, rows] - log_ref[0, :, rows]))
        grad_prob = by_rows(value_ref[span, :], grad)
        grad_raw = (prob * (grad_prob - inner)).astype(LOW)
        value_out[span, :] += matmul(prob.astype(LOW), grad)
        key_out[span, :] += matmul(grad_raw, rot)
        back = matmul(key_t_ref[:, span], grad_raw).T * HD**-0.5
        query_out[rows, :] = turn(back, cos_ref[rows, :], -sin_ref[rows, :]).astype(LOW)


def attend_back(rot, grad, mixed, logs, key_value, key_segments, query_segments, cosine, sine):
    queries, width = rot.shape
    keys = key_value.shape[0]
    heads = width // HD
    block = min(256, queries)
    head = pl.BlockSpec((queries, HD), lambda h: (0, h))
    whole = lambda shape: pl.BlockSpec(shape, lambda h: (0,) * len(shape))
    return pl.pallas_call(
        functools.partial(attend_back_kernel, block, HD**-0.5 * LOG2E),
        grid=(heads,),
        in_specs=[
            head,
            head,
            head,
            pl.BlockSpec((1, 1, queries), lambda h: (h, 0, 0)),
            pl.BlockSpec((keys, HD), lambda h: (0, 0)),
            pl.BlockSpec((keys, HD), lambda h: (0, 1)),
            whole((keys, 1)),
            whole((1, queries)),
            whole((queries, HD)),
            whole((queries, HD)),
        ],
        out_specs=[head, whole((keys, HD)), whole((keys, HD))],
        out_shape=[
            jax.ShapeDtypeStruct((queries, width), LOW),
            jax.ShapeDtypeStruct((keys, HD), FULL),
            jax.ShapeDtypeStruct((keys, HD), FULL),
        ],
        scratch_shapes=[pltpu.VMEM((keys, queries), FULL), pltpu.VMEM((HD, keys), LOW)],
        compiler_params=pltpu.CompilerParams(vmem_limit_bytes=40 * MIB),
        cost_estimate=LIGHT,
    )(
        rot,
        grad,
        mixed,
        logs,
        key_value,
        key_value,
        key_segments[:, None],
        query_segments[None, :],
        cosine,
        sine,
    )


GELU_A = 0.7978845608028654
GELU_B = 0.044715


def hidden_kernel(count, *refs):
    normed_refs, cot_refs, pieces = refs[:2], refs[2:4], refs[4 : 4 + count]
    out_ref, weights_out, weights, sems = refs[4 + count :]
    step, steps = pl.program_id(0), pl.num_programs(0)
    me = lax.axis_index("tok")
    side, z, ring = (me // SIDE) % 2, me // RING, count // 2
    rows = weights.shape[0] // count

    def load(k):
        if count == 1:
            start = 0
        else:
            start = 2 * ((z - k // 2 + ring) % ring) + (side if k % 2 == 0 else 1 - side)
        return pltpu.make_async_copy(
            pieces[k], weights.at[pl.ds(pl.multiple_of(start * rows, 16), rows)], sems.at[k]
        )

    keep = pltpu.make_async_copy(weights, weights_out, sems.at[count])

    @pl.when(step == 0)
    def _():
        for k in range(count):
            load(k).start()
        for k in range(count):
            load(k).wait()
        keep.start()

    early = step < steps // 2
    normed = jnp.where(early, normed_refs[0][...], normed_refs[1][...])
    cotangent = jnp.where(early, cot_refs[0][...], cot_refs[1][...])
    columns = out_ref.shape[2]
    gate = matmul(normed, weights[:, :columns])
    up = matmul(normed, weights[:, columns : 2 * columns])
    grad_hidden = matmul(cotangent, weights[:, 2 * columns :])
    activation_grads(out_ref, gate, up, grad_hidden)

    @pl.when(step == steps - 1)
    def _():
        keep.wait()


def hidden_and_grads(normed, cotangent, pieces):
    half, width = normed[0].shape
    columns = pieces[0].shape[1] // 3
    rows = min(256, half)
    steps = half // rows
    count = len(pieces)
    if count >= 4 and pieces[0].shape[0] % 64 == 0:
        return hidden_by_depth(normed, cotangent, pieces)
    blocks = [
        pl.BlockSpec((rows, width), lambda i: (jnp.minimum(i, steps - 1), 0)),
        pl.BlockSpec((rows, width), lambda i: (jnp.maximum(i - steps, 0), 0)),
    ]
    anywhere = pl.BlockSpec(memory_space=pl.ANY)
    return pl.pallas_call(
        functools.partial(hidden_kernel, count),
        grid=(2 * steps,),
        in_specs=blocks * 2 + [anywhere] * count,
        out_specs=[pl.BlockSpec((3, rows, columns), lambda i: (0, i, 0)), anywhere],
        out_shape=[
            jax.ShapeDtypeStruct((3, 2 * half, columns), LOW),
            jax.ShapeDtypeStruct((width, 3 * columns), LOW),
        ],
        scratch_shapes=[
            pltpu.VMEM((width, 3 * columns), LOW),
            pltpu.SemaphoreType.DMA((count + 1,)),
        ],
        compiler_params=pltpu.CompilerParams(vmem_limit_bytes=48 * MIB),
        cost_estimate=LIGHT,
    )(*normed, *cotangent, *pieces)


def activation_grads(out_ref, gate, up, grad_hidden):
    square = gate * gate
    bent = jnp.tanh(gate * (GELU_A + GELU_A * GELU_B * square))
    half = 0.5 * (1.0 + bent)
    value = gate * half
    slope = half + 0.5 * gate * (1.0 - bent * bent) * (GELU_A + 3.0 * GELU_A * GELU_B * square)
    out_ref[0] = (grad_hidden * up * slope).astype(LOW)
    out_ref[1] = (grad_hidden * value).astype(LOW)
    out_ref[2] = (value * up).astype(LOW)


def depth_kernel(ring, first, count, last, *refs):
    normed_refs, cot_refs, pieces, refs = refs[:2], refs[2:4], refs[4 : 4 + count], refs[4 + count :]
    if last:
        partial_ref, _, out_ref, weights_out, weights, sems = refs
    else:
        out_ref, weights_out, weights, sems = refs
    step, steps = pl.program_id(0), pl.num_programs(0)
    me = lax.axis_index("tok")
    side, z = (me // SIDE) % 2, me // RING
    rows = weights.shape[0] // count
    wide = 2 * rows

    def chunk(k):
        return (z - first - k + 2 * ring) % ring

    def load(k):
        start = wide * (k // 2) + rows * (side if k % 2 == 0 else 1 - side)
        return pltpu.make_async_copy(
            pieces[k], weights.at[pl.ds(pl.multiple_of(start, 16), rows)], sems.at[k]
        )

    def keep(k):
        return pltpu.make_async_copy(
            weights.at[pl.ds(wide * k, wide)],
            weights_out.at[pl.ds(pl.multiple_of(chunk(k) * wide, 16), wide)],
            sems.at[count + k],
        )

    @pl.when(step == 0)
    def _():
        for k in range(count):
            load(k).start()
        for k in range(count):
            load(k).wait()
        for k in range(count // 2):
            keep(k).start()

    early = step < steps // 2

    def columns_of(pair):
        parts = []
        for k in range(count // 2):
            lanes = pl.ds(pl.multiple_of(chunk(k) * wide, HD), wide)
            parts.append(jnp.where(early, pair[0][:, lanes], pair[1][:, lanes]))
        return parts[0] if len(parts) == 1 else jnp.concatenate(parts, axis=1)

    normed, cotangent = columns_of(normed_refs), columns_of(cot_refs)
    columns = out_ref.shape[2]
    products = [
        matmul(left, weights[:, k * columns : (k + 1) * columns])
        for k, left in enumerate((normed, normed, cotangent))
    ]
    if last:
        activation_grads(out_ref, *(products[k] + partial_ref[k].astype(FULL) for k in range(3)))
    else:
        for k in range(3):
            out_ref[k] = products[k].astype(LOW)

    @pl.when(step == steps - 1)
    def _():
        for k in range(count // 2):
            keep(k).wait()


def hidden_by_depth(normed, cotangent, pieces):
    half, width = normed[0].shape
    columns = pieces[0].shape[1] // 3
    rows = min(256, half)
    steps = half // rows
    ring = len(pieces) // 2
    deep = width // ring
    blocks = [
        pl.BlockSpec((rows, width), lambda i: (jnp.minimum(i, steps - 1), 0)),
        pl.BlockSpec((rows, width), lambda i: (jnp.maximum(i - steps, 0), 0)),
    ]
    anywhere = pl.BlockSpec(memory_space=pl.ANY)
    block = pl.BlockSpec((3, rows, columns), lambda i: (0, i, 0))
    weights_shape = jax.ShapeDtypeStruct((width, 3 * columns), LOW)

    def part(first, given, more):
        count = len(given)
        return pl.pallas_call(
            functools.partial(depth_kernel, ring, first, count, len(more) > 0),
            grid=(2 * steps,),
            in_specs=blocks * 2 + [anywhere] * count + [block, anywhere][: len(more)],
            out_specs=[block, anywhere],
            out_shape=[jax.ShapeDtypeStruct((3, 2 * half, columns), LOW), weights_shape],
            input_output_aliases={5 + count: 1} if more else {},
            scratch_shapes=[
                pltpu.VMEM((deep * (count // 2), 3 * columns), LOW),
                pltpu.SemaphoreType.DMA((count + count // 2,)),
            ],
            compiler_params=pltpu.CompilerParams(vmem_limit_bytes=48 * MIB),
            cost_estimate=LIGHT,
        )(*normed, *cotangent, *given, *more)

    partial = part(0, pieces[:-2], [])
    return part(ring - 1, pieces[-2:], partial)


def project_sum_kernel(count, array_ref, *refs):
    weight_refs, out_refs = refs[:count], refs[count : count + 2]
    away, arrived, send_sem, recv_sem = refs[count + 2 :]
    step = pl.program_id(0)
    me = lax.axis_index("tok")
    mate = me + 1 - 2 * (me % 2)

    def crossing(block):
        return pltpu.make_async_remote_copy(
            src_ref=away.at[block],
            dst_ref=arrived.at[block],
            send_sem=send_sem.at[block],
            recv_sem=recv_sem.at[block],
            device_id=(mate,),
            device_id_type=pl.DeviceIdType.MESH,
        )

    @pl.when(step == 0)
    def _():
        barrier = pltpu.get_barrier_semaphore()
        pl.semaphore_signal(
            barrier, inc=1, device_id=(mate,), device_id_type=pl.DeviceIdType.MESH
        )
        pl.semaphore_wait(barrier, 1)

    total = by_rows(array_ref[0], weight_refs[0][...])
    for k in range(1, count):
        total += by_rows(array_ref[k], weight_refs[k][...])
    for block in range(2):

        @pl.when(step == block)
        def _():
            away[block] = total.astype(LOW)
            crossing(block).start()

        @pl.when(step == 2 + block)
        def _():
            crossing(block).wait()
            out_refs[block][...] = (total + arrived[block].astype(FULL)).astype(LOW)


def project_sum(array, pack, first, count, identity, marks=()):
    array = after(array, *jax.tree.leaves(marks))
    tokens, columns = array.shape[1:]
    width = pack.shape[0]
    rows = tokens // 4
    whole = pl.BlockSpec((rows, width), lambda i: (0, 0))
    return pl.pallas_call(
        functools.partial(project_sum_kernel, count),
        grid=(4,),
        in_specs=[pl.BlockSpec((count, rows, columns), lambda i: (first // count, (i + 2) % 4, 0))]
        + [
            pl.BlockSpec(
                (width, columns), lambda i, k=k: (0, first + k), pipeline_mode=pl.Buffered(1)
            )
            for k in range(count)
        ],
        out_specs=[whole] * 2,
        out_shape=[jax.ShapeDtypeStruct((rows, width), LOW)] * 2,
        scratch_shapes=[
            pltpu.VMEM((2, rows, width), LOW),
            pltpu.VMEM((2, rows, width), LOW),
            pltpu.SemaphoreType.DMA((2,)),
            pltpu.SemaphoreType.DMA((2,)),
        ],
        compiler_params=pltpu.CompilerParams(
            collective_id=identity, has_side_effects=True, vmem_limit_bytes=44 * MIB
        ),
        cost_estimate=LIGHT,
    )(array, *([pack] * count))


def outer_kernel(chunk_ref, *refs):
    normed_refs, cot_refs, right_ref, give_ref, keep_ref, total = refs[:2], refs[2:4], *refs[4:]
    step, steps = pl.program_id(0), pl.num_programs(0)
    early = step < steps // 2
    normed = jnp.where(early, normed_refs[0][...], normed_refs[1][...])
    cotangent = jnp.where(early, cot_refs[0][...], cot_refs[1][...])
    columns = right_ref.shape[2]

    @pl.when(step == 0)
    def _():
        total[...] = jnp.zeros_like(total)

    for k, left in enumerate((normed, normed, cotangent)):
        total[:, k * columns : (k + 1) * columns] += outer_sum(left, right_ref[k])

    @pl.when(step == steps - 1)
    def _():
        rows = keep_ref.shape[0]
        side = (lax.axis_index("tok") // SIDE) % 2
        for ref, place_of in ((give_ref, 1 - side), (keep_ref, side)):
            ref[...] = total[pl.ds(pl.multiple_of(place_of * rows, 16), rows), :].astype(LOW)


def outer_products(normed, cotangent, array, chunk, rows):
    tokens, columns = array.shape[1:]
    deep = min(512, tokens // 2)
    steps = tokens // 2 // deep
    lefts = [
        pl.BlockSpec((deep, rows), lambda i, chunk_ref: (jnp.minimum(i, steps - 1), chunk_ref[0])),
        pl.BlockSpec((deep, rows), lambda i, chunk_ref: (jnp.maximum(i - steps, 0), chunk_ref[0])),
    ]
    return pl.pallas_call(
        outer_kernel,
        grid_spec=pltpu.PrefetchScalarGridSpec(
            num_scalar_prefetch=1,
            grid=(2 * steps,),
            in_specs=lefts * 2
            + [pl.BlockSpec((3, deep, columns), lambda i, chunk_ref: (0, i, 0))],
            out_specs=[pl.BlockSpec((rows // 2, 3 * columns), lambda i, chunk_ref: (0, 0))] * 2,
            scratch_shapes=[pltpu.VMEM((rows, 3 * columns), FULL)],
        ),
        out_shape=[jax.ShapeDtypeStruct((rows // 2, 3 * columns), LOW)] * 2,
        compiler_params=pltpu.CompilerParams(vmem_limit_bytes=40 * MIB),
        cost_estimate=LIGHT,
    )(chunk[None].astype(jnp.int32), *normed, *cotangent, array)


def join_kernel(count, epsilon, *refs):
    inputs_ref, gain_ref, weight_ref = refs[:3]
    parts, (middle_ref, normed_ref, inverse_ref) = refs[3 : 3 + count], refs[3 + count :]
    total, start = inputs_ref[...].astype(FULL), 0
    for part in parts:
        columns = part.shape[1]
        total += by_rows(part[...], weight_ref[:, start : start + columns])
        start += columns
    inverse = lax.rsqrt(jnp.mean(total * total, axis=1, keepdims=True) + epsilon)
    middle_ref[...] = total
    inverse_ref[...] = jnp.broadcast_to(inverse, inverse_ref.shape)
    normed_ref[...] = (total * inverse * gain_ref[...]).astype(LOW)


def join(tokens, gain, weight, parts):
    count, width = tokens.shape
    rows = min(256, count)
    block = lambda columns: pl.BlockSpec((rows, columns), lambda i: (i, 0))
    return pl.pallas_call(
        functools.partial(join_kernel, len(parts), EPSILON),
        grid=(count // rows,),
        in_specs=[
            block(width),
            pl.BlockSpec((1, width), lambda i: (0, 0)),
            pl.BlockSpec((width, width), lambda i: (0, 0), pipeline_mode=pl.Buffered(1)),
        ]
        + [block(part.shape[1]) for part in parts],
        out_specs=[block(width), block(width), block(HD)],
        out_shape=[
            jax.ShapeDtypeStruct((count, width), FULL),
            jax.ShapeDtypeStruct((count, width), LOW),
            jax.ShapeDtypeStruct((count, HD), FULL),
        ],
        compiler_params=pltpu.CompilerParams(vmem_limit_bytes=40 * MIB),
        cost_estimate=LIGHT,
    )(tokens, gain[None], weight, *parts)


def branch_kernel(
    group_ref, near_ref, cot_ref, middle_ref, inverse_ref, gain_ref, weight_ref,
    grad_ref, branch_ref, mixed_ref, scaled_ref,
):
    grad = group_ref[...].astype(FULL) + near_ref[...].astype(FULL)
    middle, inverse = middle_ref[...], inverse_ref[:, :1]
    normal = middle * inverse
    scaled_ref[...] = (grad * normal).astype(LOW)
    scaled = grad * gain_ref[...]
    total = (
        cot_ref[...].astype(FULL)
        + inverse * scaled
        - normal * (inverse * jnp.mean(scaled * normal, axis=1, keepdims=True))
    )
    grad_ref[...] = total
    branch = total.astype(LOW)
    branch_ref[...] = branch
    mixed_ref[...] = matmul(branch, weight_ref[...]).astype(LOW)


def branch_back(group, near, cotangent, middle, inverse, gain, weight):
    count, width = middle.shape
    rows = min(256, count)
    block = lambda columns: pl.BlockSpec((rows, columns), lambda i: (i, 0))
    return pl.pallas_call(
        branch_kernel,
        grid=(count // rows,),
        in_specs=[
            block(width),
            block(width),
            block(width),
            block(width),
            block(HD),
            pl.BlockSpec((1, width), lambda i: (0, 0)),
            pl.BlockSpec((width, width), lambda i: (0, 0), pipeline_mode=pl.Buffered(1)),
        ],
        out_specs=[block(width)] * 4,
        out_shape=[
            jax.ShapeDtypeStruct((count, width), FULL),
            jax.ShapeDtypeStruct((count, width), LOW),
            jax.ShapeDtypeStruct((count, width), LOW),
            jax.ShapeDtypeStruct((count, width), LOW),
        ],
        compiler_params=pltpu.CompilerParams(vmem_limit_bytes=48 * MIB),
        cost_estimate=LIGHT,
    )(group, near, cotangent, middle, inverse, gain[None], weight)


def on_device(
    tokens, cotangent, attn_gain, ffn_gain, w_query, w_key, w_value, w_out, w_gate, w_up, w_down,
    segments, positions,
):
    token_count, width = tokens.shape
    own_rows, hidden_width = w_gate.shape
    slice_width = hidden_width // GROUP
    heads_width = w_query.shape[1]
    tail_rows = min(token_count, WINDOW)
    hop_count = WINDOW // tail_rows
    device = lax.axis_index("tok")
    inputs = tokens.astype(FULL)

    frequency = 10000.0 ** (-jnp.arange(HD // 2, dtype=FULL) * 2.0 / HD)
    angles = positions.astype(FULL)[:, None] * frequency[None, :]
    cosine = jnp.concatenate([jnp.cos(angles)] * 2, axis=1)
    sine_half = jnp.sin(angles)
    sine = jnp.concatenate([-sine_half, sine_half], axis=1)
    padded_segments = jnp.concatenate([jnp.full((WINDOW,), -1, jnp.int32), segments])
    key_segments = lax.dynamic_slice_in_dim(
        padded_segments, device * token_count, WINDOW + token_count
    )
    query_segments = lax.dynamic_slice_in_dim(segments, device * token_count, token_count)

    attn_pack = jnp.concatenate(
        [
            w_query,
            w_key,
            w_value,
            jnp.pad(
                jnp.stack([attn_gain, ffn_gain], axis=1), ((0, 0), (0, HD - 2))
            ),
        ],
        axis=1,
    )
    edge = heads_width + 2 * HD
    def sliced(weight):
        return weight.reshape(own_rows, GROUP, slice_width).transpose(1, 0, 2)

    ffn_pack = jnp.concatenate([sliced(w_gate), sliced(w_up), sliced(w_down)], axis=2)
    attn_all, ffn_rows = gather(attn_pack, ffn_pack)
    out_w = lax.all_gather(w_out, "tok", axis=0, tiled=True)
    query_w, kv_w = attn_all[:, :heads_width], attn_all[:, heads_width:edge]
    gains = attn_all[:, edge : edge + 2].astype(FULL)
    gain_one, gain_two = gains[:, 0], gains[:, 1]

    inverse_one = lax.rsqrt(jnp.mean(inputs * inputs, axis=-1, keepdims=True) + EPSILON)
    normed = (inputs * inverse_one * gain_one).astype(LOW)
    kv = matmul(normed, kv_w)

    def turned(values, sine_signed):
        half = HD // 2
        rolled = jnp.concatenate([values[:, half:], values[:, :half]], axis=1)
        return values * cosine + rolled * sine_signed

    key_value = jnp.concatenate([turned(kv[:, :HD], sine), kv[:, HD:]], axis=1).astype(LOW)
    received = [passed_along(key_value, hop) for hop in range(hop_count, 0, -1)]
    all_keys = jnp.concatenate(received + [key_value], axis=0)
    raw_query = matmul(normed, query_w)
    heads = heads_width // HD
    given = (all_keys, key_segments, query_segments, cosine, sine)
    early = attend(raw_query, *given, 0, heads // 2)
    pieces, steps = spread(ffn_rows, (early[1],))
    cot_group = rows_to_group(after(cotangent, attn_all), steps[1])
    late = attend(
        after(raw_query, early[1]), *given, heads // 2, heads - heads // 2
    )
    rot, mixed = (jnp.concatenate([early[k], late[k]], axis=1) for k in range(2))
    logs = jnp.concatenate([early[2], late[2]], axis=0)
    middle, normed_two, inverse_two = join(tokens, gain_two, out_w, (early[1], late[1]))

    normed_group = rows_to_group(after(normed_two, *steps[1]), steps[2])
    hidden_pack, ffn_w = hidden_and_grads(normed_group, cot_group, pieces)
    reduction = Reduction(normed_group, cot_group, hidden_pack)
    pairs_done = reduction.multiply(0)
    reduction.begin()
    pairs_done = reduction.multiply(1, pairs_done)
    own_sum, near_sum = project_sum(hidden_pack, ffn_w, 0, 2, 2, pairs_done)
    near_sent = flip(near_sum, NEAR)
    marks = reduction.advance(0, near_sum)
    pairs_done = reduction.multiply(2, marks)
    pairs_done = reduction.multiply(3, pairs_done)
    marks = reduction.advance(1, pairs_done)
    output_own, output_near = project_sum(hidden_pack, ffn_w, 2, 1, 3, marks)
    output_near = flip(after(output_near, near_sent), NEAR)

    grad_middle, branch, grad_mixed, gain_two_parts = branch_back(
        own_sum, after(near_sent, output_own), cotangent, middle, inverse_two, gain_two, out_w
    )
    grad_out_w = outer_sum(branch, mixed).astype(LOW)
    out_sum = lax.psum_scatter(grad_out_w, "tok", scatter_dimension=0, tiled=True).astype(FULL)
    marks = reduction.advance(2, grad_mixed)
    query_low, key_grads, value_grads = attend_back(
        rot, after(grad_mixed, *marks), mixed, logs, all_keys, key_segments, query_segments, cosine, sine
    )
    output = (
        middle + output_own.astype(FULL) + after(output_near, query_low).astype(FULL)
    ).astype(LOW)
    grads = jnp.concatenate([key_grads * HD**-0.5, value_grads], axis=1)
    shares = grads[WINDOW:]
    for hop in range(1, hop_count + 1):
        first_row = (hop_count - hop) * tail_rows
        returned = passed_along(grads[first_row : first_row + tail_rows].astype(LOW), -hop)
        shares = shares.at[token_count - tail_rows :].add(returned.astype(FULL))
    kv_low = jnp.concatenate([turned(shares[:, :HD], -sine), shares[:, HD:]], axis=1).astype(LOW)
    grad_query_w = outer_sum(normed, query_low).astype(LOW)
    grad_kv_w = outer_sum(normed, kv_low).astype(LOW)
    grad_normed = by_rows(query_low, query_w) + by_rows(kv_low, kv_w)
    scaled_one = grad_normed * gain_one
    grad_inputs = inverse_one * scaled_one - inputs * inverse_one**3 * jnp.mean(
        scaled_one * inputs, axis=-1, keepdims=True
    )
    grad_tokens = (grad_middle + grad_inputs).astype(LOW)
    lane = lax.broadcasted_iota(jnp.int32, (token_count, HD), 1)
    grad_gains = (
        outer_sum((grad_normed * inputs * inverse_one).astype(LOW), (lane == 0).astype(LOW))
        + outer_sum(gain_two_parts, (lane == 1).astype(LOW))
    ).astype(LOW)
    reduction.advance(3, grad_query_w)
    attn_sum, ffn_parts = scatter(
        [grad_query_w, grad_kv_w, grad_gains], reduction.result()
    )

    def joined(parts):
        return parts.transpose(1, 0, 2).reshape(own_rows, hidden_width).astype(FULL)

    return (
        output,
        grad_tokens,
        attn_sum[:, edge],
        attn_sum[:, edge + 1],
        attn_sum[:, :heads_width],
        attn_sum[:, heads_width : heads_width + HD],
        attn_sum[:, heads_width + HD : edge],
        out_sum,
        joined(ffn_parts[:, :, :slice_width]),
        joined(ffn_parts[:, :, slice_width : 2 * slice_width]),
        joined(ffn_parts[:, :, 2 * slice_width :]),
    )


def solution(mesh):
    rows, flat = P("tok", None), P("tok")
    return jax.shard_map(
        on_device,
        mesh=mesh,
        in_specs=(rows, rows, flat, flat, rows, rows, rows, rows, rows, rows, rows, P(), flat),
        out_specs=(rows, rows, flat, flat, rows, rows, rows, rows, rows, rows, rows),
        check_vma=False,
    )
```

```python
import functools

import jax
import jax.numpy as jnp
from jax import lax
from jax.experimental import pallas as pl
from jax.experimental.pallas import tpu as pltpu
from jax.sharding import PartitionSpec as P

HQ = 12
HD = 128
WINDOW = 1024
EPSILON = 1e-06

CORE, NEAR, SIDE, GROUP, RING = 1, 2, 4, 4, 8
LONGEST_RING = 8
LOG2E = 1.4426950408889634
LOW = jnp.bfloat16
FULL = jnp.float32
MIB = 1024 * 1024
LIGHT = pl.CostEstimate(flops=1024, bytes_accessed=1024, transcendentals=0)


def flip(array, bit):
    size = lax.axis_size("tok")
    return lax.ppermute(array, "tok", [(i, i ^ bit) for i in range(size)])


def around(array):
    size = lax.axis_size("tok")
    return lax.ppermute(array, "tok", [(i, (i + RING) % size) for i in range(size)])


def passed_along(array, by):
    size = lax.axis_size("tok")
    pairs = [(i, i + by) for i in range(size) if 0 <= i + by < size]
    return lax.ppermute(array, "tok", pairs)


def rms_norm(values, scales):
    return values * lax.rsqrt(jnp.mean(values * values, axis=-1, keepdims=True) + EPSILON) * scales


def outer_sum(left_side, right_side):
    return lax.dot_general(
        left_side, right_side, (((0,), (0,)), ((), ())), preferred_element_type=FULL
    )


def by_rows(left_side, right_side):
    return lax.dot_general(
        left_side, right_side, (((1,), (1,)), ((), ())), preferred_element_type=FULL
    )


def matmul(left_side, right_side):
    return jnp.dot(left_side, right_side, preferred_element_type=FULL)


def pick(array, index):
    return lax.dynamic_index_in_dim(array, index, 0, keepdims=False)


def place():
    device = lax.axis_index("tok")
    return device, device % 2, (device // 2) % 2, (device // 4) % 2, device // RING


def rows_to_group(array, marks=()):
    two = jnp.concatenate([array, after(flip(array, NEAR), *marks)], axis=0)
    return two, flip(two, CORE)


def slices_to_group(parts):
    _, core, near, _, _ = place()
    rows, columns = parts.shape[1:]
    mine = lax.dynamic_slice_in_dim(parts, 2 * near, 2, 0)
    theirs = flip(lax.dynamic_slice_in_dim(parts, 2 * (1 - near), 2, 0), NEAR)
    here = jnp.stack([pick(mine, core), pick(theirs, core)])
    away = flip(jnp.stack([pick(mine, 1 - core), pick(theirs, 1 - core)]), CORE)
    by_core = jnp.where(core == 0, jnp.stack([here, away], 1), jnp.stack([away, here], 1))
    by_near = jnp.where(near == 0, by_core, by_core[::-1])
    return by_near.reshape(4 * rows, columns)


def slices_from_group(block):
    _, core, near, _, _ = place()
    rows, columns = block.shape[0] // 4, block.shape[1]
    parts = block.astype(LOW).reshape(2, 2, rows, columns)
    mine, theirs = pick(parts, near), flip(pick(parts, 1 - near), NEAR)
    here = jnp.stack([pick(mine, core), pick(theirs, core)])
    away = flip(jnp.stack([pick(mine, 1 - core), pick(theirs, 1 - core)]), CORE)
    by_core = jnp.where(core == 0, jnp.stack([here, away], 1), jnp.stack([away, here], 1))
    by_near = jnp.where(near == 0, by_core, by_core[::-1])
    return by_near.reshape(4, rows, columns)


def gather_kernel(
    ring, bands, attn_ref, ffn_ref, attn_out, ffn_out, local_sem, send_sem, recv_sem
):
    size = ring * RING
    me = lax.axis_index("tok")
    core, near, side, z = me % 2, (me // 2) % 2, (me // 4) % 2, me // RING
    core_mate, near_mate, side_mate = me + 1 - 2 * core, me + 2 - 4 * near, me + 4 - 8 * side
    far_mate = near_mate + 1 - 2 * core
    up, down = (me + RING) % size, (me + size - RING) % size

    barrier = pltpu.get_barrier_semaphore()
    partners = (core_mate, near_mate, side_mate, far_mate, up, down)
    for partner in partners:
        pl.semaphore_signal(
            barrier, inc=1, device_id=(partner,), device_id_type=pl.DeviceIdType.MESH
        )
    pl.semaphore_wait(barrier, len(partners))

    own = pltpu.make_async_copy(attn_ref, attn_out.at[z, side, near, core], local_sem.at[0])
    own.start()
    own_slice = pltpu.make_async_copy(
        ffn_ref.at[2 * near + core], ffn_out.at[2 * near + core], local_sem.at[1]
    )
    own_slice.start()

    copies = []

    def send(src, dst, to):
        index = len(copies)
        copy = pltpu.make_async_remote_copy(
            src_ref=src,
            dst_ref=dst,
            send_sem=send_sem.at[index],
            recv_sem=recv_sem.at[index],
            device_id=(to,),
            device_id_type=pl.DeviceIdType.MESH,
        )
        copy.start()
        copies.append(copy)
        return copy

    def forward(ref, to):
        return send(ref, ref, to)

    def chunk_of(step):
        return (z - step + ring) % ring

    def piece(step, band):
        return attn_out.at[chunk_of(step), side, near, core, bands[band]]

    hops, first, second, last = {}, {}, {}, {}
    over = []

    def finish(step):
        first[0, step].wait_recv()
        second[0, step] = forward(attn_out.at[chunk_of(step), side, :, core, bands[0]], side_mate)
        first[1, step].wait_recv()
        second[1, step] = forward(attn_out.at[chunk_of(step), :, near, core, bands[1]], near_mate)

    def hand_over(step):
        second[0, step].wait_recv()
        second[1, step].wait_recv()
        over.append(forward(attn_out.at[chunk_of(step), :, :, core], core_mate))

    for step in range(ring):
        for band in (0, 1):
            if step > 0:
                hops[band, step].wait_recv()
            source = attn_ref.at[bands[band]] if step == 0 else piece(step, band)
            if step < ring - 1:
                hops[band, step + 1] = send(source, piece(step, band), up)
            mate = near_mate if band == 0 else side_mate
            first[band, step] = send(source, piece(step, band), mate)
        if step == 0:
            begun = send(attn_ref.at[bands[2]], piece(0, 2), near_mate)
            slices = [
                send(ffn_ref.at[index], ffn_out.at[2 * near + core], mate)
                for mate, index in (
                    (near_mate, 2 * (1 - near) + core),
                    (far_mate, 2 * (1 - near) + 1 - core),
                    (core_mate, 2 * near + 1 - core),
                )
            ]
            own.wait()
            begun.wait_recv()
            last[0] = forward(attn_out.at[z, side, :, core, bands[2]], side_mate)
        else:
            last[step - 1].wait_recv()
            last[step] = forward(attn_out.at[chunk_of(step - 1), :, :, core, bands[2]], up)
            finish(step - 1)
        if step >= 2:
            hand_over(step - 2)
    finish(ring - 1)
    hand_over(ring - 2)
    last[ring - 1].wait_recv()
    hand_over(ring - 1)
    own_slice.wait()
    for copy in slices + over:
        copy.wait_recv()
    for copy in copies:
        copy.wait_send()


def gather(attn_pack, ffn_pack):
    size = lax.axis_size("tok")
    ring = size // RING
    rows, columns = attn_pack.shape
    if ring > LONGEST_RING or ring < 2 or rows % 48:
        return lax.all_gather(attn_pack, "tok", axis=0, tiled=True), slices_to_group(ffn_pack)
    third = rows // 3
    bands = [pl.ds(third * band, third) for band in range(3)]
    count = 3 + 2 * (ring - 1) + 2 * ring + 2 * ring + 1 + ring + ring
    anywhere = pl.BlockSpec(memory_space=pl.ANY)
    attn_all, ffn_rows = pl.pallas_call(
        functools.partial(gather_kernel, ring, bands),
        in_specs=[anywhere] * 2,
        out_specs=[anywhere] * 2,
        out_shape=[
            jax.ShapeDtypeStruct((ring, 2, 2, 2, rows, columns), attn_pack.dtype),
            jax.ShapeDtypeStruct(ffn_pack.shape, ffn_pack.dtype),
        ],
        scratch_shapes=[
            pltpu.SemaphoreType.DMA((2,)),
            pltpu.SemaphoreType.DMA((count,)),
            pltpu.SemaphoreType.DMA((count,)),
        ],
        compiler_params=pltpu.CompilerParams(collective_id=0, has_side_effects=True),
    )(attn_pack, ffn_pack)
    return attn_all.reshape(size * rows, columns), ffn_rows.reshape(GROUP * rows, -1)


def scatter_kernel(
    ring, bands, edges, *refs
):
    count = len(edges) - 1
    grad_refs, ffn_ref, attn_out, ffn_out = refs[:count], refs[count], refs[count + 1], refs[count + 2]
    pack, core_in, a_side, a_near, a_ring, b_near, b_side, b_ring, c_ring, c_side, c_near = refs[
        count + 3 : count + 14
    ]
    local_sem, send_sem, recv_sem = refs[count + 14 :]
    size = ring * RING
    me = lax.axis_index("tok")
    core, near, side, z = me % 2, (me // 2) % 2, (me // 4) % 2, me // RING
    core_mate, near_mate, side_mate = me + 1 - 2 * core, me + 2 - 4 * near, me + 4 - 8 * side
    far_mate = near_mate + 1 - 2 * core
    up, down = (me + RING) % size, (me + size - RING) % size

    def chunk_of(step):
        return (z - 1 - step + 2 * ring) % ring

    loads = []
    for step in range(ring):
        row = []
        for k in range(count):
            load = pltpu.make_async_copy(
                grad_refs[k].at[chunk_of(step)],
                pack.at[chunk_of(step), :, :, :, :, pl.ds(edges[k], edges[k + 1] - edges[k])],
                local_sem.at[step * count + k],
            )
            load.start()
            row.append(load)
        loads.append(row)
    own_slice = pltpu.make_async_copy(
        ffn_ref.at[2 * near + core], ffn_out.at[2 * near + core], local_sem.at[ring * count]
    )
    own_slice.start()

    barrier = pltpu.get_barrier_semaphore()
    partners = (core_mate, near_mate, side_mate, far_mate, up, down)
    for partner in partners:
        pl.semaphore_signal(
            barrier, inc=1, device_id=(partner,), device_id_type=pl.DeviceIdType.MESH
        )
    pl.semaphore_wait(barrier, len(partners))

    copies = []

    def send(src, dst, to):
        index = len(copies)
        copy = pltpu.make_async_remote_copy(
            src_ref=src,
            dst_ref=dst,
            send_sem=send_sem.at[index],
            recv_sem=recv_sem.at[index],
            device_id=(to,),
            device_id_type=pl.DeviceIdType.MESH,
        )
        copy.start()
        copies.append(copy)
        return copy

    def add(held, arrived):
        held[...] = (held[...].astype(FULL) + arrived[...].astype(FULL)).astype(LOW)

    def part(step, y, x, band):
        return pack.at[chunk_of(step), y, x, core, bands[band]]

    def own(step, band):
        return part(step, side, near, band)

    across, first, second, hops = {}, {}, {}, {}

    def begin(step):
        chunk = chunk_of(step)
        across[step].wait_recv()

        def one(k, _):
            add(pack.at[chunk, k // 2, k % 2, core], core_in.at[chunk, k // 2, k % 2])
            return 0

        lax.fori_loop(0, 4, one, 0)
        first[0, step] = send(
            pack.at[chunk, 1 - side, :, core, bands[0]], a_side.at[step], side_mate
        )
        first[1, step] = send(
            pack.at[chunk, :, 1 - near, core, bands[1]], b_near.at[step], near_mate
        )
        if step > 0:
            hops[2, step].wait_recv()
            for k in range(4):
                add(part(step, k // 2, k % 2, 2), c_ring.at[step - 1, k // 2, k % 2])
        if step < ring - 1:
            hops[2, step + 1] = send(
                pack.at[chunk, :, :, core, bands[2]], c_ring.at[step], up
            )

    def middle(step):
        first[0, step].wait_recv()
        for x in range(2):
            add(part(step, side, x, 0), a_side.at[step, x])
        second[0, step] = send(part(step, side, 1 - near, 0), a_near.at[step], near_mate)
        first[1, step].wait_recv()
        for y in range(2):
            add(part(step, y, near, 1), b_near.at[step, y])
        second[1, step] = send(part(step, 1 - side, near, 1), b_side.at[step], side_mate)

    def end(step):
        for band, arrived, passing in ((0, a_near, a_ring), (1, b_side, b_ring)):
            second[band, step].wait_recv()
            add(own(step, band), arrived.at[step])
            if step > 0:
                hops[band, step].wait_recv()
                add(own(step, band), passing.at[step - 1])
            if step < ring - 1:
                hops[band, step + 1] = send(own(step, band), passing.at[step], up)

    for step in range(ring):
        for load in loads[step]:
            load.wait()
        across[step] = send(
            pack.at[chunk_of(step), :, :, 1 - core], core_in.at[chunk_of(step)], core_mate
        )
    slices = []
    for step in range(ring + 2):
        if step < ring:
            begin(step)
        if step == 0:
            slices += [
                send(ffn_ref.at[index], ffn_out.at[2 * near + core], mate)
                for mate, index in (
                    (near_mate, 2 * (1 - near) + core),
                    (far_mate, 2 * (1 - near) + 1 - core),
                    (core_mate, 2 * near + 1 - core),
                )
            ]
        if 1 <= step <= ring:
            middle(step - 1)
        if step == ring:
            last = ring - 1
            to_side = send(pack.at[z, 1 - side, :, core, bands[2]], c_side, side_mate)
        if step >= 2:
            end(step - 2)
        if step == ring:
            to_side.wait_recv()
            for x in range(2):
                add(part(last, side, x, 2), c_side.at[x])
            to_near = send(part(last, side, 1 - near, 2), c_near, near_mate)
    to_near.wait_recv()
    add(own(last, 2), c_near)
    attn_out[...] = pack[z, side, near, core].astype(FULL)
    own_slice.wait()
    for copy in slices:
        copy.wait_recv()
    for copy in copies:
        copy.wait_send()


def scatter(grads, ffn_sum):
    size = lax.axis_size("tok")
    ring = size // RING
    rows = grads[0].shape[0] // size
    if ring > LONGEST_RING or ring < 2 or rows % 48:
        joined = jnp.concatenate(grads, axis=1).astype(FULL)
        return (
            lax.psum_scatter(joined, "tok", scatter_dimension=0, tiled=True),
            slices_from_group(ffn_sum),
        )
    third = rows // 3
    bands = [pl.ds(third * band, third) for band in range(3)]
    edges = [0]
    for grad in grads:
        edges.append(edges[-1] + grad.shape[1])
    columns = edges[-1]
    count = ring + 2 * ring + (ring - 1) + 3 + 2 * ring + 1 + 2 * (ring - 1) + 1
    anywhere = pl.BlockSpec(memory_space=pl.ANY)
    band = (third, columns)
    low = lambda *shape: pltpu.VMEM((*shape, *band), LOW)
    return pl.pallas_call(
        functools.partial(scatter_kernel, ring, bands, edges),
        in_specs=[anywhere] * (len(grads) + 1),
        out_specs=[pl.BlockSpec(memory_space=pltpu.VMEM), anywhere],
        out_shape=[
            jax.ShapeDtypeStruct((rows, columns), FULL),
            jax.ShapeDtypeStruct((GROUP, rows, ffn_sum.shape[1]), LOW),
        ],
        scratch_shapes=[
            pltpu.VMEM((ring, 2, 2, 2, rows, columns), LOW),
            pltpu.VMEM((ring, 2, 2, rows, columns), LOW),
            low(ring, 2),
            low(ring),
            low(ring - 1),
            low(ring, 2),
            low(ring),
            low(ring - 1),
            low(ring - 1, 2, 2),
            low(2),
            low(),
            pltpu.SemaphoreType.DMA((ring * len(grads) + 1,)),
            pltpu.SemaphoreType.DMA((count,)),
            pltpu.SemaphoreType.DMA((count,)),
        ],
        compiler_params=pltpu.CompilerParams(
            collective_id=1, has_side_effects=True, vmem_limit_bytes=44 * MIB
        ),
    )(
        *[grad.reshape(ring, 2, 2, 2, rows, -1) for grad in grads],
        ffn_sum.astype(LOW).reshape(GROUP, rows, -1),
    )


def after(value, *marks):
    return lax.optimization_barrier((value, *marks))[0]


def groups_of(stride):
    size = lax.axis_size("tok")
    return [[s + stride * k for k in range(size // stride)] for s in range(stride)]


def spread(block, marks):
    size = lax.axis_size("tok")
    ring = size // RING
    if ring > LONGEST_RING:
        gathered = lax.all_gather(
            block, "tok", axis=0, tiled=True, axis_index_groups=groups_of(GROUP)
        )
        return [gathered], [()] * 3
    own, crossed = [block], []
    for step in range(ring):
        crossed.append(flip(own[-1], SIDE))
        if step < ring - 1:
            arrived = around(own[-1])
            if step == 0:
                arrived, crossed[0] = lax.optimization_barrier((arrived, crossed[0], *marks))[:2]
            own.append(arrived)
    pieces = [piece for pair in zip(own, crossed) for piece in pair]
    return pieces, [(*own[step + 1 : step + 2], crossed[step]) for step in range(ring)]


class Reduction:
    def __init__(self, normed, cotangent, array):
        self.given = (normed, cotangent, array)
        self.size = lax.axis_size("tok")
        self.ring = self.size // RING
        _, _, _, _, self.z = place()
        self.rows = normed[0].shape[1] // (self.ring * 2)
        self.short = 2 <= self.ring <= LONGEST_RING and self.rows % 64 == 0
        self.blocks, self.crossing, self.total = {}, None, None

    def multiply(self, step, mark=None):
        if not self.short:
            return ()
        chunk = lax.rem(self.z - 1 - step + 2 * self.ring, self.ring)
        normed, cotangent, array = self.given
        array = after(array, *jax.tree.leaves(mark))
        self.blocks[step] = outer_products(normed, cotangent, array, chunk, 2 * self.rows)
        return self.blocks[step][0]

    def begin(self):
        if self.short:
            self.crossing = flip(self.blocks[0][0], SIDE)

    def advance(self, step, *marks):
        if not self.short:
            return ()
        arrived = (self.crossing,) if self.total is None else (self.crossing, self.total)
        give = self.blocks[min(step + 1, self.ring - 1)][0]
        give, *arrived = lax.optimization_barrier((give, *arrived, *marks))[: len(arrived) + 1]
        total = self.blocks[step][1].astype(FULL)
        for part in arrived:
            total = total + part.astype(FULL)
        if step == self.ring - 1:
            self.sum = total.astype(LOW)
            return (self.sum,)
        low = total.astype(LOW)
        self.total, self.crossing = around(low), flip(give, SIDE)
        return (low, give)

    def result(self):
        if self.short:
            return self.sum
        normed, cotangent = (jnp.concatenate(pair, axis=0) for pair in self.given[:2])
        array = self.given[2]
        joined = jnp.concatenate(
            [outer_sum(normed, array[0]), outer_sum(normed, array[1]), outer_sum(cotangent, array[2])],
            axis=1,
        )
        return lax.psum_scatter(
            joined, "tok", scatter_dimension=0, tiled=True, axis_index_groups=groups_of(GROUP)
        )


def turn(values, cosine, sine):
    return values * cosine + pltpu.roll(values, HD // 2, 1) * sine


def mask_into(bias, key_segments, query_segments, block):
    keys, queries = bias.shape
    for start in range(0, queries, block):
        offset = (
            lax.broadcasted_iota(jnp.int32, (keys, block), 0)
            - lax.broadcasted_iota(jnp.int32, (keys, block), 1)
            - start
        )
        same = key_segments[...] == query_segments[:, start : start + block]
        allowed = same & (offset > 0) & (offset <= WINDOW)
        bias[:, start : start + block] = jnp.where(allowed, 0.0, -jnp.inf)


def attend_kernel(
    block, factor, q_ref, key_ref, value_t_ref, ks_ref, qs_ref, cos_ref, sin_ref,
    rot_ref, mixed_ref, log_ref, bias,
):
    @pl.when(pl.program_id(0) == 0)
    def _():
        mask_into(bias, ks_ref, qs_ref, block)

    queries = q_ref.shape[0]
    rot_ref[...] = turn(q_ref[...], cos_ref[...], sin_ref[...]).astype(LOW)
    for start in range(0, queries, block):
        rows, span = pl.ds(start, block), pl.ds(start, WINDOW + block)
        raw = by_rows(key_ref[span, :], rot_ref[rows, :])
        score = raw * factor + bias[span, rows]
        top = jnp.max(score, axis=0, keepdims=True)
        expo = jnp.exp2(score - top)
        total = jnp.sum(expo, axis=0, keepdims=True)
        mixed_t = matmul(value_t_ref[:, span], expo.astype(LOW)) / total
        mixed_ref[rows, :] = mixed_t.T.astype(LOW)
        log_ref[0, :, rows] = top + jnp.log2(total)


def attend(raw_query, key_value, key_segments, query_segments, cosine, sine, first, heads):
    queries, width = raw_query.shape[0], heads * HD
    keys = key_value.shape[0]
    block = min(256, queries)
    head = pl.BlockSpec((queries, HD), lambda h: (0, h))
    whole = lambda shape: pl.BlockSpec(shape, lambda h: (0,) * len(shape))
    return pl.pallas_call(
        functools.partial(attend_kernel, block, HD**-0.5 * LOG2E),
        grid=(heads,),
        in_specs=[
            pl.BlockSpec((queries, HD), lambda h: (0, first + h)),
            whole((keys, HD)),
            whole((HD, keys)),
            whole((keys, 1)),
            whole((1, queries)),
            whole((queries, HD)),
            whole((queries, HD)),
        ],
        out_specs=[head, head, pl.BlockSpec((1, 1, queries), lambda h: (h, 0, 0))],
        out_shape=[
            jax.ShapeDtypeStruct((queries, width), LOW),
            jax.ShapeDtypeStruct((queries, width), LOW),
            jax.ShapeDtypeStruct((heads, 1, queries), FULL),
        ],
        scratch_shapes=[pltpu.VMEM((keys, queries), FULL)],
        compiler_params=pltpu.CompilerParams(vmem_limit_bytes=40 * MIB),
        cost_estimate=LIGHT,
    )(
        raw_query,
        key_value[:, :HD],
        key_value[:, HD:].T,
        key_segments[:, None],
        query_segments[None, :],
        cosine,
        sine,
    )


def attend_back_kernel(
    block, factor, rot_ref, grad_ref, mixed_ref, log_ref, key_ref, value_ref, ks_ref, qs_ref,
    cos_ref, sin_ref, query_out, key_out, value_out, bias, key_t_ref,
):
    @pl.when(pl.program_id(0) == 0)
    def _():
        mask_into(bias, ks_ref, qs_ref, block)
        key_t_ref[...] = key_ref[...].T
        key_out[...] = jnp.zeros_like(key_out)
        value_out[...] = jnp.zeros_like(value_out)

    queries = rot_ref.shape[0]
    for start in range(0, queries, block):
        rows, span = pl.ds(start, block), pl.ds(start, WINDOW + block)
        rot, grad = rot_ref[rows, :], grad_ref[rows, :]
        product = grad.astype(FULL) * mixed_ref[rows, :].astype(FULL)
        inner = jnp.sum(product.T, axis=0, keepdims=True)
        raw = by_rows(key_ref[span, :], rot)
        prob = jnp.exp2(raw * factor + (bias[span, rows] - log_ref[0, :, rows]))
        grad_prob = by_rows(value_ref[span, :], grad)
        grad_raw = (prob * (grad_prob - inner)).astype(LOW)
        value_out[span, :] += matmul(prob.astype(LOW), grad)
        key_out[span, :] += matmul(grad_raw, rot)
        back = matmul(key_t_ref[:, span], grad_raw).T * HD**-0.5
        query_out[rows, :] = turn(back, cos_ref[rows, :], -sin_ref[rows, :]).astype(LOW)


def attend_back(rot, grad, mixed, logs, key_value, key_segments, query_segments, cosine, sine):
    queries, width = rot.shape
    keys = key_value.shape[0]
    heads = width // HD
    block = min(256, queries)
    head = pl.BlockSpec((queries, HD), lambda h: (0, h))
    whole = lambda shape: pl.BlockSpec(shape, lambda h: (0,) * len(shape))
    return pl.pallas_call(
        functools.partial(attend_back_kernel, block, HD**-0.5 * LOG2E),
        grid=(heads,),
        in_specs=[
            head,
            head,
            head,
            pl.BlockSpec((1, 1, queries), lambda h: (h, 0, 0)),
            pl.BlockSpec((keys, HD), lambda h: (0, 0)),
            pl.BlockSpec((keys, HD), lambda h: (0, 1)),
            whole((keys, 1)),
            whole((1, queries)),
            whole((queries, HD)),
            whole((queries, HD)),
        ],
        out_specs=[head, whole((keys, HD)), whole((keys, HD))],
        out_shape=[
            jax.ShapeDtypeStruct((queries, width), LOW),
            jax.ShapeDtypeStruct((keys, HD), FULL),
            jax.ShapeDtypeStruct((keys, HD), FULL),
        ],
        scratch_shapes=[pltpu.VMEM((keys, queries), FULL), pltpu.VMEM((HD, keys), LOW)],
        compiler_params=pltpu.CompilerParams(vmem_limit_bytes=40 * MIB),
        cost_estimate=LIGHT,
    )(
        rot,
        grad,
        mixed,
        logs,
        key_value,
        key_value,
        key_segments[:, None],
        query_segments[None, :],
        cosine,
        sine,
    )


GELU_A = 0.7978845608028654
GELU_B = 0.044715


def hidden_kernel(count, *refs):
    normed_refs, cot_refs, pieces = refs[:2], refs[2:4], refs[4 : 4 + count]
    out_ref, weights_out, weights, sems = refs[4 + count :]
    step, steps = pl.program_id(0), pl.num_programs(0)
    me = lax.axis_index("tok")
    side, z, ring = (me // SIDE) % 2, me // RING, count // 2
    rows = weights.shape[0] // count

    def load(k):
        if count == 1:
            start = 0
        else:
            start = 2 * ((z - k // 2 + ring) % ring) + (side if k % 2 == 0 else 1 - side)
        return pltpu.make_async_copy(
            pieces[k], weights.at[pl.ds(pl.multiple_of(start * rows, 16), rows)], sems.at[k]
        )

    keep = pltpu.make_async_copy(weights, weights_out, sems.at[count])

    @pl.when(step == 0)
    def _():
        for k in range(count):
            load(k).start()
        for k in range(count):
            load(k).wait()
        keep.start()

    early = step < steps // 2
    normed = jnp.where(early, normed_refs[0][...], normed_refs[1][...])
    cotangent = jnp.where(early, cot_refs[0][...], cot_refs[1][...])
    columns = out_ref.shape[2]
    gate = matmul(normed, weights[:, :columns])
    up = matmul(normed, weights[:, columns : 2 * columns])
    grad_hidden = matmul(cotangent, weights[:, 2 * columns :])
    activation_grads(out_ref, gate, up, grad_hidden)

    @pl.when(step == steps - 1)
    def _():
        keep.wait()


def hidden_and_grads(normed, cotangent, pieces):
    half, width = normed[0].shape
    columns = pieces[0].shape[1] // 3
    rows = min(256, half)
    steps = half // rows
    count = len(pieces)
    if count >= 4 and pieces[0].shape[0] % 64 == 0:
        return hidden_by_depth(normed, cotangent, pieces)
    blocks = [
        pl.BlockSpec((rows, width), lambda i: (jnp.minimum(i, steps - 1), 0)),
        pl.BlockSpec((rows, width), lambda i: (jnp.maximum(i - steps, 0), 0)),
    ]
    anywhere = pl.BlockSpec(memory_space=pl.ANY)
    return pl.pallas_call(
        functools.partial(hidden_kernel, count),
        grid=(2 * steps,),
        in_specs=blocks * 2 + [anywhere] * count,
        out_specs=[pl.BlockSpec((3, rows, columns), lambda i: (0, i, 0)), anywhere],
        out_shape=[
            jax.ShapeDtypeStruct((3, 2 * half, columns), LOW),
            jax.ShapeDtypeStruct((width, 3 * columns), LOW),
        ],
        scratch_shapes=[
            pltpu.VMEM((width, 3 * columns), LOW),
            pltpu.SemaphoreType.DMA((count + 1,)),
        ],
        compiler_params=pltpu.CompilerParams(vmem_limit_bytes=48 * MIB),
        cost_estimate=LIGHT,
    )(*normed, *cotangent, *pieces)


def activation_grads(out_ref, gate, up, grad_hidden):
    square = gate * gate
    bent = jnp.tanh(gate * (GELU_A + GELU_A * GELU_B * square))
    half = 0.5 * (1.0 + bent)
    value = gate * half
    slope = half + 0.5 * gate * (1.0 - bent * bent) * (GELU_A + 3.0 * GELU_A * GELU_B * square)
    out_ref[0] = (grad_hidden * up * slope).astype(LOW)
    out_ref[1] = (grad_hidden * value).astype(LOW)
    out_ref[2] = (value * up).astype(LOW)


def depth_kernel(ring, first, count, last, *refs):
    normed_refs, cot_refs, pieces, refs = refs[:2], refs[2:4], refs[4 : 4 + count], refs[4 + count :]
    if last:
        partial_ref, _, out_ref, weights_out, weights, sems = refs
    else:
        out_ref, weights_out, weights, sems = refs
    step, steps = pl.program_id(0), pl.num_programs(0)
    me = lax.axis_index("tok")
    side, z = (me // SIDE) % 2, me // RING
    rows = weights.shape[0] // count
    wide = 2 * rows

    def chunk(k):
        return (z - first - k + 2 * ring) % ring

    def load(k):
        start = wide * (k // 2) + rows * (side if k % 2 == 0 else 1 - side)
        return pltpu.make_async_copy(
            pieces[k], weights.at[pl.ds(pl.multiple_of(start, 16), rows)], sems.at[k]
        )

    def keep(k):
        return pltpu.make_async_copy(
            weights.at[pl.ds(wide * k, wide)],
            weights_out.at[pl.ds(pl.multiple_of(chunk(k) * wide, 16), wide)],
            sems.at[count + k],
        )

    @pl.when(step == 0)
    def _():
        for k in range(count):
            load(k).start()
        for k in range(count):
            load(k).wait()
        for k in range(count // 2):
            keep(k).start()

    early = step < steps // 2

    def columns_of(pair):
        parts = []
        for k in range(count // 2):
            lanes = pl.ds(pl.multiple_of(chunk(k) * wide, HD), wide)
            parts.append(jnp.where(early, pair[0][:, lanes], pair[1][:, lanes]))
        return parts[0] if len(parts) == 1 else jnp.concatenate(parts, axis=1)

    normed, cotangent = columns_of(normed_refs), columns_of(cot_refs)
    columns = out_ref.shape[2]
    products = [
        matmul(left, weights[:, k * columns : (k + 1) * columns])
        for k, left in enumerate((normed, normed, cotangent))
    ]
    if last:
        activation_grads(out_ref, *(products[k] + partial_ref[k].astype(FULL) for k in range(3)))
    else:
        for k in range(3):
            out_ref[k] = products[k].astype(LOW)

    @pl.when(step == steps - 1)
    def _():
        for k in range(count // 2):
            keep(k).wait()


def hidden_by_depth(normed, cotangent, pieces):
    half, width = normed[0].shape
    columns = pieces[0].shape[1] // 3
    rows = min(256, half)
    steps = half // rows
    ring = len(pieces) // 2
    deep = width // ring
    blocks = [
        pl.BlockSpec((rows, width), lambda i: (jnp.minimum(i, steps - 1), 0)),
        pl.BlockSpec((rows, width), lambda i: (jnp.maximum(i - steps, 0), 0)),
    ]
    anywhere = pl.BlockSpec(memory_space=pl.ANY)
    block = pl.BlockSpec((3, rows, columns), lambda i: (0, i, 0))
    weights_shape = jax.ShapeDtypeStruct((width, 3 * columns), LOW)

    def part(first, given, more):
        count = len(given)
        return pl.pallas_call(
            functools.partial(depth_kernel, ring, first, count, len(more) > 0),
            grid=(2 * steps,),
            in_specs=blocks * 2 + [anywhere] * count + [block, anywhere][: len(more)],
            out_specs=[block, anywhere],
            out_shape=[jax.ShapeDtypeStruct((3, 2 * half, columns), LOW), weights_shape],
            input_output_aliases={5 + count: 1} if more else {},
            scratch_shapes=[
                pltpu.VMEM((deep * (count // 2), 3 * columns), LOW),
                pltpu.SemaphoreType.DMA((count + count // 2,)),
            ],
            compiler_params=pltpu.CompilerParams(vmem_limit_bytes=48 * MIB),
            cost_estimate=LIGHT,
        )(*normed, *cotangent, *given, *more)

    partial = part(0, pieces[:-2], [])
    return part(ring - 1, pieces[-2:], partial)


def project_sum_kernel(count, array_ref, *refs):
    weight_refs, out_refs = refs[:count], refs[count : count + 2]
    away, arrived, send_sem, recv_sem = refs[count + 2 :]
    step = pl.program_id(0)
    me = lax.axis_index("tok")
    mate = me + 1 - 2 * (me % 2)

    def crossing(block):
        return pltpu.make_async_remote_copy(
            src_ref=away.at[block],
            dst_ref=arrived.at[block],
            send_sem=send_sem.at[block],
            recv_sem=recv_sem.at[block],
            device_id=(mate,),
            device_id_type=pl.DeviceIdType.MESH,
        )

    @pl.when(step == 0)
    def _():
        barrier = pltpu.get_barrier_semaphore()
        pl.semaphore_signal(
            barrier, inc=1, device_id=(mate,), device_id_type=pl.DeviceIdType.MESH
        )
        pl.semaphore_wait(barrier, 1)

    total = by_rows(array_ref[0], weight_refs[0][...])
    for k in range(1, count):
        total += by_rows(array_ref[k], weight_refs[k][...])
    for block in range(2):

        @pl.when(step == block)
        def _():
            away[block] = total.astype(LOW)
            crossing(block).start()

        @pl.when(step == 2 + block)
        def _():
            crossing(block).wait()
            out_refs[block][...] = (total + arrived[block].astype(FULL)).astype(LOW)


def project_sum(array, pack, first, count, identity, marks=()):
    array = after(array, *jax.tree.leaves(marks))
    tokens, columns = array.shape[1:]
    width = pack.shape[0]
    rows = tokens // 4
    whole = pl.BlockSpec((rows, width), lambda i: (0, 0))
    return pl.pallas_call(
        functools.partial(project_sum_kernel, count),
        grid=(4,),
        in_specs=[pl.BlockSpec((count, rows, columns), lambda i: (first // count, (i + 2) % 4, 0))]
        + [
            pl.BlockSpec(
                (width, columns), lambda i, k=k: (0, first + k), pipeline_mode=pl.Buffered(1)
            )
            for k in range(count)
        ],
        out_specs=[whole] * 2,
        out_shape=[jax.ShapeDtypeStruct((rows, width), LOW)] * 2,
        scratch_shapes=[
            pltpu.VMEM((2, rows, width), LOW),
            pltpu.VMEM((2, rows, width), LOW),
            pltpu.SemaphoreType.DMA((2,)),
            pltpu.SemaphoreType.DMA((2,)),
        ],
        compiler_params=pltpu.CompilerParams(
            collective_id=identity, has_side_effects=True, vmem_limit_bytes=44 * MIB
        ),
        cost_estimate=LIGHT,
    )(array, *([pack] * count))


def outer_kernel(chunk_ref, *refs):
    normed_refs, cot_refs, right_ref, give_ref, keep_ref, total = refs[:2], refs[2:4], *refs[4:]
    step, steps = pl.program_id(0), pl.num_programs(0)
    early = step < steps // 2
    normed = jnp.where(early, normed_refs[0][...], normed_refs[1][...])
    cotangent = jnp.where(early, cot_refs[0][...], cot_refs[1][...])
    columns = right_ref.shape[2]

    @pl.when(step == 0)
    def _():
        total[...] = jnp.zeros_like(total)

    for k, left in enumerate((normed, normed, cotangent)):
        total[:, k * columns : (k + 1) * columns] += outer_sum(left, right_ref[k])

    @pl.when(step == steps - 1)
    def _():
        rows = keep_ref.shape[0]
        side = (lax.axis_index("tok") // SIDE) % 2
        for ref, place_of in ((give_ref, 1 - side), (keep_ref, side)):
            ref[...] = total[pl.ds(pl.multiple_of(place_of * rows, 16), rows), :].astype(LOW)


def outer_products(normed, cotangent, array, chunk, rows):
    tokens, columns = array.shape[1:]
    deep = min(512, tokens // 2)
    steps = tokens // 2 // deep
    lefts = [
        pl.BlockSpec((deep, rows), lambda i, chunk_ref: (jnp.minimum(i, steps - 1), chunk_ref[0])),
        pl.BlockSpec((deep, rows), lambda i, chunk_ref: (jnp.maximum(i - steps, 0), chunk_ref[0])),
    ]
    return pl.pallas_call(
        outer_kernel,
        grid_spec=pltpu.PrefetchScalarGridSpec(
            num_scalar_prefetch=1,
            grid=(2 * steps,),
            in_specs=lefts * 2
            + [pl.BlockSpec((3, deep, columns), lambda i, chunk_ref: (0, i, 0))],
            out_specs=[pl.BlockSpec((rows // 2, 3 * columns), lambda i, chunk_ref: (0, 0))] * 2,
            scratch_shapes=[pltpu.VMEM((rows, 3 * columns), FULL)],
        ),
        out_shape=[jax.ShapeDtypeStruct((rows // 2, 3 * columns), LOW)] * 2,
        compiler_params=pltpu.CompilerParams(vmem_limit_bytes=40 * MIB),
        cost_estimate=LIGHT,
    )(chunk[None].astype(jnp.int32), *normed, *cotangent, array)


def join_kernel(count, epsilon, *refs):
    inputs_ref, gain_ref, weight_ref = refs[:3]
    parts, (middle_ref, normed_ref, inverse_ref) = refs[3 : 3 + count], refs[3 + count :]
    total, start = inputs_ref[...].astype(FULL), 0
    for part in parts:
        columns = part.shape[1]
        total += by_rows(part[...], weight_ref[:, start : start + columns])
        start += columns
    inverse = lax.rsqrt(jnp.mean(total * total, axis=1, keepdims=True) + epsilon)
    middle_ref[...] = total
    inverse_ref[...] = jnp.broadcast_to(inverse, inverse_ref.shape)
    normed_ref[...] = (total * inverse * gain_ref[...]).astype(LOW)


def join(tokens, gain, weight, parts):
    count, width = tokens.shape
    rows = min(256, count)
    block = lambda columns: pl.BlockSpec((rows, columns), lambda i: (i, 0))
    return pl.pallas_call(
        functools.partial(join_kernel, len(parts), EPSILON),
        grid=(count // rows,),
        in_specs=[
            block(width),
            pl.BlockSpec((1, width), lambda i: (0, 0)),
            pl.BlockSpec((width, width), lambda i: (0, 0), pipeline_mode=pl.Buffered(1)),
        ]
        + [block(part.shape[1]) for part in parts],
        out_specs=[block(width), block(width), block(HD)],
        out_shape=[
            jax.ShapeDtypeStruct((count, width), FULL),
            jax.ShapeDtypeStruct((count, width), LOW),
            jax.ShapeDtypeStruct((count, HD), FULL),
        ],
        compiler_params=pltpu.CompilerParams(vmem_limit_bytes=40 * MIB),
        cost_estimate=LIGHT,
    )(tokens, gain[None], weight, *parts)


def branch_kernel(
    group_ref, near_ref, cot_ref, middle_ref, inverse_ref, gain_ref, weight_ref,
    grad_ref, branch_ref, mixed_ref, scaled_ref,
):
    grad = group_ref[...].astype(FULL) + near_ref[...].astype(FULL)
    middle, inverse = middle_ref[...], inverse_ref[:, :1]
    normal = middle * inverse
    scaled_ref[...] = (grad * normal).astype(LOW)
    scaled = grad * gain_ref[...]
    total = (
        cot_ref[...].astype(FULL)
        + inverse * scaled
        - normal * (inverse * jnp.mean(scaled * normal, axis=1, keepdims=True))
    )
    grad_ref[...] = total
    branch = total.astype(LOW)
    branch_ref[...] = branch
    mixed_ref[...] = matmul(branch, weight_ref[...]).astype(LOW)


def branch_back(group, near, cotangent, middle, inverse, gain, weight):
    count, width = middle.shape
    rows = min(256, count)
    block = lambda columns: pl.BlockSpec((rows, columns), lambda i: (i, 0))
    return pl.pallas_call(
        branch_kernel,
        grid=(count // rows,),
        in_specs=[
            block(width),
            block(width),
            block(width),
            block(width),
            block(HD),
            pl.BlockSpec((1, width), lambda i: (0, 0)),
            pl.BlockSpec((width, width), lambda i: (0, 0), pipeline_mode=pl.Buffered(1)),
        ],
        out_specs=[block(width)] * 4,
        out_shape=[
            jax.ShapeDtypeStruct((count, width), FULL),
            jax.ShapeDtypeStruct((count, width), LOW),
            jax.ShapeDtypeStruct((count, width), LOW),
            jax.ShapeDtypeStruct((count, width), LOW),
        ],
        compiler_params=pltpu.CompilerParams(vmem_limit_bytes=48 * MIB),
        cost_estimate=LIGHT,
    )(group, near, cotangent, middle, inverse, gain[None], weight)


def on_device(
    tokens, cotangent, attn_gain, ffn_gain, w_query, w_key, w_value, w_out, w_gate, w_up, w_down,
    segments, positions,
):
    token_count, width = tokens.shape
    own_rows, hidden_width = w_gate.shape
    slice_width = hidden_width // GROUP
    heads_width = w_query.shape[1]
    tail_rows = min(token_count, WINDOW)
    hop_count = WINDOW // tail_rows
    device = lax.axis_index("tok")
    inputs = tokens.astype(FULL)

    frequency = 10000.0 ** (-jnp.arange(HD // 2, dtype=FULL) * 2.0 / HD)
    angles = positions.astype(FULL)[:, None] * frequency[None, :]
    cosine = jnp.concatenate([jnp.cos(angles)] * 2, axis=1)
    sine_half = jnp.sin(angles)
    sine = jnp.concatenate([-sine_half, sine_half], axis=1)
    padded_segments = jnp.concatenate([jnp.full((WINDOW,), -1, jnp.int32), segments])
    key_segments = lax.dynamic_slice_in_dim(
        padded_segments, device * token_count, WINDOW + token_count
    )
    query_segments = lax.dynamic_slice_in_dim(segments, device * token_count, token_count)

    attn_pack = jnp.concatenate(
        [
            w_query,
            w_key,
            w_value,
            jnp.pad(
                jnp.stack([attn_gain, ffn_gain], axis=1), ((0, 0), (0, HD - 2))
            ),
        ],
        axis=1,
    )
    edge = heads_width + 2 * HD
    def sliced(weight):
        return weight.reshape(own_rows, GROUP, slice_width).transpose(1, 0, 2)

    ffn_pack = jnp.concatenate([sliced(w_gate), sliced(w_up), sliced(w_down)], axis=2)
    attn_all, ffn_rows = gather(attn_pack, ffn_pack)
    out_w = lax.all_gather(w_out, "tok", axis=0, tiled=True)
    query_w, kv_w = attn_all[:, :heads_width], attn_all[:, heads_width:edge]
    gains = attn_all[:, edge : edge + 2].astype(FULL)
    gain_one, gain_two = gains[:, 0], gains[:, 1]

    inverse_one = lax.rsqrt(jnp.mean(inputs * inputs, axis=-1, keepdims=True) + EPSILON)
    normed = (inputs * inverse_one * gain_one).astype(LOW)
    kv = matmul(normed, kv_w)

    def turned(values, sine_signed):
        half = HD // 2
        rolled = jnp.concatenate([values[:, half:], values[:, :half]], axis=1)
        return values * cosine + rolled * sine_signed

    key_value = jnp.concatenate([turned(kv[:, :HD], sine), kv[:, HD:]], axis=1).astype(LOW)
    received = [passed_along(key_value, hop) for hop in range(hop_count, 0, -1)]
    all_keys = jnp.concatenate(received + [key_value], axis=0)
    raw_query = matmul(normed, query_w)
    heads = heads_width // HD
    given = (all_keys, key_segments, query_segments, cosine, sine)
    early = attend(raw_query, *given, 0, heads // 2)
    pieces, steps = spread(ffn_rows, (early[1],))
    cot_group = rows_to_group(after(cotangent, attn_all), steps[1])
    late = attend(
        after(raw_query, early[1]), *given, heads // 2, heads - heads // 2
    )
    rot, mixed = (jnp.concatenate([early[k], late[k]], axis=1) for k in range(2))
    logs = jnp.concatenate([early[2], late[2]], axis=0)
    middle, normed_two, inverse_two = join(tokens, gain_two, out_w, (early[1], late[1]))

    normed_group = rows_to_group(after(normed_two, *steps[1]), steps[2])
    hidden_pack, ffn_w = hidden_and_grads(normed_group, cot_group, pieces)
    reduction = Reduction(normed_group, cot_group, hidden_pack)
    pairs_done = reduction.multiply(0)
    reduction.begin()
    pairs_done = reduction.multiply(1, pairs_done)
    own_sum, near_sum = project_sum(hidden_pack, ffn_w, 0, 2, 2, pairs_done)
    near_sent = flip(near_sum, NEAR)
    marks = reduction.advance(0, near_sum)
    pairs_done = reduction.multiply(2, marks)
    pairs_done = reduction.multiply(3, pairs_done)
    marks = reduction.advance(1, pairs_done)
    output_own, output_near = project_sum(hidden_pack, ffn_w, 2, 1, 3, marks)
    output_near = flip(after(output_near, near_sent), NEAR)

    grad_middle, branch, grad_mixed, gain_two_parts = branch_back(
        own_sum, after(near_sent, output_own), cotangent, middle, inverse_two, gain_two, out_w
    )
    grad_out_w = outer_sum(branch, mixed).astype(LOW)
    cut = heads_width // 2
    out_sum = lax.psum_scatter(grad_out_w[:, :cut], "tok", scatter_dimension=0, tiled=True)
    marks = reduction.advance(2, grad_mixed)
    query_low, key_grads, value_grads = attend_back(
        rot, after(grad_mixed, *marks), mixed, logs, all_keys, key_segments, query_segments, cosine, sine
    )
    output = (
        middle + output_own.astype(FULL) + after(output_near, query_low).astype(FULL)
    ).astype(LOW)
    grads = jnp.concatenate([key_grads * HD**-0.5, value_grads], axis=1)
    shares = grads[WINDOW:]
    for hop in range(1, hop_count + 1):
        first_row = (hop_count - hop) * tail_rows
        returned = passed_along(grads[first_row : first_row + tail_rows].astype(LOW), -hop)
        shares = shares.at[token_count - tail_rows :].add(returned.astype(FULL))
    kv_low = jnp.concatenate([turned(shares[:, :HD], -sine), shares[:, HD:]], axis=1).astype(LOW)
    grad_query_w = outer_sum(normed, query_low).astype(LOW)
    grad_kv_w = outer_sum(normed, kv_low).astype(LOW)
    grad_normed = by_rows(query_low, query_w) + by_rows(kv_low, kv_w)
    scaled_one = grad_normed * gain_one
    grad_inputs = inverse_one * scaled_one - inputs * inverse_one**3 * jnp.mean(
        scaled_one * inputs, axis=-1, keepdims=True
    )
    grad_tokens = (grad_middle + grad_inputs).astype(LOW)
    lane = lax.broadcasted_iota(jnp.int32, (token_count, HD), 1)
    grad_gains = (
        outer_sum((grad_normed * inputs * inverse_one).astype(LOW), (lane == 0).astype(LOW))
        + outer_sum(gain_two_parts, (lane == 1).astype(LOW))
    ).astype(LOW)
    reduction.advance(3, grad_query_w)
    attn_sum, ffn_parts = scatter(
        [grad_query_w, grad_kv_w, grad_gains, grad_out_w[:, cut:]], reduction.result()
    )

    def joined(parts):
        return parts.transpose(1, 0, 2).reshape(own_rows, hidden_width).astype(FULL)

    return (
        output,
        grad_tokens,
        attn_sum[:, edge],
        attn_sum[:, edge + 1],
        attn_sum[:, :heads_width],
        attn_sum[:, heads_width : heads_width + HD],
        attn_sum[:, heads_width + HD : edge],
        jnp.concatenate([out_sum.astype(FULL), attn_sum[:, edge + HD :]], axis=1),
        joined(ffn_parts[:, :, :slice_width]),
        joined(ffn_parts[:, :, slice_width : 2 * slice_width]),
        joined(ffn_parts[:, :, 2 * slice_width :]),
    )


def solution(mesh):
    rows, flat = P("tok", None), P("tok")
    return jax.shard_map(
        on_device,
        mesh=mesh,
        in_specs=(rows, rows, flat, flat, rows, rows, rows, rows, rows, rows, rows, P(), flat),
        out_specs=(rows, rows, flat, flat, rows, rows, rows, rows, rows, rows, rows),
        check_vma=False,
    )
```

```python
import functools

import jax
import jax.numpy as jnp
from jax import lax
from jax.experimental import pallas as pl
from jax.experimental.pallas import tpu as pltpu
from jax.sharding import PartitionSpec as P

HQ = 12
HD = 128
WINDOW = 1024
EPSILON = 1e-06

CORE, NEAR, SIDE, GROUP, RING = 1, 2, 4, 4, 8
LONGEST_RING = 8
LOG2E = 1.4426950408889634
LOW = jnp.bfloat16
FULL = jnp.float32
MIB = 1024 * 1024
LIGHT = pl.CostEstimate(flops=1024, bytes_accessed=1024, transcendentals=0)


def flip(array, bit):
    size = lax.axis_size("tok")
    return lax.ppermute(array, "tok", [(i, i ^ bit) for i in range(size)])


def around(array):
    size = lax.axis_size("tok")
    return lax.ppermute(array, "tok", [(i, (i + RING) % size) for i in range(size)])


def passed_along(array, by):
    size = lax.axis_size("tok")
    pairs = [(i, i + by) for i in range(size) if 0 <= i + by < size]
    return lax.ppermute(array, "tok", pairs)


def rms_norm(values, scales):
    return values * lax.rsqrt(jnp.mean(values * values, axis=-1, keepdims=True) + EPSILON) * scales


def outer_sum(left_side, right_side):
    return lax.dot_general(
        left_side, right_side, (((0,), (0,)), ((), ())), preferred_element_type=FULL
    )


def by_rows(left_side, right_side):
    return lax.dot_general(
        left_side, right_side, (((1,), (1,)), ((), ())), preferred_element_type=FULL
    )


def matmul(left_side, right_side):
    return jnp.dot(left_side, right_side, preferred_element_type=FULL)


def pick(array, index):
    return lax.dynamic_index_in_dim(array, index, 0, keepdims=False)


def place():
    device = lax.axis_index("tok")
    return device, device % 2, (device // 2) % 2, (device // 4) % 2, device // RING


def rows_to_group(array, marks=()):
    two = jnp.concatenate([array, after(flip(array, NEAR), *marks)], axis=0)
    return two, flip(two, CORE)


def slices_to_group(parts):
    _, core, near, _, _ = place()
    rows, columns = parts.shape[1:]
    mine = lax.dynamic_slice_in_dim(parts, 2 * near, 2, 0)
    theirs = flip(lax.dynamic_slice_in_dim(parts, 2 * (1 - near), 2, 0), NEAR)
    here = jnp.stack([pick(mine, core), pick(theirs, core)])
    away = flip(jnp.stack([pick(mine, 1 - core), pick(theirs, 1 - core)]), CORE)
    by_core = jnp.where(core == 0, jnp.stack([here, away], 1), jnp.stack([away, here], 1))
    by_near = jnp.where(near == 0, by_core, by_core[::-1])
    return by_near.reshape(4 * rows, columns)


def slices_from_group(block):
    _, core, near, _, _ = place()
    rows, columns = block.shape[0] // 4, block.shape[1]
    parts = block.astype(LOW).reshape(2, 2, rows, columns)
    mine, theirs = pick(parts, near), flip(pick(parts, 1 - near), NEAR)
    here = jnp.stack([pick(mine, core), pick(theirs, core)])
    away = flip(jnp.stack([pick(mine, 1 - core), pick(theirs, 1 - core)]), CORE)
    by_core = jnp.where(core == 0, jnp.stack([here, away], 1), jnp.stack([away, here], 1))
    by_near = jnp.where(near == 0, by_core, by_core[::-1])
    return by_near.reshape(4, rows, columns)


def gather_kernel(
    ring, bands, attn_ref, ffn_ref, attn_out, ffn_out, local_sem, send_sem, recv_sem
):
    size = ring * RING
    me = lax.axis_index("tok")
    core, near, side, z = me % 2, (me // 2) % 2, (me // 4) % 2, me // RING
    core_mate, near_mate, side_mate = me + 1 - 2 * core, me + 2 - 4 * near, me + 4 - 8 * side
    far_mate = near_mate + 1 - 2 * core
    up, down = (me + RING) % size, (me + size - RING) % size

    barrier = pltpu.get_barrier_semaphore()
    partners = (core_mate, near_mate, side_mate, far_mate, up, down)
    for partner in partners:
        pl.semaphore_signal(
            barrier, inc=1, device_id=(partner,), device_id_type=pl.DeviceIdType.MESH
        )
    pl.semaphore_wait(barrier, len(partners))

    own = pltpu.make_async_copy(attn_ref, attn_out.at[z, side, near, core], local_sem.at[0])
    own.start()
    own_slice = pltpu.make_async_copy(
        ffn_ref.at[2 * near + core], ffn_out.at[2 * near + core], local_sem.at[1]
    )
    own_slice.start()

    copies = []

    def send(src, dst, to):
        index = len(copies)
        copy = pltpu.make_async_remote_copy(
            src_ref=src,
            dst_ref=dst,
            send_sem=send_sem.at[index],
            recv_sem=recv_sem.at[index],
            device_id=(to,),
            device_id_type=pl.DeviceIdType.MESH,
        )
        copy.start()
        copies.append(copy)
        return copy

    def forward(ref, to):
        return send(ref, ref, to)

    def chunk_of(step):
        return (z - step + ring) % ring

    def piece(step, band):
        return attn_out.at[chunk_of(step), side, near, core, :, bands[band]]

    hops, first, second, last = {}, {}, {}, {}
    over = []

    def finish(step):
        first[0, step].wait_recv()
        second[0, step] = forward(attn_out.at[chunk_of(step), side, :, core, :, bands[0]], side_mate)
        first[1, step].wait_recv()
        second[1, step] = forward(attn_out.at[chunk_of(step), :, near, core, :, bands[1]], near_mate)

    def hand_over(step):
        second[0, step].wait_recv()
        second[1, step].wait_recv()
        over.append(forward(attn_out.at[chunk_of(step), :, :, core], core_mate))

    for step in range(ring):
        for band in (0, 1):
            if step > 0:
                hops[band, step].wait_recv()
            source = attn_ref.at[:, bands[band]] if step == 0 else piece(step, band)
            if step < ring - 1:
                hops[band, step + 1] = send(source, piece(step, band), up)
            mate = near_mate if band == 0 else side_mate
            first[band, step] = send(source, piece(step, band), mate)
        if step == 0:
            begun = send(attn_ref.at[:, bands[2]], piece(0, 2), near_mate)
            slices = [
                send(ffn_ref.at[index], ffn_out.at[2 * near + core], mate)
                for mate, index in (
                    (near_mate, 2 * (1 - near) + core),
                    (far_mate, 2 * (1 - near) + 1 - core),
                    (core_mate, 2 * near + 1 - core),
                )
            ]
            own.wait()
            begun.wait_recv()
            last[0] = forward(attn_out.at[z, side, :, core, :, bands[2]], side_mate)
        else:
            last[step - 1].wait_recv()
            last[step] = forward(attn_out.at[chunk_of(step - 1), :, :, core, :, bands[2]], up)
            finish(step - 1)
        if step >= 2:
            hand_over(step - 2)
    finish(ring - 1)
    hand_over(ring - 2)
    last[ring - 1].wait_recv()
    hand_over(ring - 1)
    own_slice.wait()
    for copy in slices + over:
        copy.wait_recv()
    for copy in copies:
        copy.wait_send()


def gather(attn_pack, ffn_pack):
    size = lax.axis_size("tok")
    ring = size // RING
    rows, columns = attn_pack.shape
    if ring > LONGEST_RING or ring < 2 or rows % 48:
        return lax.all_gather(attn_pack, "tok", axis=0, tiled=True), slices_to_group(ffn_pack)
    lanes = columns // HD
    crossed = lanes * 4 // 15
    first = (lanes - crossed + 1) // 2
    ends = (0, first * HD, (lanes - crossed) * HD, columns)
    bands = [pl.ds(ends[band], ends[band + 1] - ends[band]) for band in range(3)]
    count = 3 + 2 * (ring - 1) + 2 * ring + 2 * ring + 1 + ring + ring
    anywhere = pl.BlockSpec(memory_space=pl.ANY)
    attn_all, ffn_rows = pl.pallas_call(
        functools.partial(gather_kernel, ring, bands),
        in_specs=[anywhere] * 2,
        out_specs=[anywhere] * 2,
        out_shape=[
            jax.ShapeDtypeStruct((ring, 2, 2, 2, rows, columns), attn_pack.dtype),
            jax.ShapeDtypeStruct(ffn_pack.shape, ffn_pack.dtype),
        ],
        scratch_shapes=[
            pltpu.SemaphoreType.DMA((2,)),
            pltpu.SemaphoreType.DMA((count,)),
            pltpu.SemaphoreType.DMA((count,)),
        ],
        compiler_params=pltpu.CompilerParams(collective_id=0, has_side_effects=True),
    )(attn_pack, ffn_pack)
    return attn_all.reshape(size * rows, columns), ffn_rows.reshape(GROUP * rows, -1)


def scatter_kernel(
    ring, bands, edges, *refs
):
    count = len(edges) - 1
    grad_refs, ffn_ref, attn_out, ffn_out = refs[:count], refs[count], refs[count + 1], refs[count + 2]
    pack, core_in, a_side, a_near, a_ring, b_near, b_side, b_ring, c_ring, c_side, c_near = refs[
        count + 3 : count + 14
    ]
    local_sem, send_sem, recv_sem = refs[count + 14 :]
    size = ring * RING
    me = lax.axis_index("tok")
    core, near, side, z = me % 2, (me // 2) % 2, (me // 4) % 2, me // RING
    core_mate, near_mate, side_mate = me + 1 - 2 * core, me + 2 - 4 * near, me + 4 - 8 * side
    far_mate = near_mate + 1 - 2 * core
    up, down = (me + RING) % size, (me + size - RING) % size

    def chunk_of(step):
        return (z - 1 - step + 2 * ring) % ring

    loads = []
    for step in range(ring):
        row = []
        for k in range(count):
            load = pltpu.make_async_copy(
                grad_refs[k].at[chunk_of(step)],
                pack.at[chunk_of(step), :, :, :, :, pl.ds(edges[k], edges[k + 1] - edges[k])],
                local_sem.at[step * count + k],
            )
            load.start()
            row.append(load)
        loads.append(row)
    own_slice = pltpu.make_async_copy(
        ffn_ref.at[2 * near + core], ffn_out.at[2 * near + core], local_sem.at[ring * count]
    )
    own_slice.start()

    barrier = pltpu.get_barrier_semaphore()
    partners = (core_mate, near_mate, side_mate, far_mate, up, down)
    for partner in partners:
        pl.semaphore_signal(
            barrier, inc=1, device_id=(partner,), device_id_type=pl.DeviceIdType.MESH
        )
    pl.semaphore_wait(barrier, len(partners))

    copies = []

    def send(src, dst, to):
        index = len(copies)
        copy = pltpu.make_async_remote_copy(
            src_ref=src,
            dst_ref=dst,
            send_sem=send_sem.at[index],
            recv_sem=recv_sem.at[index],
            device_id=(to,),
            device_id_type=pl.DeviceIdType.MESH,
        )
        copy.start()
        copies.append(copy)
        return copy

    def add(held, arrived):
        held[...] = (held[...].astype(FULL) + arrived[...].astype(FULL)).astype(LOW)

    def part(step, y, x, band):
        return pack.at[chunk_of(step), y, x, core, bands[band]]

    def own(step, band):
        return part(step, side, near, band)

    across, first, second, hops = {}, {}, {}, {}

    def begin(step):
        chunk = chunk_of(step)
        across[step].wait_recv()

        def one(k, _):
            add(pack.at[chunk, k // 2, k % 2, core], core_in.at[chunk, k // 2, k % 2])
            return 0

        lax.fori_loop(0, 4, one, 0)
        first[0, step] = send(
            pack.at[chunk, 1 - side, :, core, bands[0]], a_side.at[step], side_mate
        )
        first[1, step] = send(
            pack.at[chunk, :, 1 - near, core, bands[1]], b_near.at[step], near_mate
        )
        if step > 0:
            hops[2, step].wait_recv()
            for k in range(4):
                add(part(step, k // 2, k % 2, 2), c_ring.at[step - 1, k // 2, k % 2])
        if step < ring - 1:
            hops[2, step + 1] = send(
                pack.at[chunk, :, :, core, bands[2]], c_ring.at[step], up
            )

    def middle(step):
        first[0, step].wait_recv()
        for x in range(2):
            add(part(step, side, x, 0), a_side.at[step, x])
        second[0, step] = send(part(step, side, 1 - near, 0), a_near.at[step], near_mate)
        first[1, step].wait_recv()
        for y in range(2):
            add(part(step, y, near, 1), b_near.at[step, y])
        second[1, step] = send(part(step, 1 - side, near, 1), b_side.at[step], side_mate)

    def end(step):
        for band, arrived, passing in ((0, a_near, a_ring), (1, b_side, b_ring)):
            second[band, step].wait_recv()
            add(own(step, band), arrived.at[step])
            if step > 0:
                hops[band, step].wait_recv()
                add(own(step, band), passing.at[step - 1])
            if step < ring - 1:
                hops[band, step + 1] = send(own(step, band), passing.at[step], up)

    for step in range(ring):
        for load in loads[step]:
            load.wait()
        across[step] = send(
            pack.at[chunk_of(step), :, :, 1 - core], core_in.at[chunk_of(step)], core_mate
        )
    slices = []
    for step in range(ring + 2):
        if step < ring:
            begin(step)
        if step == 0:
            slices += [
                send(ffn_ref.at[index], ffn_out.at[2 * near + core], mate)
                for mate, index in (
                    (near_mate, 2 * (1 - near) + core),
                    (far_mate, 2 * (1 - near) + 1 - core),
                    (core_mate, 2 * near + 1 - core),
                )
            ]
        if 1 <= step <= ring:
            middle(step - 1)
        if step == ring:
            last = ring - 1
            to_side = send(pack.at[z, 1 - side, :, core, bands[2]], c_side, side_mate)
        if step >= 2:
            end(step - 2)
        if step == ring:
            to_side.wait_recv()
            for x in range(2):
                add(part(last, side, x, 2), c_side.at[x])
            to_near = send(part(last, side, 1 - near, 2), c_near, near_mate)
    to_near.wait_recv()
    add(own(last, 2), c_near)
    attn_out[...] = pack[z, side, near, core].astype(FULL)
    own_slice.wait()
    for copy in slices:
        copy.wait_recv()
    for copy in copies:
        copy.wait_send()


def scatter(grads, ffn_sum):
    size = lax.axis_size("tok")
    ring = size // RING
    rows = grads[0].shape[0] // size
    if ring > LONGEST_RING or ring < 2 or rows % 48:
        joined = jnp.concatenate(grads, axis=1).astype(FULL)
        return (
            lax.psum_scatter(joined, "tok", scatter_dimension=0, tiled=True),
            slices_from_group(ffn_sum),
        )
    third = rows // 3
    bands = [pl.ds(third * band, third) for band in range(3)]
    edges = [0]
    for grad in grads:
        edges.append(edges[-1] + grad.shape[1])
    columns = edges[-1]
    count = ring + 2 * ring + (ring - 1) + 3 + 2 * ring + 1 + 2 * (ring - 1) + 1
    anywhere = pl.BlockSpec(memory_space=pl.ANY)
    band = (third, columns)
    low = lambda *shape: pltpu.VMEM((*shape, *band), LOW)
    return pl.pallas_call(
        functools.partial(scatter_kernel, ring, bands, edges),
        in_specs=[anywhere] * (len(grads) + 1),
        out_specs=[pl.BlockSpec(memory_space=pltpu.VMEM), anywhere],
        out_shape=[
            jax.ShapeDtypeStruct((rows, columns), FULL),
            jax.ShapeDtypeStruct((GROUP, rows, ffn_sum.shape[1]), LOW),
        ],
        scratch_shapes=[
            pltpu.VMEM((ring, 2, 2, 2, rows, columns), LOW),
            pltpu.VMEM((ring, 2, 2, rows, columns), LOW),
            low(ring, 2),
            low(ring),
            low(ring - 1),
            low(ring, 2),
            low(ring),
            low(ring - 1),
            low(ring - 1, 2, 2),
            low(2),
            low(),
            pltpu.SemaphoreType.DMA((ring * len(grads) + 1,)),
            pltpu.SemaphoreType.DMA((count,)),
            pltpu.SemaphoreType.DMA((count,)),
        ],
        compiler_params=pltpu.CompilerParams(
            collective_id=1, has_side_effects=True, vmem_limit_bytes=44 * MIB
        ),
    )(
        *[grad.reshape(ring, 2, 2, 2, rows, -1) for grad in grads],
        ffn_sum.astype(LOW).reshape(GROUP, rows, -1),
    )


def after(value, *marks):
    return lax.optimization_barrier((value, *marks))[0]


def groups_of(stride):
    size = lax.axis_size("tok")
    return [[s + stride * k for k in range(size // stride)] for s in range(stride)]


def spread(block, marks):
    size = lax.axis_size("tok")
    ring = size // RING
    if ring > LONGEST_RING:
        gathered = lax.all_gather(
            block, "tok", axis=0, tiled=True, axis_index_groups=groups_of(GROUP)
        )
        return [gathered], [()] * 3
    own, crossed = [block], []
    for step in range(ring):
        crossed.append(flip(own[-1], SIDE))
        if step < ring - 1:
            arrived = around(own[-1])
            if step == 0:
                arrived, crossed[0] = lax.optimization_barrier((arrived, crossed[0], *marks))[:2]
            own.append(arrived)
    pieces = [piece for pair in zip(own, crossed) for piece in pair]
    return pieces, [(*own[step + 1 : step + 2], crossed[step]) for step in range(ring)]


class Reduction:
    def __init__(self, normed, cotangent, array):
        self.given = (normed, cotangent, array)
        self.size = lax.axis_size("tok")
        self.ring = self.size // RING
        _, _, _, _, self.z = place()
        self.rows = normed[0].shape[1] // (self.ring * 2)
        self.short = 2 <= self.ring <= LONGEST_RING and self.rows % 64 == 0
        self.blocks, self.crossing, self.total = {}, None, None

    def multiply(self, step, mark=None):
        if not self.short:
            return ()
        chunk = lax.rem(self.z - 1 - step + 2 * self.ring, self.ring)
        normed, cotangent, array = self.given
        array = after(array, *jax.tree.leaves(mark))
        self.blocks[step] = outer_products(normed, cotangent, array, chunk, 2 * self.rows)
        return self.blocks[step][0]

    def begin(self):
        if self.short:
            self.crossing = flip(self.blocks[0][0], SIDE)

    def advance(self, step, *marks):
        if not self.short:
            return ()
        arrived = (self.crossing,) if self.total is None else (self.crossing, self.total)
        give = self.blocks[min(step + 1, self.ring - 1)][0]
        give, *arrived = lax.optimization_barrier((give, *arrived, *marks))[: len(arrived) + 1]
        total = self.blocks[step][1].astype(FULL)
        for part in arrived:
            total = total + part.astype(FULL)
        if step == self.ring - 1:
            self.sum = total.astype(LOW)
            return (self.sum,)
        low = total.astype(LOW)
        self.total, self.crossing = around(low), flip(give, SIDE)
        return (low, give)

    def result(self):
        if self.short:
            return self.sum
        normed, cotangent = (jnp.concatenate(pair, axis=0) for pair in self.given[:2])
        array = self.given[2]
        joined = jnp.concatenate(
            [outer_sum(normed, array[0]), outer_sum(normed, array[1]), outer_sum(cotangent, array[2])],
            axis=1,
        )
        return lax.psum_scatter(
            joined, "tok", scatter_dimension=0, tiled=True, axis_index_groups=groups_of(GROUP)
        )


def turn(values, cosine, sine):
    return values * cosine + pltpu.roll(values, HD // 2, 1) * sine


def mask_into(bias, key_segments, query_segments, block):
    keys, queries = bias.shape
    for start in range(0, queries, block):
        offset = (
            lax.broadcasted_iota(jnp.int32, (keys, block), 0)
            - lax.broadcasted_iota(jnp.int32, (keys, block), 1)
            - start
        )
        same = key_segments[...] == query_segments[:, start : start + block]
        allowed = same & (offset > 0) & (offset <= WINDOW)
        bias[:, start : start + block] = jnp.where(allowed, 0.0, -jnp.inf)


def attend_kernel(
    block, factor, q_ref, key_ref, value_t_ref, ks_ref, qs_ref, cos_ref, sin_ref,
    rot_ref, mixed_ref, log_ref, bias,
):
    @pl.when(pl.program_id(0) == 0)
    def _():
        mask_into(bias, ks_ref, qs_ref, block)

    queries = q_ref.shape[0]
    rot_ref[...] = turn(q_ref[...], cos_ref[...], sin_ref[...]).astype(LOW)
    for start in range(0, queries, block):
        rows, span = pl.ds(start, block), pl.ds(start, WINDOW + block)
        raw = by_rows(key_ref[span, :], rot_ref[rows, :])
        score = raw * factor + bias[span, rows]
        top = jnp.max(score, axis=0, keepdims=True)
        expo = jnp.exp2(score - top)
        total = jnp.sum(expo, axis=0, keepdims=True)
        mixed_t = matmul(value_t_ref[:, span], expo.astype(LOW)) / total
        mixed_ref[rows, :] = mixed_t.T.astype(LOW)
        log_ref[0, :, rows] = top + jnp.log2(total)


def attend(raw_query, key_value, key_segments, query_segments, cosine, sine, first, heads):
    queries, width = raw_query.shape[0], heads * HD
    keys = key_value.shape[0]
    block = min(256, queries)
    head = pl.BlockSpec((queries, HD), lambda h: (0, h))
    whole = lambda shape: pl.BlockSpec(shape, lambda h: (0,) * len(shape))
    return pl.pallas_call(
        functools.partial(attend_kernel, block, HD**-0.5 * LOG2E),
        grid=(heads,),
        in_specs=[
            pl.BlockSpec((queries, HD), lambda h: (0, first + h)),
            whole((keys, HD)),
            whole((HD, keys)),
            whole((keys, 1)),
            whole((1, queries)),
            whole((queries, HD)),
            whole((queries, HD)),
        ],
        out_specs=[head, head, pl.BlockSpec((1, 1, queries), lambda h: (h, 0, 0))],
        out_shape=[
            jax.ShapeDtypeStruct((queries, width), LOW),
            jax.ShapeDtypeStruct((queries, width), LOW),
            jax.ShapeDtypeStruct((heads, 1, queries), FULL),
        ],
        scratch_shapes=[pltpu.VMEM((keys, queries), FULL)],
        compiler_params=pltpu.CompilerParams(vmem_limit_bytes=40 * MIB),
        cost_estimate=LIGHT,
    )(
        raw_query,
        key_value[:, :HD],
        key_value[:, HD:].T,
        key_segments[:, None],
        query_segments[None, :],
        cosine,
        sine,
    )


def attend_back_kernel(
    block, factor, rot_ref, grad_ref, mixed_ref, log_ref, key_ref, value_ref, ks_ref, qs_ref,
    cos_ref, sin_ref, query_out, key_out, value_out, bias, key_t_ref,
):
    @pl.when(pl.program_id(0) == 0)
    def _():
        mask_into(bias, ks_ref, qs_ref, block)
        key_t_ref[...] = key_ref[...].T
        key_out[...] = jnp.zeros_like(key_out)
        value_out[...] = jnp.zeros_like(value_out)

    queries = rot_ref.shape[0]
    for start in range(0, queries, block):
        rows, span = pl.ds(start, block), pl.ds(start, WINDOW + block)
        rot, grad = rot_ref[rows, :], grad_ref[rows, :]
        product = grad.astype(FULL) * mixed_ref[rows, :].astype(FULL)
        inner = jnp.sum(product.T, axis=0, keepdims=True)
        raw = by_rows(key_ref[span, :], rot)
        prob = jnp.exp2(raw * factor + (bias[span, rows] - log_ref[0, :, rows]))
        grad_prob = by_rows(value_ref[span, :], grad)
        grad_raw = (prob * (grad_prob - inner)).astype(LOW)
        value_out[span, :] += matmul(prob.astype(LOW), grad)
        key_out[span, :] += matmul(grad_raw, rot)
        back = matmul(key_t_ref[:, span], grad_raw).T * HD**-0.5
        query_out[rows, :] = turn(back, cos_ref[rows, :], -sin_ref[rows, :]).astype(LOW)


def attend_back(rot, grad, mixed, logs, key_value, key_segments, query_segments, cosine, sine):
    queries, width = rot.shape
    keys = key_value.shape[0]
    heads = width // HD
    block = min(256, queries)
    head = pl.BlockSpec((queries, HD), lambda h: (0, h))
    whole = lambda shape: pl.BlockSpec(shape, lambda h: (0,) * len(shape))
    return pl.pallas_call(
        functools.partial(attend_back_kernel, block, HD**-0.5 * LOG2E),
        grid=(heads,),
        in_specs=[
            head,
            head,
            head,
            pl.BlockSpec((1, 1, queries), lambda h: (h, 0, 0)),
            pl.BlockSpec((keys, HD), lambda h: (0, 0)),
            pl.BlockSpec((keys, HD), lambda h: (0, 1)),
            whole((keys, 1)),
            whole((1, queries)),
            whole((queries, HD)),
            whole((queries, HD)),
        ],
        out_specs=[head, whole((keys, HD)), whole((keys, HD))],
        out_shape=[
            jax.ShapeDtypeStruct((queries, width), LOW),
            jax.ShapeDtypeStruct((keys, HD), FULL),
            jax.ShapeDtypeStruct((keys, HD), FULL),
        ],
        scratch_shapes=[pltpu.VMEM((keys, queries), FULL), pltpu.VMEM((HD, keys), LOW)],
        compiler_params=pltpu.CompilerParams(vmem_limit_bytes=40 * MIB),
        cost_estimate=LIGHT,
    )(
        rot,
        grad,
        mixed,
        logs,
        key_value,
        key_value,
        key_segments[:, None],
        query_segments[None, :],
        cosine,
        sine,
    )


GELU_A = 0.7978845608028654
GELU_B = 0.044715


def hidden_kernel(count, *refs):
    normed_refs, cot_refs, pieces = refs[:2], refs[2:4], refs[4 : 4 + count]
    out_ref, weights_out, weights, sems = refs[4 + count :]
    step, steps = pl.program_id(0), pl.num_programs(0)
    me = lax.axis_index("tok")
    side, z, ring = (me // SIDE) % 2, me // RING, count // 2
    rows = weights.shape[0] // count

    def load(k):
        if count == 1:
            start = 0
        else:
            start = 2 * ((z - k // 2 + ring) % ring) + (side if k % 2 == 0 else 1 - side)
        return pltpu.make_async_copy(
            pieces[k], weights.at[pl.ds(pl.multiple_of(start * rows, 16), rows)], sems.at[k]
        )

    keep = pltpu.make_async_copy(weights, weights_out, sems.at[count])

    @pl.when(step == 0)
    def _():
        for k in range(count):
            load(k).start()
        for k in range(count):
            load(k).wait()
        keep.start()

    early = step < steps // 2
    normed = jnp.where(early, normed_refs[0][...], normed_refs[1][...])
    cotangent = jnp.where(early, cot_refs[0][...], cot_refs[1][...])
    columns = out_ref.shape[2]
    gate = matmul(normed, weights[:, :columns])
    up = matmul(normed, weights[:, columns : 2 * columns])
    grad_hidden = matmul(cotangent, weights[:, 2 * columns :])
    activation_grads(out_ref, gate, up, grad_hidden)

    @pl.when(step == steps - 1)
    def _():
        keep.wait()


def hidden_and_grads(normed, cotangent, pieces):
    half, width = normed[0].shape
    columns = pieces[0].shape[1] // 3
    rows = min(256, half)
    steps = half // rows
    count = len(pieces)
    if count >= 4 and pieces[0].shape[0] % 64 == 0:
        return hidden_by_depth(normed, cotangent, pieces)
    blocks = [
        pl.BlockSpec((rows, width), lambda i: (jnp.minimum(i, steps - 1), 0)),
        pl.BlockSpec((rows, width), lambda i: (jnp.maximum(i - steps, 0), 0)),
    ]
    anywhere = pl.BlockSpec(memory_space=pl.ANY)
    return pl.pallas_call(
        functools.partial(hidden_kernel, count),
        grid=(2 * steps,),
        in_specs=blocks * 2 + [anywhere] * count,
        out_specs=[pl.BlockSpec((3, rows, columns), lambda i: (0, i, 0)), anywhere],
        out_shape=[
            jax.ShapeDtypeStruct((3, 2 * half, columns), LOW),
            jax.ShapeDtypeStruct((width, 3 * columns), LOW),
        ],
        scratch_shapes=[
            pltpu.VMEM((width, 3 * columns), LOW),
            pltpu.SemaphoreType.DMA((count + 1,)),
        ],
        compiler_params=pltpu.CompilerParams(vmem_limit_bytes=48 * MIB),
        cost_estimate=LIGHT,
    )(*normed, *cotangent, *pieces)


def activation_grads(out_ref, gate, up, grad_hidden):
    square = gate * gate
    bent = jnp.tanh(gate * (GELU_A + GELU_A * GELU_B * square))
    half = 0.5 * (1.0 + bent)
    value = gate * half
    slope = half + 0.5 * gate * (1.0 - bent * bent) * (GELU_A + 3.0 * GELU_A * GELU_B * square)
    out_ref[0] = (grad_hidden * up * slope).astype(LOW)
    out_ref[1] = (grad_hidden * value).astype(LOW)
    out_ref[2] = (value * up).astype(LOW)


def depth_kernel(ring, first, count, last, *refs):
    normed_refs, cot_refs, pieces, refs = refs[:2], refs[2:4], refs[4 : 4 + count], refs[4 + count :]
    if last:
        partial_ref, _, out_ref, weights_out, weights, sems = refs
    else:
        out_ref, weights_out, weights, sems = refs
    step, steps = pl.program_id(0), pl.num_programs(0)
    me = lax.axis_index("tok")
    side, z = (me // SIDE) % 2, me // RING
    rows = weights.shape[0] // count
    wide = 2 * rows

    def chunk(k):
        return (z - first - k + 2 * ring) % ring

    def load(k):
        start = wide * (k // 2) + rows * (side if k % 2 == 0 else 1 - side)
        return pltpu.make_async_copy(
            pieces[k], weights.at[pl.ds(pl.multiple_of(start, 16), rows)], sems.at[k]
        )

    def keep(k):
        return pltpu.make_async_copy(
            weights.at[pl.ds(wide * k, wide)],
            weights_out.at[pl.ds(pl.multiple_of(chunk(k) * wide, 16), wide)],
            sems.at[count + k],
        )

    @pl.when(step == 0)
    def _():
        for k in range(count):
            load(k).start()
        for k in range(count):
            load(k).wait()
        for k in range(count // 2):
            keep(k).start()

    early = step < steps // 2

    def columns_of(pair):
        parts = []
        for k in range(count // 2):
            lanes = pl.ds(pl.multiple_of(chunk(k) * wide, HD), wide)
            parts.append(jnp.where(early, pair[0][:, lanes], pair[1][:, lanes]))
        return parts[0] if len(parts) == 1 else jnp.concatenate(parts, axis=1)

    normed, cotangent = columns_of(normed_refs), columns_of(cot_refs)
    columns = out_ref.shape[2]
    products = [
        matmul(left, weights[:, k * columns : (k + 1) * columns])
        for k, left in enumerate((normed, normed, cotangent))
    ]
    if last:
        activation_grads(out_ref, *(products[k] + partial_ref[k].astype(FULL) for k in range(3)))
    else:
        for k in range(3):
            out_ref[k] = products[k].astype(LOW)

    @pl.when(step == steps - 1)
    def _():
        for k in range(count // 2):
            keep(k).wait()


def hidden_by_depth(normed, cotangent, pieces):
    half, width = normed[0].shape
    columns = pieces[0].shape[1] // 3
    rows = min(256, half)
    steps = half // rows
    ring = len(pieces) // 2
    deep = width // ring
    blocks = [
        pl.BlockSpec((rows, width), lambda i: (jnp.minimum(i, steps - 1), 0)),
        pl.BlockSpec((rows, width), lambda i: (jnp.maximum(i - steps, 0), 0)),
    ]
    anywhere = pl.BlockSpec(memory_space=pl.ANY)
    block = pl.BlockSpec((3, rows, columns), lambda i: (0, i, 0))
    weights_shape = jax.ShapeDtypeStruct((width, 3 * columns), LOW)

    def part(first, given, more):
        count = len(given)
        return pl.pallas_call(
            functools.partial(depth_kernel, ring, first, count, len(more) > 0),
            grid=(2 * steps,),
            in_specs=blocks * 2 + [anywhere] * count + [block, anywhere][: len(more)],
            out_specs=[block, anywhere],
            out_shape=[jax.ShapeDtypeStruct((3, 2 * half, columns), LOW), weights_shape],
            input_output_aliases={5 + count: 1} if more else {},
            scratch_shapes=[
                pltpu.VMEM((deep * (count // 2), 3 * columns), LOW),
                pltpu.SemaphoreType.DMA((count + count // 2,)),
            ],
            compiler_params=pltpu.CompilerParams(vmem_limit_bytes=48 * MIB),
            cost_estimate=LIGHT,
        )(*normed, *cotangent, *given, *more)

    partial = part(0, pieces[:-2], [])
    return part(ring - 1, pieces[-2:], partial)


def project_sum_kernel(count, array_ref, *refs):
    weight_refs, out_refs = refs[:count], refs[count : count + 2]
    away, arrived, send_sem, recv_sem = refs[count + 2 :]
    step = pl.program_id(0)
    me = lax.axis_index("tok")
    mate = me + 1 - 2 * (me % 2)

    def crossing(block):
        return pltpu.make_async_remote_copy(
            src_ref=away.at[block],
            dst_ref=arrived.at[block],
            send_sem=send_sem.at[block],
            recv_sem=recv_sem.at[block],
            device_id=(mate,),
            device_id_type=pl.DeviceIdType.MESH,
        )

    @pl.when(step == 0)
    def _():
        barrier = pltpu.get_barrier_semaphore()
        pl.semaphore_signal(
            barrier, inc=1, device_id=(mate,), device_id_type=pl.DeviceIdType.MESH
        )
        pl.semaphore_wait(barrier, 1)

    total = by_rows(array_ref[0], weight_refs[0][...])
    for k in range(1, count):
        total += by_rows(array_ref[k], weight_refs[k][...])
    for block in range(2):

        @pl.when(step == block)
        def _():
            away[block] = total.astype(LOW)
            crossing(block).start()

        @pl.when(step == 2 + block)
        def _():
            crossing(block).wait()
            out_refs[block][...] = (total + arrived[block].astype(FULL)).astype(LOW)


def project_sum(array, pack, first, count, identity, marks=()):
    array = after(array, *jax.tree.leaves(marks))
    tokens, columns = array.shape[1:]
    width = pack.shape[0]
    rows = tokens // 4
    whole = pl.BlockSpec((rows, width), lambda i: (0, 0))
    return pl.pallas_call(
        functools.partial(project_sum_kernel, count),
        grid=(4,),
        in_specs=[pl.BlockSpec((count, rows, columns), lambda i: (first // count, (i + 2) % 4, 0))]
        + [
            pl.BlockSpec(
                (width, columns), lambda i, k=k: (0, first + k), pipeline_mode=pl.Buffered(1)
            )
            for k in range(count)
        ],
        out_specs=[whole] * 2,
        out_shape=[jax.ShapeDtypeStruct((rows, width), LOW)] * 2,
        scratch_shapes=[
            pltpu.VMEM((2, rows, width), LOW),
            pltpu.VMEM((2, rows, width), LOW),
            pltpu.SemaphoreType.DMA((2,)),
            pltpu.SemaphoreType.DMA((2,)),
        ],
        compiler_params=pltpu.CompilerParams(
            collective_id=identity, has_side_effects=True, vmem_limit_bytes=44 * MIB
        ),
        cost_estimate=LIGHT,
    )(array, *([pack] * count))


def outer_kernel(chunk_ref, *refs):
    normed_refs, cot_refs, right_ref, give_ref, keep_ref, total = refs[:2], refs[2:4], *refs[4:]
    step, steps = pl.program_id(0), pl.num_programs(0)
    early = step < steps // 2
    normed = jnp.where(early, normed_refs[0][...], normed_refs[1][...])
    cotangent = jnp.where(early, cot_refs[0][...], cot_refs[1][...])
    columns = right_ref.shape[2]

    @pl.when(step == 0)
    def _():
        total[...] = jnp.zeros_like(total)

    for k, left in enumerate((normed, normed, cotangent)):
        total[:, k * columns : (k + 1) * columns] += outer_sum(left, right_ref[k])

    @pl.when(step == steps - 1)
    def _():
        rows = keep_ref.shape[0]
        side = (lax.axis_index("tok") // SIDE) % 2
        for ref, place_of in ((give_ref, 1 - side), (keep_ref, side)):
            ref[...] = total[pl.ds(pl.multiple_of(place_of * rows, 16), rows), :].astype(LOW)


def outer_products(normed, cotangent, array, chunk, rows):
    tokens, columns = array.shape[1:]
    deep = min(512, tokens // 2)
    steps = tokens // 2 // deep
    lefts = [
        pl.BlockSpec((deep, rows), lambda i, chunk_ref: (jnp.minimum(i, steps - 1), chunk_ref[0])),
        pl.BlockSpec((deep, rows), lambda i, chunk_ref: (jnp.maximum(i - steps, 0), chunk_ref[0])),
    ]
    return pl.pallas_call(
        outer_kernel,
        grid_spec=pltpu.PrefetchScalarGridSpec(
            num_scalar_prefetch=1,
            grid=(2 * steps,),
            in_specs=lefts * 2
            + [pl.BlockSpec((3, deep, columns), lambda i, chunk_ref: (0, i, 0))],
            out_specs=[pl.BlockSpec((rows // 2, 3 * columns), lambda i, chunk_ref: (0, 0))] * 2,
            scratch_shapes=[pltpu.VMEM((rows, 3 * columns), FULL)],
        ),
        out_shape=[jax.ShapeDtypeStruct((rows // 2, 3 * columns), LOW)] * 2,
        compiler_params=pltpu.CompilerParams(vmem_limit_bytes=40 * MIB),
        cost_estimate=LIGHT,
    )(chunk[None].astype(jnp.int32), *normed, *cotangent, array)


def join_kernel(count, epsilon, *refs):
    inputs_ref, gain_ref, weight_ref = refs[:3]
    parts, (middle_ref, normed_ref, inverse_ref) = refs[3 : 3 + count], refs[3 + count :]
    total, start = inputs_ref[...].astype(FULL), 0
    for part in parts:
        columns = part.shape[1]
        total += by_rows(part[...], weight_ref[:, start : start + columns])
        start += columns
    inverse = lax.rsqrt(jnp.mean(total * total, axis=1, keepdims=True) + epsilon)
    middle_ref[...] = total
    inverse_ref[...] = jnp.broadcast_to(inverse, inverse_ref.shape)
    normed_ref[...] = (total * inverse * gain_ref[...]).astype(LOW)


def join(tokens, gain, weight, parts):
    count, width = tokens.shape
    rows = min(256, count)
    block = lambda columns: pl.BlockSpec((rows, columns), lambda i: (i, 0))
    return pl.pallas_call(
        functools.partial(join_kernel, len(parts), EPSILON),
        grid=(count // rows,),
        in_specs=[
            block(width),
            pl.BlockSpec((1, width), lambda i: (0, 0)),
            pl.BlockSpec((width, width), lambda i: (0, 0), pipeline_mode=pl.Buffered(1)),
        ]
        + [block(part.shape[1]) for part in parts],
        out_specs=[block(width), block(width), block(HD)],
        out_shape=[
            jax.ShapeDtypeStruct((count, width), FULL),
            jax.ShapeDtypeStruct((count, width), LOW),
            jax.ShapeDtypeStruct((count, HD), FULL),
        ],
        compiler_params=pltpu.CompilerParams(vmem_limit_bytes=40 * MIB),
        cost_estimate=LIGHT,
    )(tokens, gain[None], weight, *parts)


def branch_kernel(
    group_ref, near_ref, cot_ref, middle_ref, inverse_ref, gain_ref, weight_ref,
    grad_ref, branch_ref, mixed_ref, scaled_ref,
):
    grad = group_ref[...].astype(FULL) + near_ref[...].astype(FULL)
    middle, inverse = middle_ref[...], inverse_ref[:, :1]
    normal = middle * inverse
    scaled_ref[...] = (grad * normal).astype(LOW)
    scaled = grad * gain_ref[...]
    total = (
        cot_ref[...].astype(FULL)
        + inverse * scaled
        - normal * (inverse * jnp.mean(scaled * normal, axis=1, keepdims=True))
    )
    grad_ref[...] = total
    branch = total.astype(LOW)
    branch_ref[...] = branch
    mixed_ref[...] = matmul(branch, weight_ref[...]).astype(LOW)


def branch_back(group, near, cotangent, middle, inverse, gain, weight):
    count, width = middle.shape
    rows = min(256, count)
    block = lambda columns: pl.BlockSpec((rows, columns), lambda i: (i, 0))
    return pl.pallas_call(
        branch_kernel,
        grid=(count // rows,),
        in_specs=[
            block(width),
            block(width),
            block(width),
            block(width),
            block(HD),
            pl.BlockSpec((1, width), lambda i: (0, 0)),
            pl.BlockSpec((width, width), lambda i: (0, 0), pipeline_mode=pl.Buffered(1)),
        ],
        out_specs=[block(width)] * 4,
        out_shape=[
            jax.ShapeDtypeStruct((count, width), FULL),
            jax.ShapeDtypeStruct((count, width), LOW),
            jax.ShapeDtypeStruct((count, width), LOW),
            jax.ShapeDtypeStruct((count, width), LOW),
        ],
        compiler_params=pltpu.CompilerParams(vmem_limit_bytes=48 * MIB),
        cost_estimate=LIGHT,
    )(group, near, cotangent, middle, inverse, gain[None], weight)


def on_device(
    tokens, cotangent, attn_gain, ffn_gain, w_query, w_key, w_value, w_out, w_gate, w_up, w_down,
    segments, positions,
):
    token_count, width = tokens.shape
    own_rows, hidden_width = w_gate.shape
    slice_width = hidden_width // GROUP
    heads_width = w_query.shape[1]
    tail_rows = min(token_count, WINDOW)
    hop_count = WINDOW // tail_rows
    device = lax.axis_index("tok")
    inputs = tokens.astype(FULL)

    frequency = 10000.0 ** (-jnp.arange(HD // 2, dtype=FULL) * 2.0 / HD)
    angles = positions.astype(FULL)[:, None] * frequency[None, :]
    cosine = jnp.concatenate([jnp.cos(angles)] * 2, axis=1)
    sine_half = jnp.sin(angles)
    sine = jnp.concatenate([-sine_half, sine_half], axis=1)
    padded_segments = jnp.concatenate([jnp.full((WINDOW,), -1, jnp.int32), segments])
    key_segments = lax.dynamic_slice_in_dim(
        padded_segments, device * token_count, WINDOW + token_count
    )
    query_segments = lax.dynamic_slice_in_dim(segments, device * token_count, token_count)

    attn_pack = jnp.concatenate(
        [
            w_query,
            w_key,
            w_value,
            jnp.pad(
                jnp.stack([attn_gain, ffn_gain], axis=1), ((0, 0), (0, HD - 2))
            ),
        ],
        axis=1,
    )
    edge = heads_width + 2 * HD
    def sliced(weight):
        return weight.reshape(own_rows, GROUP, slice_width).transpose(1, 0, 2)

    ffn_pack = jnp.concatenate([sliced(w_gate), sliced(w_up), sliced(w_down)], axis=2)
    attn_all, ffn_rows = gather(attn_pack, ffn_pack)
    out_w = lax.all_gather(w_out, "tok", axis=0, tiled=True)
    query_w, kv_w = attn_all[:, :heads_width], attn_all[:, heads_width:edge]
    gains = attn_all[:, edge : edge + 2].astype(FULL)
    gain_one, gain_two = gains[:, 0], gains[:, 1]

    inverse_one = lax.rsqrt(jnp.mean(inputs * inputs, axis=-1, keepdims=True) + EPSILON)
    normed = (inputs * inverse_one * gain_one).astype(LOW)
    kv = matmul(normed, kv_w)

    def turned(values, sine_signed):
        half = HD // 2
        rolled = jnp.concatenate([values[:, half:], values[:, :half]], axis=1)
        return values * cosine + rolled * sine_signed

    key_value = jnp.concatenate([turned(kv[:, :HD], sine), kv[:, HD:]], axis=1).astype(LOW)
    received = [passed_along(key_value, hop) for hop in range(hop_count, 0, -1)]
    all_keys = jnp.concatenate(received + [key_value], axis=0)
    raw_query = matmul(normed, query_w)
    heads = heads_width // HD
    given = (all_keys, key_segments, query_segments, cosine, sine)
    early = attend(raw_query, *given, 0, heads // 2)
    pieces, steps = spread(ffn_rows, (early[1],))
    cot_group = rows_to_group(after(cotangent, attn_all), steps[1])
    late = attend(
        after(raw_query, early[1]), *given, heads // 2, heads - heads // 2
    )
    rot, mixed = (jnp.concatenate([early[k], late[k]], axis=1) for k in range(2))
    logs = jnp.concatenate([early[2], late[2]], axis=0)
    middle, normed_two, inverse_two = join(tokens, gain_two, out_w, (early[1], late[1]))

    normed_group = rows_to_group(after(normed_two, *steps[1]), steps[2])
    hidden_pack, ffn_w = hidden_and_grads(normed_group, cot_group, pieces)
    reduction = Reduction(normed_group, cot_group, hidden_pack)
    pairs_done = reduction.multiply(0)
    reduction.begin()
    pairs_done = reduction.multiply(1, pairs_done)
    own_sum, near_sum = project_sum(hidden_pack, ffn_w, 0, 2, 2, pairs_done)
    near_sent = flip(near_sum, NEAR)
    marks = reduction.advance(0, near_sum)
    pairs_done = reduction.multiply(2, marks)
    pairs_done = reduction.multiply(3, pairs_done)
    marks = reduction.advance(1, pairs_done)
    output_own, output_near = project_sum(hidden_pack, ffn_w, 2, 1, 3, marks)
    output_near = flip(after(output_near, near_sent), NEAR)

    grad_middle, branch, grad_mixed, gain_two_parts = branch_back(
        own_sum, after(near_sent, output_own), cotangent, middle, inverse_two, gain_two, out_w
    )
    grad_out_w = outer_sum(branch, mixed).astype(LOW)
    cut = heads_width // 2
    out_sum = lax.psum_scatter(grad_out_w[:, :cut], "tok", scatter_dimension=0, tiled=True)
    marks = reduction.advance(2, grad_mixed)
    query_low, key_grads, value_grads = attend_back(
        rot, after(grad_mixed, *marks), mixed, logs, all_keys, key_segments, query_segments, cosine, sine
    )
    output = (
        middle + output_own.astype(FULL) + after(output_near, query_low).astype(FULL)
    ).astype(LOW)
    grads = jnp.concatenate([key_grads * HD**-0.5, value_grads], axis=1)
    shares = grads[WINDOW:]
    for hop in range(1, hop_count + 1):
        first_row = (hop_count - hop) * tail_rows
        returned = passed_along(grads[first_row : first_row + tail_rows].astype(LOW), -hop)
        shares = shares.at[token_count - tail_rows :].add(returned.astype(FULL))
    kv_low = jnp.concatenate([turned(shares[:, :HD], -sine), shares[:, HD:]], axis=1).astype(LOW)
    grad_query_w = outer_sum(normed, query_low).astype(LOW)
    grad_kv_w = outer_sum(normed, kv_low).astype(LOW)
    grad_normed = by_rows(query_low, query_w) + by_rows(kv_low, kv_w)
    scaled_one = grad_normed * gain_one
    grad_inputs = inverse_one * scaled_one - inputs * inverse_one**3 * jnp.mean(
        scaled_one * inputs, axis=-1, keepdims=True
    )
    grad_tokens = (grad_middle + grad_inputs).astype(LOW)
    lane = lax.broadcasted_iota(jnp.int32, (token_count, HD), 1)
    grad_gains = (
        outer_sum((grad_normed * inputs * inverse_one).astype(LOW), (lane == 0).astype(LOW))
        + outer_sum(gain_two_parts, (lane == 1).astype(LOW))
    ).astype(LOW)
    reduction.advance(3, grad_query_w)
    attn_sum, ffn_parts = scatter(
        [grad_query_w, grad_kv_w, grad_gains, grad_out_w[:, cut:]], reduction.result()
    )

    def joined(parts):
        return parts.transpose(1, 0, 2).reshape(own_rows, hidden_width).astype(FULL)

    return (
        output,
        grad_tokens,
        attn_sum[:, edge],
        attn_sum[:, edge + 1],
        attn_sum[:, :heads_width],
        attn_sum[:, heads_width : heads_width + HD],
        attn_sum[:, heads_width + HD : edge],
        jnp.concatenate([out_sum.astype(FULL), attn_sum[:, edge + HD :]], axis=1),
        joined(ffn_parts[:, :, :slice_width]),
        joined(ffn_parts[:, :, slice_width : 2 * slice_width]),
        joined(ffn_parts[:, :, 2 * slice_width :]),
    )


def solution(mesh):
    rows, flat = P("tok", None), P("tok")
    return jax.shard_map(
        on_device,
        mesh=mesh,
        in_specs=(rows, rows, flat, flat, rows, rows, rows, rows, rows, rows, rows, P(), flat),
        out_specs=(rows, rows, flat, flat, rows, rows, rows, rows, rows, rows, rows),
        check_vma=False,
    )
```
